32 devices in a mesh: seq: 8 (over z, y), tp: 4 (over x, core).
Axes of the slice: x: 2, y: 2, z: 4, core: 2. Of those that a mesh axis runs over, the one named last changes fastest.
Arguments:
- features: bfloat16 [1024, 3, 4096], P('seq', None, 'tp'), may hold values from -6 to 6
- short_taps: bfloat16 [3, 3, 4096], P(None, None, 'tp'), may hold values from -3.5 to 3.5
- rates: float32 [4096, 16], P('tp'), may hold values from 9.765625e-05 to 0.2
- residues: float32 [4096, 16], P('tp'), may hold values from -0.25 to 0.25
- skip: float32 [4096], P('tp'), may hold values from -6 to 6
- out_weight: bfloat16 [4096, 4096], P('seq', 'tp'), may hold values from -0.09375 to 0.09375
Outputs:
- layer_out: bfloat16 [1024, 4096], P('seq', 'tp')
The draws below stay inside these ranges and needn't reach their ends.
All inputs are finite; a program needn't handle non-finite values.
Results may differ from the reference program's by a relative error of at most 0.025.
Values may be sent and summed in bfloat16 or wider, within the bound.
No kernel may reach another device: no remote copies, remote signals or barrier semaphores. Data moves between devices by JAX's collectives and lax.ppermute only.
A program may use at most 128 MiB of HBM per device.

```python
import math
import jax
import jax.numpy as jnp
from jax import lax

D = 4096
R = 16
SHORT = 3
TOK_DEV = 128
TOKENS = 1024
N_TP = 4


def draw_rates(key, part):
    key_slow, key_fast, key_pick = jax.random.split(key, 3)
    slow_rates = jnp.exp(jax.random.uniform(key_slow, (D, R), jnp.float32, math.log(0.1 / TOKENS), math.log(2.0 / TOKENS)))
    fast_rates = jnp.exp(jax.random.uniform(key_fast, (D, R), jnp.float32, math.log(0.04), math.log(0.2)))
    share = 0.5
    picked = jax.random.uniform(key_pick, (D, R), jnp.float32) < share
    return jnp.where(picked, slow_rates, fast_rates).astype(jnp.float32)


def levels(rng, extent, cuts, least, top_value):
    def one(axis_at, shards_of):
        draws = jax.random.uniform(jax.random.fold_in(jax.random.fold_in(rng, 6), axis_at), (shards_of,), jnp.float32, least / len(cuts), top_value / len(cuts))
        return jnp.repeat(jnp.exp(draws), extent[axis_at] // shards_of).reshape((-1,) + (1,) * (len(extent) - axis_at - 1))

    level = one(*cuts[0])
    for cut in cuts[1:]:
        level = level * one(*cut)
    return level


def normal_values(stream_key, dims, width, limit, pieces=(), held_as=jnp.bfloat16):
    drawn = width * jax.random.normal(stream_key, dims, jnp.float32)
    if pieces:
        drawn = drawn * levels(stream_key, dims, pieces, -0.22, 0.18)
    return jnp.clip(drawn, -limit, limit).astype(held_as)


def setup_inputs(seed: int = 0) -> dict:
    keys = jax.random.split(jax.random.key(seed), 7)
    return {
        "features": normal_values(keys[0], (TOKENS, 3, D), 1.0, 6.0, ((0, 8), (2, 4))),
        "short_taps": normal_values(keys[1], (3, SHORT, D), SHORT ** -0.5, 3.5, ((2, 4),)),
        "rates": draw_rates(jax.random.fold_in(keys[6], 71), 0),
        "residues": normal_values(keys[3], (D, R), (2.0 * (R * TOKENS) ** -0.5), 0.25, ((0, 4),), jnp.float32),
        "skip": normal_values(keys[4], (D,), 1.0, 6.0, ((0, 4),), jnp.float32),
        "out_weight": normal_values(keys[5], (D, D), D ** -0.5, 0.09375, ((0, 8), (1, 4))),
    }


def short_mix(features, short_taps):
    signal = features.astype(jnp.float32)
    tap_values = short_taps.astype(jnp.float32)
    mixed = tap_values[:, 0, :] * signal
    for shift_rows in range(1, SHORT):
        moved = jnp.concatenate([jnp.zeros((shift_rows,) + signal.shape[1:], jnp.float32), signal[:-shift_rows]], axis=0)
        mixed = mixed + tap_values[:, shift_rows, :] * moved
    return mixed


def reference(features, short_taps, rates, residues, skip, out_weight):
    mixed = short_mix(features, short_taps)
    signal = mixed[:, 1, :] * mixed[:, 2, :]
    step_decay = jnp.exp(-rates)
    block_decay = jnp.exp(-rates * TOK_DEV)
    offsets = jnp.arange(1, TOK_DEV + 1).astype(jnp.float32)
    far_weight = residues[None] * jnp.exp(-rates[None] * offsets[:, None, None])

    def advance(modes, current):
        modes = step_decay * modes + current[:, None]
        return modes, jnp.sum(residues * modes, axis=1)

    def per_block(state, block_signal):
        block_end, near_part = lax.scan(advance, jnp.zeros((D, R), jnp.float32), block_signal)
        far_part = jnp.sum(far_weight * state[None], axis=2)
        return block_decay * state + block_end, near_part + far_part

    _, filtered = lax.scan(per_block, jnp.zeros((D, R), jnp.float32), signal.reshape(TOKENS // TOK_DEV, TOK_DEV, D))
    conv = filtered.reshape(TOKENS, D) + skip[None] * signal
    gated = (mixed[:, 0, :] * conv).astype(jnp.bfloat16)
    group = D // N_TP
    total = jnp.zeros((TOKENS, D), jnp.float32)
    for index in range(N_TP):
        lower = index * group
        part_sum = jnp.dot(gated[:, lower:lower + group], out_weight[:, lower:lower + group].T, preferred_element_type=jnp.float32)
        part_sum = lax.optimization_barrier(part_sum.astype(jnp.bfloat16)).astype(jnp.float32)
        total = total + part_sum
    return total.astype(jnp.bfloat16)
```

```python
import functools

import jax
import jax.numpy as jnp
from jax import lax
from jax.experimental import pallas as pl
from jax.experimental.pallas import tpu as pltpu
from jax.sharding import PartitionSpec as P

LANES = 128
F32 = jnp.float32
BF16 = jnp.bfloat16
VMEM = pl.BlockSpec(memory_space=pltpu.VMEM)
SMEM = pl.BlockSpec(memory_space=pltpu.SMEM)
AXES = ("seq", "tp")


def cost(flops, bytes_accessed):
    return pl.CostEstimate(flops=flops, bytes_accessed=bytes_accessed, transcendentals=0)


def params(**kw):
    return pltpu.CompilerParams(vmem_limit_bytes=40 * 1024 * 1024, **kw)


def local_kernel(
    q_ref, k_ref, v_ref, taps_ref, rates_ref, residues_ref, skip_ref,
    out_ref, message_ref, table_ref,
    signal_s, conv_s, gate_s, message_s,
):
    tokens, channels = q_ref.shape
    poles = rates_ref.shape[1]
    taps = taps_ref.shape[1]
    fold = channels // LANES
    edge = taps - 1
    tap_base = 2 * poles * fold
    skip_base = tap_base + 3 * taps * fold
    later = lax.broadcasted_iota(jnp.int32, (tokens, LANES), 0) >= edge
    table_ref[skip_base : skip_base + fold, :] = skip_ref[...]
    for j in range(fold):
        lanes = slice(j * LANES, (j + 1) * LANES)
        table_ref[pl.ds(j, poles, stride=fold), :] = rates_ref[lanes, :].T
        table_ref[pl.ds(poles * fold + j, poles, stride=fold), :] = residues_ref[lanes, :].T
        mixed = []
        for group, ref in enumerate((q_ref, k_ref, v_ref)):
            value = ref[:, lanes].astype(F32)
            total = None
            for shift in range(taps):
                tap = taps_ref[group, shift : shift + 1, lanes].astype(F32)
                row = tap_base + (group * taps + shift) * fold + j
                table_ref[row : row + 1, :] = tap
                moved = value if shift == 0 else pltpu.roll(value, shift, axis=0)
                total = tap * moved if total is None else total + tap * moved
            mixed.append(total)
            for place in range(2 * edge):
                source = place if place < edge else tokens - 2 * edge + place
                row = (poles + group * 2 * edge + place) * fold + j
                message_s[row : row + 1, :] = value[source : source + 1, :]
        gate_s[:, lanes] = mixed[0]
        signal = jnp.where(later, mixed[1] * mixed[2], 0.0)
        signal_s[pl.ds(j, tokens, stride=fold), :] = signal
    decay = [jnp.exp(-table_ref[r * fold : (r + 1) * fold, :]) for r in range(poles)]
    residue = [table_ref[(poles + r) * fold : (poles + r + 1) * fold, :] for r in range(poles)]
    skip = skip_ref[...]

    def step(t, modes):
        rows = pl.ds(pl.multiple_of(t * fold, fold), fold)
        value = signal_s[rows, :]
        modes = tuple(d * m + c * value for d, c, m in zip(decay, residue, modes))
        conv_s[rows, :] = tree_sum(modes + (skip * value,))
        return modes

    modes = lax.fori_loop(0, tokens, step, (jnp.zeros((fold, LANES), F32),) * poles, unroll=4)
    for r in range(poles):
        message_s[r * fold : (r + 1) * fold, :] = modes[r]
    message_ref[...] = message_s[...].astype(BF16)
    for j in range(fold):
        lanes = slice(j * LANES, (j + 1) * LANES)
        conv = conv_s[pl.ds(j, tokens, stride=fold), :]
        out_ref[:, lanes] = (gate_s[:, lanes] * conv).astype(BF16)


def tree_sum(values):
    values = list(values)
    while len(values) > 1:
        values = [a + b for a, b in zip(values[::2], values[1::2])] + (
            [values[-1]] if len(values) % 2 else []
        )
    return values[0]


def local_part(features, short_taps, rates, residues, skip):
    tokens, _, channels = features.shape
    poles, taps = rates.shape[1], short_taps.shape[1]
    fold = channels // LANES
    message_rows = (poles + 6 * (taps - 1)) * fold
    table_rows = (2 * poles + 3 * taps + 1) * fold
    return pl.pallas_call(
        local_kernel,
        out_shape=(
            jax.ShapeDtypeStruct((tokens, channels), BF16),
            jax.ShapeDtypeStruct((message_rows, LANES), BF16),
            jax.ShapeDtypeStruct((table_rows, LANES), F32),
        ),
        in_specs=[VMEM] * 7,
        out_specs=(VMEM,) * 3,
        scratch_shapes=[
            pltpu.VMEM((tokens * fold, LANES), F32),
            pltpu.VMEM((tokens * fold, LANES), F32),
            pltpu.VMEM((tokens, channels), F32),
            pltpu.VMEM((message_rows, LANES), F32),
        ],
        compiler_params=params(),
        cost_estimate=cost(4 * tokens * channels * poles, 3 << 20),
        name="local_filter",
    )(
        features[:, 0], features[:, 1], features[:, 2],
        short_taps, rates, residues, skip.reshape(fold, LANES),
    )


def far_kernel(poles, taps, count, place_ref, near_ref, q_ref, table_ref, *refs):
    message_refs, (out_ref, conv_s) = refs[:count], refs[count:]
    tokens, channels = near_ref.shape
    fold = channels // LANES
    edge = taps - 1
    shard = place_ref[0]
    tap_base = 2 * poles * fold
    skip_base = tap_base + 3 * taps * fold
    rates = table_ref[0 : poles * fold, :].reshape(poles, fold, LANES)
    residues = table_ref[poles * fold : 2 * poles * fold, :].reshape(poles, fold, LANES)
    skip = table_ref[skip_base : skip_base + fold, :]
    span = jnp.exp(-rates * float(tokens))
    lead = [jnp.exp(-rates * float(tokens - 1 - i)) * residues for i in range(edge)]

    def tap(group, shift):
        row = tap_base + (group * taps + shift) * fold
        return table_ref[row : row + fold, :]

    def message(index):
        if count == 1:
            value = message_refs[0][index]
        else:
            value = message_refs[0][...]
            for i in range(1, count):
                value = jnp.where(index == i, message_refs[i][...], value)
        return value.astype(F32).reshape(-1, fold, LANES)

    def edges(index):
        current = message(index)
        before = jnp.where(index > 0, message(jnp.maximum(index - 1, 0)), 0.0)
        mixed = []
        for group in range(3):
            base = poles + group * 2 * edge
            rows = [before[base + edge + i] for i in range(edge)] + [current[base + i] for i in range(edge)]
            mixed.append(
                [
                    sum(tap(group, shift) * rows[edge + i - shift] for shift in range(taps))
                    for i in range(edge)
                ]
            )
        return current, before, mixed

    def one(index, state):
        current, _, mixed = edges(index)
        state = span * state + current[:poles]
        for i in range(edge):
            state = state + lead[i] * (mixed[1][i] * mixed[2][i])[None]
        return state

    state = lax.fori_loop(0, shard, one, jnp.zeros((poles, fold, LANES), F32))
    _, before, mixed = edges(shard)
    decay = [jnp.exp(-rates[r]) for r in range(poles)]
    modes = tuple(state[r] for r in range(poles))
    for t in range(edge):
        value = mixed[1][t] * mixed[2][t]
        modes = tuple(decay[r] * modes[r] + residues[r] * value for r in range(poles))
        conv_s[t * fold : (t + 1) * fold, :] = tree_sum(modes + (skip * value,))

    def step(t, modes):
        modes = tuple(d * m for d, m in zip(decay, modes))
        conv_s[pl.ds(pl.multiple_of(t * fold, fold), fold), :] = tree_sum(modes)
        return modes

    lax.fori_loop(edge, tokens, step, modes, unroll=6)
    row_id = lax.broadcasted_iota(jnp.int32, (tokens, LANES), 0)
    for j in range(fold):
        lanes = slice(j * LANES, (j + 1) * LANES)
        value = q_ref[:, lanes].astype(F32)
        gate = None
        for shift in range(taps):
            row = tap_base + shift * fold + j
            moved = value if shift == 0 else pltpu.roll(value, shift, axis=0)
            for t in range(shift):
                halo = before[poles + 2 * edge - shift + t][j : j + 1, :]
                moved = jnp.where(row_id == t, halo, moved)
            term = table_ref[row : row + 1, :] * moved
            gate = term if gate is None else gate + term
        conv = conv_s[pl.ds(j, tokens, stride=fold), :]
        out_ref[:, lanes] = (near_ref[:, lanes].astype(F32) + gate * conv).astype(BF16)


def far_part(shard, near, q, table, messages, poles, taps):
    tokens, channels = near.shape
    fold = channels // LANES
    count = len(messages)
    return pl.pallas_call(
        functools.partial(far_kernel, poles, taps, count),
        out_shape=jax.ShapeDtypeStruct((tokens, channels), BF16),
        in_specs=[SMEM] + [VMEM] * (3 + count),
        out_specs=VMEM,
        scratch_shapes=[pltpu.VMEM((tokens * fold, LANES), F32)],
        compiler_params=params(),
        cost_estimate=cost(4 * tokens * channels * poles, 3 << 20),
        name="far_filter",
    )(shard.reshape(1).astype(jnp.int32), near, q, table, *messages)


def project_kernel(place_ref, own_ref, other_ref, w00, w01, w10, w11, out_ref, rows_s):
    z0, y, core = place_ref[0], place_ref[1], place_ref[2]
    tokens = own_ref.shape[0]
    rows_s[:tokens] = own_ref[...]
    rows_s[tokens:] = other_ref[...]
    for dz, dy, ref in ((0, 0, w00), (0, 1, w01), (1, 0, w10), (1, 1, w11)):
        part = lax.dot_general(
            rows_s[...], ref[...], (((1,), (1,)), ((), ())), preferred_element_type=F32
        ).astype(BF16)
        which = (z0 ^ dz) ^ core
        half = y ^ dy
        out_ref[which, 0, half] = part[:tokens]
        out_ref[which, 1, half] = part[tokens:]


def finish_kernel(place_ref, own_ref, side_ref, straight_ref, across_ref, out_ref):
    width = own_ref.shape[2]

    @pl.when(place_ref[0] == 0)
    def _():
        for h in range(2):
            total = own_ref[h].astype(F32) + side_ref[h].astype(F32)
            out_ref[:, h * width : (h + 1) * width] = total.astype(BF16)

    @pl.when(place_ref[0] != 0)
    def _():
        for h in range(2):
            total = straight_ref[h].astype(F32) + across_ref[h].astype(F32)
            out_ref[:, h * width : (h + 1) * width] = total.astype(BF16)


def permute(x, move, keep=None):
    pairs = []
    for index in range(32):
        place = (index // 8, index // 4 % 2, index // 2 % 2, index % 2)
        if keep is None or keep(*place):
            z, y, x_, c = move(*place)
            pairs.append((index, ((z * 2 + y) * 2 + x_) * 2 + c))
    return lax.ppermute(x, AXES, pairs)


def over_y(z, y, x, c):
    return z, 1 - y, x, c


def over_z0(z, y, x, c):
    return z ^ 1, y, x, c


def over_z1(z, y, x, c):
    return z ^ 2, y, x, c


def over_core(z, y, x, c):
    return z, y, x, 1 - c


def per_device_32(features, short_taps, rates, residues, skip, out_weight):
    tokens, _, channels = features.shape
    poles, taps = rates.shape[1], short_taps.shape[1]
    seq, tp = lax.axis_index("seq"), lax.axis_index("tp")
    z, y, x, core = seq // 2, seq % 2, tp // 2, tp % 2
    z1, z0 = z // 2, z % 2
    near, message, table = local_part(features, short_taps, rates, residues, skip)
    pair = jnp.stack([message, permute(message, over_y)])
    by_z = [pair] + [permute(pair, lambda z, y, x, c, k=k: ((z + k) % 4, y, x, c)) for k in (1, 2, 3)]
    table_all = jnp.stack(by_z)
    order = jnp.arange(8)
    messages = table_all[(z - order // 2) % 4, (order % 2) ^ y]
    half_rows = out_weight.shape[0] // 2
    w_y = permute(out_weight, over_y)
    w_z = permute(out_weight, over_z0)
    w_zy = jnp.concatenate(
        [permute(w_z[:half_rows], over_y), permute(w_y[half_rows:], over_z0)], axis=0
    )
    gated = far_part(seq, near, features[:, 0], table, [messages], poles, taps)
    other = permute(gated, over_z1)
    rows = out_weight.shape[0]
    place = jnp.stack([z0, y, core]).astype(jnp.int32)
    partial = pl.pallas_call(
        project_kernel,
        out_shape=jax.ShapeDtypeStruct((2, 2, 2, tokens, rows), BF16),
        in_specs=[SMEM] + [VMEM] * 6,
        out_specs=VMEM,
        scratch_shapes=[pltpu.VMEM((2 * tokens, channels), BF16)],
        compiler_params=params(),
        cost_estimate=cost(16 * tokens * channels * rows, 6 << 20),
        name="project",
    )(place, gated, other, out_weight, w_y, w_z, w_zy)
    from_core = permute(partial[1], over_core)
    summed = (partial[0].astype(F32) + from_core.astype(F32)).astype(BF16)
    own, away = summed[0], summed[1]
    side = permute(own, lambda z, y, x, c: (z, y, 1 - x, c), lambda z, y, x, c: x != z // 2)
    straight = permute(away, over_z1, lambda z, y, x, c: x == z // 2)
    across = permute(
        away, lambda z, y, x, c: (z ^ 2, y, 1 - x, c), lambda z, y, x, c: x != z // 2
    )
    return pl.pallas_call(
        finish_kernel,
        out_shape=jax.ShapeDtypeStruct((tokens, 2 * rows), BF16),
        in_specs=[SMEM] + [VMEM] * 4,
        out_specs=VMEM,
        compiler_params=params(),
        cost_estimate=cost(4 * tokens * rows, 2 << 20),
        name="finish",
    )((x ^ z1).reshape(1).astype(jnp.int32), own, side, straight, across)


def per_device(features, short_taps, rates, residues, skip, out_weight):
    poles, taps = rates.shape[1], short_taps.shape[1]
    near, message, table = local_part(features, short_taps, rates, residues, skip)
    messages = lax.all_gather(message, "seq")
    gated = far_part(
        lax.axis_index("seq"), near, features[:, 0], table, [messages], poles, taps
    )
    partial = lax.dot_general(
        gated,
        lax.all_gather(out_weight, "seq", axis=0, tiled=True),
        (((1,), (1,)), ((), ())),
        preferred_element_type=F32,
    )
    return lax.psum_scatter(partial.astype(BF16), "tp", scatter_dimension=1, tiled=True)


def solution(mesh):
    in_specs = (
        P("seq", None, "tp"),
        P(None, None, "tp"),
        P("tp", None),
        P("tp", None),
        P("tp"),
        P("seq", "tp"),
    )
    out_specs = P("seq", "tp")
    body = per_device_32 if (mesh.shape["seq"], mesh.shape["tp"]) == (8, 4) else per_device
    return jax.shard_map(body, mesh=mesh, in_specs=in_specs, out_specs=out_specs, check_vma=False)
```

```python
import functools

import jax
import jax.numpy as jnp
from jax import lax
from jax.experimental import pallas as pl
from jax.experimental.pallas import tpu as pltpu
from jax.sharding import PartitionSpec as P

LANES = 128
F32 = jnp.float32
BF16 = jnp.bfloat16
VMEM = pl.BlockSpec(memory_space=pltpu.VMEM)
SMEM = pl.BlockSpec(memory_space=pltpu.SMEM)
AXES = ("seq", "tp")


def cost(flops, bytes_accessed):
    return pl.CostEstimate(flops=flops, bytes_accessed=bytes_accessed, transcendentals=0)


def params(**kw):
    return pltpu.CompilerParams(vmem_limit_bytes=40 * 1024 * 1024, **kw)


def local_kernel(
    q_ref, k_ref, v_ref, taps_ref, rates_ref, residues_ref, skip_ref,
    out_ref, message_ref, table_ref,
    signal_s, conv_s, gate_s, message_s,
):
    tokens, channels = q_ref.shape
    poles = rates_ref.shape[0]
    taps = taps_ref.shape[1]
    fold = channels // LANES
    edge = taps - 1
    tap_base = 2 * poles * fold
    skip_base = tap_base + 3 * taps * fold
    later = lax.broadcasted_iota(jnp.int32, (tokens, LANES), 0) >= edge
    table_ref[skip_base : skip_base + fold, :] = skip_ref[...]
    for j in range(fold):
        lanes = slice(j * LANES, (j + 1) * LANES)
        table_ref[pl.ds(j, poles, stride=fold), :] = rates_ref[:, lanes]
        table_ref[pl.ds(poles * fold + j, poles, stride=fold), :] = residues_ref[:, lanes]
        mixed = []
        for group, ref in enumerate((q_ref, k_ref, v_ref)):
            value = ref[:, lanes].astype(F32)
            total = None
            for shift in range(taps):
                tap = taps_ref[group, shift : shift + 1, lanes].astype(F32)
                row = tap_base + (group * taps + shift) * fold + j
                table_ref[row : row + 1, :] = tap
                moved = value if shift == 0 else pltpu.roll(value, shift, axis=0)
                total = tap * moved if total is None else total + tap * moved
            mixed.append(total)
            for place in range(2 * edge):
                source = place if place < edge else tokens - 2 * edge + place
                row = (poles + group * 2 * edge + place) * fold + j
                message_s[row : row + 1, :] = value[source : source + 1, :]
        gate_s[:, lanes] = mixed[0]
        signal = jnp.where(later, mixed[1] * mixed[2], 0.0)
        signal_s[pl.ds(j, tokens, stride=fold), :] = signal
    decay = [jnp.exp(-table_ref[r * fold : (r + 1) * fold, :]) for r in range(poles)]
    residue = [table_ref[(poles + r) * fold : (poles + r + 1) * fold, :] for r in range(poles)]
    skip = skip_ref[...]

    def step(t, modes):
        rows = pl.ds(pl.multiple_of(t * fold, fold), fold)
        value = signal_s[rows, :]
        modes = tuple(d * m + c * value for d, c, m in zip(decay, residue, modes))
        conv_s[rows, :] = tree_sum(modes + (skip * value,))
        return modes

    modes = lax.fori_loop(0, tokens, step, (jnp.zeros((fold, LANES), F32),) * poles, unroll=4)
    for r in range(poles):
        message_s[r * fold : (r + 1) * fold, :] = modes[r]
    message_ref[...] = message_s[...].astype(BF16)
    for j in range(fold):
        lanes = slice(j * LANES, (j + 1) * LANES)
        conv = conv_s[pl.ds(j, tokens, stride=fold), :]
        out_ref[:, lanes] = (gate_s[:, lanes] * conv).astype(BF16)


def tree_sum(values):
    values = list(values)
    while len(values) > 1:
        values = [a + b for a, b in zip(values[::2], values[1::2])] + (
            [values[-1]] if len(values) % 2 else []
        )
    return values[0]


def local_part(features, short_taps, rates, residues, skip):
    tokens, _, channels = features.shape
    poles, taps = rates.shape[1], short_taps.shape[1]
    fold = channels // LANES
    message_rows = (poles + 6 * (taps - 1)) * fold
    table_rows = (2 * poles + 3 * taps + 1) * fold
    return pl.pallas_call(
        local_kernel,
        out_shape=(
            jax.ShapeDtypeStruct((tokens, channels), BF16),
            jax.ShapeDtypeStruct((message_rows, LANES), BF16),
            jax.ShapeDtypeStruct((table_rows, LANES), F32),
        ),
        in_specs=[VMEM] * 7,
        out_specs=(VMEM,) * 3,
        scratch_shapes=[
            pltpu.VMEM((tokens * fold, LANES), F32),
            pltpu.VMEM((tokens * fold, LANES), F32),
            pltpu.VMEM((tokens, channels), F32),
            pltpu.VMEM((message_rows, LANES), F32),
        ],
        compiler_params=params(),
        cost_estimate=cost(4 * tokens * channels * poles, 3 << 20),
        name="local_filter",
    )(
        features[:, 0], features[:, 1], features[:, 2],
        short_taps, rates.T, residues.T, skip.reshape(fold, LANES),
    )


class Table:
    def __init__(self, ref, poles, taps, fold, tokens):
        self.ref, self.poles, self.taps, self.fold, self.edge = ref, poles, taps, fold, taps - 1
        self.rates = ref[0 : poles * fold, :].reshape(poles, fold, LANES)
        self.residues = ref[poles * fold : 2 * poles * fold, :].reshape(poles, fold, LANES)
        self.tap_base = 2 * poles * fold
        skip_base = self.tap_base + 3 * taps * fold
        self.skip = ref[skip_base : skip_base + fold, :]
        self.tokens = tokens

    def span(self, shards):
        return jnp.exp(-self.rates * float(shards * self.tokens))

    def tap(self, group, shift):
        row = self.tap_base + (group * self.taps + shift) * self.fold
        return self.ref[row : row + self.fold, :]

    def message(self, value):
        return value.astype(F32).reshape(-1, self.fold, LANES)

    def first(self, message, group):
        base = self.poles + group * 2 * self.edge
        return [message[base + i] for i in range(self.edge)]

    def last(self, message, group):
        base = self.poles + group * 2 * self.edge + self.edge
        return [message[base + i] for i in range(self.edge)]

    def mixed(self, before, current, group):
        rows = self.last(before, group) + self.first(current, group)
        return [
            sum(self.tap(group, shift) * rows[self.edge + i - shift] for shift in range(self.taps))
            for i in range(self.edge)
        ]

    def signals(self, before, current):
        pairs = zip(self.mixed(before, current, 1), self.mixed(before, current, 2))
        return [k * v for k, v in pairs]

    def lead(self, shards):
        last = shards * self.tokens - 1
        return [jnp.exp(-self.rates * float(last - i)) * self.residues for i in range(self.edge)]

    def enter(self, state, span, lead, before, current):
        state = span * state + current[: self.poles]
        for weight, value in zip(lead, self.signals(before, current)):
            state = state + weight * value[None]
        return state


def enter_any(table, place_ref, messages_ref):
    span, lead = table.span(1), table.lead(1)

    def pick(index):
        current = table.message(messages_ref[index])
        before = table.message(messages_ref[jnp.maximum(index - 1, 0)])
        return jnp.where(index > 0, before, 0.0), current

    def one(index, state):
        return table.enter(state, span, lead, *pick(index))

    zero = jnp.zeros((table.poles, table.fold, LANES), F32)
    state = lax.fori_loop(0, place_ref[0], one, zero)
    return (state,) + pick(place_ref[0])


def enter_joined(spans, table, place_ref, own_ref, other_ref, *refs):
    joined = [table.message(ref[...]) for ref in refs]
    own, other = table.message(own_ref[...]), table.message(other_ref[...])
    before = jnp.zeros_like(own)
    state = before[: table.poles]
    for shards, current in zip(spans[::-1], joined[::-1]):
        state = table.enter(state, table.span(shards), table.lead(shards), before, current)
        before = current
    second = place_ref[0] == 1
    behind = table.enter(state, table.span(1), table.lead(1), before, other)
    return jnp.where(second, behind, state), jnp.where(second, other, before), own


def join_kernel(poles, taps, tokens, place_ref, own_ref, other_ref, table_ref, out_ref):
    fold = own_ref.shape[0] // (poles + 6 * (taps - 1))
    table = Table(table_ref, poles, taps, fold, tokens)
    own, other = table.message(own_ref[...]), table.message(other_ref[...])
    second = place_ref[0] == 1
    before, current = jnp.where(second, other, own), jnp.where(second, own, other)
    state = table.enter(before[:poles], table.span(1), table.lead(1), before, current)
    out = [state[r] for r in range(poles)]
    for group in range(3):
        out += table.first(before, group) + table.last(current, group)
    out_ref[...] = jnp.concatenate(out, axis=0).astype(BF16)


def join_part(place, own, other, table, tokens, poles, taps):
    return pl.pallas_call(
        functools.partial(join_kernel, poles, taps, tokens),
        out_shape=jax.ShapeDtypeStruct(own.shape, BF16),
        in_specs=[SMEM] + [VMEM] * 3,
        out_specs=VMEM,
        compiler_params=params(),
        cost_estimate=cost(1 << 20, 1 << 18),
        name="join_state",
    )(place.reshape(1).astype(jnp.int32), own, other, table)


def far_kernel(poles, taps, count, enter, place_ref, near_ref, q_ref, table_ref, *refs):
    message_refs, (out_ref, conv_s) = refs[:count], refs[count:]
    tokens, channels = near_ref.shape
    fold = channels // LANES
    table = Table(table_ref, poles, taps, fold, tokens)
    edge = table.edge
    state, before, current = enter(table, place_ref, *message_refs)
    decay = [jnp.exp(-table.rates[r]) for r in range(poles)]
    modes = tuple(state[r] for r in range(poles))
    for t, value in enumerate(table.signals(before, current)):
        modes = tuple(decay[r] * modes[r] + table.residues[r] * value for r in range(poles))
        conv_s[t * fold : (t + 1) * fold, :] = tree_sum(modes + (table.skip * value,))

    def step(t, modes):
        modes = tuple(d * m for d, m in zip(decay, modes))
        conv_s[pl.ds(pl.multiple_of(t * fold, fold), fold), :] = tree_sum(modes)
        return modes

    lax.fori_loop(edge, tokens, step, modes, unroll=6)
    row_id = lax.broadcasted_iota(jnp.int32, (tokens, LANES), 0)
    halo = table.last(before, 0)
    for j in range(fold):
        lanes = slice(j * LANES, (j + 1) * LANES)
        value = q_ref[:, lanes].astype(F32)
        gate = None
        for shift in range(taps):
            moved = value if shift == 0 else pltpu.roll(value, shift, axis=0)
            for t in range(shift):
                moved = jnp.where(row_id == t, halo[edge - shift + t][j : j + 1, :], moved)
            row = table.tap_base + shift * fold + j
            term = table_ref[row : row + 1, :] * moved
            gate = term if gate is None else gate + term
        conv = conv_s[pl.ds(j, tokens, stride=fold), :]
        out_ref[:, lanes] = (near_ref[:, lanes].astype(F32) + gate * conv).astype(BF16)


def far_part(enter, place, near, q, table, messages, poles, taps):
    tokens, channels = near.shape
    fold = channels // LANES
    count = len(messages)
    return pl.pallas_call(
        functools.partial(far_kernel, poles, taps, count, enter),
        out_shape=jax.ShapeDtypeStruct((tokens, channels), BF16),
        in_specs=[SMEM] + [VMEM] * (3 + count),
        out_specs=VMEM,
        scratch_shapes=[pltpu.VMEM((tokens * fold, LANES), F32)],
        compiler_params=params(),
        cost_estimate=cost(4 * tokens * channels * poles, 3 << 20),
        name="far_filter",
    )(place.reshape(1).astype(jnp.int32), near, q, table, *messages)


def project_kernel(count, place_ref, *refs):
    rows_refs, (own_ref, other_ref, out_ref) = refs[:count], refs[count:]
    y, first = place_ref[0], place_ref[1]
    for i, rows_ref in enumerate(rows_refs):
        for half, ref in ((y, own_ref), (1 - y, other_ref)):
            part = lax.dot_general(
                rows_ref[...], ref[...], (((1,), (1,)), ((), ())), preferred_element_type=F32
            )
            out_ref[(first ^ i) if count > 1 else 0, half] = part.astype(BF16)


def project_part(place, rows, own, other):
    tokens, channels = rows[0].shape
    width = own.shape[0]
    count = len(rows)
    return pl.pallas_call(
        functools.partial(project_kernel, count),
        out_shape=jax.ShapeDtypeStruct((count, 2, tokens, width), BF16),
        in_specs=[SMEM] + [VMEM] * (2 + count),
        out_specs=VMEM,
        compiler_params=params(),
        cost_estimate=cost(4 * count * tokens * channels * width, 3 << 20),
        name="project",
    )(place, *rows, own, other)


def finish_kernel(place_ref, *refs):
    out_ref = refs[-1]
    width = refs[0].shape[2]
    for pair in range((len(refs) - 1) // 2):

        @pl.when(place_ref[0] == pair)
        def _(pair=pair):
            for h in range(2):
                total = refs[2 * pair][h].astype(F32) + refs[2 * pair + 1][h].astype(F32)
                out_ref[:, h * width : (h + 1) * width] = total.astype(BF16)


def permute(x, move, keep=None):
    pairs = []
    for index in range(32):
        place = (index // 8, index // 4 % 2, index // 2 % 2, index % 2)
        if keep is None or keep(*place):
            z, y, x_, c = move(*place)
            pairs.append((index, ((z * 2 + y) * 2 + x_) * 2 + c))
    return lax.ppermute(x, AXES, pairs)


def over_y(z, y, x, c):
    return z, 1 - y, x, c


def over_z0(z, y, x, c):
    return z ^ 1, y, x, c


def over_z1(z, y, x, c):
    return z ^ 2, y, x, c


def over_core(z, y, x, c):
    return z, y, x, 1 - c


def after(x, *others):
    return lax.optimization_barrier((x,) + others)[0]


def per_device_32(features, short_taps, rates, residues, skip, out_weight):
    tokens, _, channels = features.shape
    poles, taps = rates.shape[1], short_taps.shape[1]
    seq, tp = lax.axis_index("seq"), lax.axis_index("tp")
    z, y = seq // 2, seq % 2
    near, message, table = local_part(features, short_taps, rates, residues, skip)
    message_y = permute(message, over_y)
    w_y = permute(after(out_weight, message_y), over_y)
    pair = join_part(y, message, message_y, table, tokens, poles, taps)
    pair_z = permute(pair, lambda z, y, x, c: (z + 1, y, x, c), lambda z, y, x, c: z + 1 < 4)
    four = join_part(jnp.ones((), jnp.int32), pair, pair_z, table, 2 * tokens, poles, taps)
    four_z = permute(four, lambda z, y, x, c: (z + 2, y, x, c), lambda z, y, x, c: z + 2 < 4)
    enter = functools.partial(enter_joined, (2, 4))
    gated = far_part(
        enter, y, near, features[:, 0], table, [message, message_y, pair_z, four_z], poles, taps
    )
    two = permute(gated, over_z1)
    one = permute(gated, over_z0)
    three = permute(two, over_z0)
    odd = (z ^ tp) % 2
    place = jnp.stack([y, odd]).astype(jnp.int32)

    def odd_of(z, y, x, c):
        return (z ^ c) % 2

    def home(summed, far):
        def move(z, y, x, c):
            return z ^ far ^ odd_of(z, y, x, c), y, z // 2, z % 2

        return [
            permute(summed, move, lambda z, y, x, c: x != z // 2),
            permute(summed, move, lambda z, y, x, c: x == z // 2),
        ]

    parts = []
    for far, rows in ((0, [gated, one]), (2, [two, three])):
        kept, sent = project_part(place, rows, out_weight, w_y)
        from_core = permute(sent, over_core)
        parts += home((kept.astype(F32) + from_core.astype(F32)).astype(BF16), far)
    kind = (z ^ tp) // 2
    return pl.pallas_call(
        finish_kernel,
        out_shape=jax.ShapeDtypeStruct((tokens, 2 * out_weight.shape[0]), BF16),
        in_specs=[SMEM] + [VMEM] * len(parts),
        out_specs=VMEM,
        compiler_params=params(),
        cost_estimate=cost(4 * tokens * out_weight.shape[0], 2 << 20),
        name="finish",
    )(kind.reshape(1).astype(jnp.int32), *parts)


def per_device(features, short_taps, rates, residues, skip, out_weight):
    poles, taps = rates.shape[1], short_taps.shape[1]
    near, message, table = local_part(features, short_taps, rates, residues, skip)
    messages = lax.all_gather(message, "seq")
    place, q = lax.axis_index("seq"), features[:, 0]
    gated = far_part(enter_any, place, near, q, table, [messages], poles, taps)
    partial = lax.dot_general(
        gated,
        lax.all_gather(out_weight, "seq", axis=0, tiled=True),
        (((1,), (1,)), ((), ())),
        preferred_element_type=F32,
    )
    return lax.psum_scatter(partial.astype(BF16), "tp", scatter_dimension=1, tiled=True)


def solution(mesh):
    in_specs = (
        P("seq", None, "tp"),
        P(None, None, "tp"),
        P("tp", None),
        P("tp", None),
        P("tp"),
        P("seq", "tp"),
    )
    out_specs = P("seq", "tp")
    body = per_device_32 if (mesh.shape["seq"], mesh.shape["tp"]) == (8, 4) else per_device
    return jax.shard_map(body, mesh=mesh, in_specs=in_specs, out_specs=out_specs, check_vma=False)
```

```python
import functools

import jax
import jax.numpy as jnp
from jax import lax
from jax.experimental import pallas as pl
from jax.experimental.pallas import tpu as pltpu
from jax.sharding import PartitionSpec as P

LANES = 128
F32 = jnp.float32
BF16 = jnp.bfloat16
VMEM = pl.BlockSpec(memory_space=pltpu.VMEM)
SMEM = pl.BlockSpec(memory_space=pltpu.SMEM)
AXES = ("seq", "tp")


def cost(flops, bytes_accessed):
    return pl.CostEstimate(flops=flops, bytes_accessed=bytes_accessed, transcendentals=0)


def params(**kw):
    return pltpu.CompilerParams(vmem_limit_bytes=16 * 1024 * 1024, **kw)


def local_kernel(
    skip_ref, q_ref, k_ref, v_ref, taps_ref, rates_ref, residues_ref,
    out_ref, gate_ref, message_ref, table_ref,
    signal_s, conv_s, message_s,
):
    tokens, channels = q_ref.shape
    poles, taps = rates_ref.shape[0], taps_ref.shape[1]
    fold = channels // LANES
    edge = taps - 1
    tap_row = 2 * poles
    skip_row = tap_row + 3 * taps
    table_ref[skip_row * fold : (skip_row + 1) * fold, :] = skip_ref[...]
    later = lax.broadcasted_iota(jnp.int32, (tokens, LANES), 0) >= edge
    for j in range(fold):
        lanes = slice(j * LANES, (j + 1) * LANES)
        table_ref[pl.ds(j, poles, stride=fold), :] = rates_ref[:, lanes]
        table_ref[pl.ds(poles * fold + j, poles, stride=fold), :] = residues_ref[:, lanes]
        mixed = []
        for group, ref in enumerate((q_ref, k_ref, v_ref)):
            value = ref[:, lanes].astype(F32)
            total = None
            for shift in range(taps):
                row = (tap_row + group * taps + shift) * fold + j
                tap = taps_ref[group, shift : shift + 1, lanes].astype(F32)
                table_ref[row : row + 1, :] = tap
                moved = value if shift == 0 else pltpu.roll(value, shift, axis=0)
                total = tap * moved if total is None else total + tap * moved
            mixed.append(total)
            for place in range(2 * edge):
                source = place if place < edge else tokens - 2 * edge + place
                row = (poles + group * 2 * edge + place) * fold + j
                message_s[row : row + 1, :] = value[source : source + 1, :]
        gate_ref[:, lanes] = mixed[0]
        signal = jnp.where(later, mixed[1] * mixed[2], 0.0)
        signal_s[pl.ds(j, tokens, stride=fold), :] = signal
    decay = [jnp.exp(-table_ref[r * fold : (r + 1) * fold, :]) for r in range(poles)]
    residue = [table_ref[(poles + r) * fold : (poles + r + 1) * fold, :] for r in range(poles)]
    skip = table_ref[skip_row * fold : (skip_row + 1) * fold, :]

    def step(t, modes):
        rows = pl.ds(pl.multiple_of(t * fold, fold), fold)
        value = signal_s[rows, :]
        modes = tuple(d * m + c * value for d, c, m in zip(decay, residue, modes))
        conv_s[rows, :] = tree_sum(modes + (skip * value,))
        return modes

    modes = lax.fori_loop(0, tokens, step, (jnp.zeros((fold, LANES), F32),) * poles, unroll=4)
    for r in range(poles):
        message_s[r * fold : (r + 1) * fold, :] = modes[r]
    message_ref[...] = message_s[...].astype(BF16)
    for j in range(fold):
        lanes = slice(j * LANES, (j + 1) * LANES)
        conv = conv_s[pl.ds(j, tokens, stride=fold), :]
        out_ref[:, lanes] = (gate_ref[:, lanes] * conv).astype(BF16)


def tree_sum(values):
    values = list(values)
    while len(values) > 1:
        values = [a + b for a, b in zip(values[::2], values[1::2])] + (
            [values[-1]] if len(values) % 2 else []
        )
    return values[0]


def local_part(q, k, v, short_taps, rates, residues, skip):
    tokens, channels = q.shape
    poles, taps = rates.shape[1], short_taps.shape[1]
    fold = channels // LANES
    message_rows = (poles + 6 * (taps - 1)) * fold
    table_rows = (2 * poles + 3 * taps + 1) * fold
    return pl.pallas_call(
        local_kernel,
        out_shape=(
            jax.ShapeDtypeStruct((tokens, channels), BF16),
            jax.ShapeDtypeStruct((tokens, channels), F32),
            jax.ShapeDtypeStruct((message_rows, LANES), BF16),
            jax.ShapeDtypeStruct((table_rows, LANES), F32),
        ),
        in_specs=[VMEM] * 7,
        out_specs=(VMEM,) * 4,
        scratch_shapes=[
            pltpu.VMEM((tokens * fold, LANES), F32),
            pltpu.VMEM((tokens * fold, LANES), F32),
            pltpu.VMEM((message_rows, LANES), F32),
        ],
        compiler_params=params(),
        cost_estimate=cost(4 * tokens * channels * poles, 3 << 20),
        name="local_filter",
    )(skip.reshape(fold, LANES), q, k, v, short_taps, rates.T, residues.T)


class Table:
    def __init__(self, ref, poles, taps, fold, tokens, weights=None):
        self.ref, self.poles, self.taps, self.fold, self.edge = ref, poles, taps, fold, taps - 1
        self.rates = ref[0 : poles * fold, :].reshape(poles, fold, LANES)
        self.residues = ref[poles * fold : 2 * poles * fold, :].reshape(poles, fold, LANES)
        self.tap_base = 2 * poles * fold
        skip_base = self.tap_base + 3 * taps * fold
        self.skip = ref[skip_base : skip_base + fold, :]
        self.tokens = tokens
        self.weights = weights

    def span(self, shards):
        if self.weights is not None:
            return self.weights[shards.bit_length() - 1, 0]
        return jnp.exp(-self.rates * float(shards * self.tokens))

    def tap(self, group, shift):
        row = self.tap_base + (group * self.taps + shift) * self.fold
        return self.ref[row : row + self.fold, :]

    def message(self, value):
        return value.astype(F32).reshape(-1, self.fold, LANES)

    def first(self, message, group):
        base = self.poles + group * 2 * self.edge
        return [message[base + i] for i in range(self.edge)]

    def last(self, message, group):
        base = self.poles + group * 2 * self.edge + self.edge
        return [message[base + i] for i in range(self.edge)]

    def mixed(self, before, current, group):
        rows = self.last(before, group) + self.first(current, group)
        return [
            sum(self.tap(group, shift) * rows[self.edge + i - shift] for shift in range(self.taps))
            for i in range(self.edge)
        ]

    def signals(self, before, current):
        pairs = zip(self.mixed(before, current, 1), self.mixed(before, current, 2))
        return [k * v for k, v in pairs]

    def lead(self, shards):
        if self.weights is not None:
            return [self.weights[shards.bit_length() - 1, 1 + i] for i in range(self.edge)]
        last = shards * self.tokens - 1
        return [jnp.exp(-self.rates * float(last - i)) * self.residues for i in range(self.edge)]

    def enter(self, state, span, lead, before, current):
        state = span * state + current[: self.poles]
        for weight, value in zip(lead, self.signals(before, current)):
            state = state + weight * value[None]
        return state


def enter_any(table, place_ref, messages_ref):
    span, lead = table.span(1), table.lead(1)

    def pick(index):
        current = table.message(messages_ref[index])
        before = table.message(messages_ref[jnp.maximum(index - 1, 0)])
        return jnp.where(index > 0, before, 0.0), current

    def one(index, state):
        return table.enter(state, span, lead, *pick(index))

    zero = jnp.zeros((table.poles, table.fold, LANES), F32)
    state = lax.fori_loop(0, place_ref[0], one, zero)
    return (state,) + pick(place_ref[0])


def enter_joined(spans, table, place_ref, own_ref, other_ref, *refs):
    joined = [table.message(ref[...]) for ref in refs]
    own, other = table.message(own_ref[...]), table.message(other_ref[...])
    before = jnp.zeros_like(own)
    state = before[: table.poles]
    for shards, current in zip(spans[::-1], joined[::-1]):
        state = table.enter(state, table.span(shards), table.lead(shards), before, current)
        before = current
    second = place_ref[0] == 1
    behind = table.enter(state, table.span(1), table.lead(1), before, other)
    return jnp.where(second, behind, state), jnp.where(second, other, before), own


def join_kernel(poles, taps, tokens, place_ref, own_ref, other_ref, table_ref, out_ref):
    fold = own_ref.shape[0] // (poles + 6 * (taps - 1))
    table = Table(table_ref, poles, taps, fold, tokens)
    own, other = table.message(own_ref[...]), table.message(other_ref[...])
    second = place_ref[0] == 1
    before, current = jnp.where(second, other, own), jnp.where(second, own, other)
    state = table.enter(before[:poles], table.span(1), table.lead(1), before, current)
    out = [state[r] for r in range(poles)]
    for group in range(3):
        out += table.first(before, group) + table.last(current, group)
    out_ref[...] = jnp.concatenate(out, axis=0).astype(BF16)


def join_part(place, own, other, table, tokens, poles, taps):
    return pl.pallas_call(
        functools.partial(join_kernel, poles, taps, tokens),
        out_shape=jax.ShapeDtypeStruct(own.shape, BF16),
        in_specs=[SMEM] + [VMEM] * 3,
        out_specs=VMEM,
        compiler_params=params(),
        cost_estimate=cost(1 << 20, 1 << 18),
        name="join_state",
    )(place.reshape(1).astype(jnp.int32), own, other, table)


def weights_kernel(poles, taps, tokens, table_ref, out_ref):
    fold = out_ref.shape[3]
    table = Table(table_ref, poles, taps, fold, tokens)
    for i in range(out_ref.shape[0]):
        for j, weight in enumerate([table.span(1 << i)] + table.lead(1 << i)):
            out_ref[i, j] = weight


def weights_part(table, tokens, poles, taps, fold):
    return pl.pallas_call(
        functools.partial(weights_kernel, poles, taps, tokens),
        out_shape=jax.ShapeDtypeStruct((3, taps, poles, fold, LANES), F32),
        in_specs=[VMEM],
        out_specs=VMEM,
        compiler_params=params(),
        cost_estimate=cost(1 << 20, 1 << 20),
        name="state_weights",
    )(table)


def far_kernel(poles, taps, count, enter, place_ref, near_ref, gate_ref, table_ref, *refs):
    message_refs, weights_refs, (out_ref, conv_s) = refs[:count], refs[count:-2], refs[-2:]
    tokens, channels = near_ref.shape
    fold = channels // LANES
    table = Table(table_ref, poles, taps, fold, tokens, *weights_refs)
    edge = table.edge
    state, before, current = enter(table, place_ref, *message_refs)
    decay = [jnp.exp(-table.rates[r]) for r in range(poles)]
    modes = tuple(state[r] for r in range(poles))
    for t, value in enumerate(table.signals(before, current)):
        modes = tuple(decay[r] * modes[r] + table.residues[r] * value for r in range(poles))
        conv_s[t * fold : (t + 1) * fold, :] = tree_sum(modes + (table.skip * value,))

    def step(t, modes):
        modes = tuple(d * m for d, m in zip(decay, modes))
        conv_s[pl.ds(pl.multiple_of(t * fold, fold), fold), :] = tree_sum(modes)
        return modes

    lax.fori_loop(edge, tokens, step, modes, unroll=6)
    row_id = lax.broadcasted_iota(jnp.int32, (tokens, LANES), 0)
    first = table.mixed(before, current, 0)
    for j in range(fold):
        lanes = slice(j * LANES, (j + 1) * LANES)
        gate = gate_ref[:, lanes]
        for t in range(edge):
            gate = jnp.where(row_id == t, first[t][j : j + 1, :], gate)
        conv = conv_s[pl.ds(j, tokens, stride=fold), :]
        out_ref[:, lanes] = (near_ref[:, lanes].astype(F32) + gate * conv).astype(BF16)


def far_part(enter, place, near, gate, table, messages, poles, taps, weights=()):
    tokens, channels = near.shape
    fold = channels // LANES
    count = len(messages)
    return pl.pallas_call(
        functools.partial(far_kernel, poles, taps, count, enter),
        out_shape=jax.ShapeDtypeStruct((tokens, channels), BF16),
        in_specs=[SMEM] + [VMEM] * (3 + count + len(weights)),
        out_specs=VMEM,
        scratch_shapes=[pltpu.VMEM((tokens * fold, LANES), F32)],
        compiler_params=params(),
        cost_estimate=cost(4 * tokens * channels * poles, 3 << 20),
        name="far_filter",
    )(place.reshape(1).astype(jnp.int32), near, gate, table, *messages, *weights)


def project_kernel(given, place_ref, *refs):
    *rows_refs, own_ref, other_ref, out_ref = refs
    y, first = place_ref[0], place_ref[1]
    for i, rows_ref in enumerate(rows_refs):
        place = (first ^ i) if len(rows_refs) > 1 else 0
        if given and i == 0:
            out_ref[place] = rows_ref[0]
            continue
        for half, ref in ((y, own_ref), (1 - y, other_ref)):
            part = lax.dot_general(
                rows_ref[...], ref[...], (((1,), (1,)), ((), ())), preferred_element_type=F32
            )
            out_ref[place, half] = part.astype(BF16)


def project_part(place, rows, own, other, given=False):
    tokens, channels = rows[-1].shape
    width = own.shape[0]
    count = len(rows)
    return pl.pallas_call(
        functools.partial(project_kernel, given),
        out_shape=jax.ShapeDtypeStruct((count, 2, tokens, width), BF16),
        in_specs=[SMEM] + [VMEM] * (2 + count),
        out_specs=VMEM,
        compiler_params=params(),
        cost_estimate=cost(4 * count * tokens * channels * width, 3 << 20),
        name="project",
    )(place, *rows, own, other)


def finish_kernel(place_ref, *refs):
    out_ref = refs[-1]
    width = refs[0].shape[2]
    for pair in range((len(refs) - 1) // 2):

        @pl.when(place_ref[0] == pair)
        def _(pair=pair):
            for h in range(2):
                total = refs[2 * pair][h].astype(F32) + refs[2 * pair + 1][h].astype(F32)
                out_ref[:, h * width : (h + 1) * width] = total.astype(BF16)


def permute(name, x, move, keep=None):
    pairs = []
    for index in range(32):
        place = (index // 8, index // 4 % 2, index // 2 % 2, index % 2)
        if keep is None or keep(*place):
            z, y, x_, c = move(*place)
            pairs.append((index, ((z * 2 + y) * 2 + x_) * 2 + c))
    with jax.named_scope(name):
        return lax.ppermute(x, AXES, pairs)


def over_y(z, y, x, c):
    return z, 1 - y, x, c


def over_z0(z, y, x, c):
    return z ^ 1, y, x, c


def over_z1(z, y, x, c):
    return z ^ 2, y, x, c


def over_core(z, y, x, c):
    return z, y, x, 1 - c


def after(x, *others):
    return lax.optimization_barrier((x,) + others)[0]


def per_device_32(features, short_taps, rates, residues, skip, out_weight):
    tokens, _, channels = features.shape
    q, k, v = (features[:, group] for group in range(3))
    poles, taps = rates.shape[1], short_taps.shape[1]
    seq, tp = lax.axis_index("seq"), lax.axis_index("tp")
    z, y = seq >> 1, seq & 1
    near, gate, message, table = local_part(q, k, v, short_taps, rates, residues, skip)
    message_y = permute("state_y", message, over_y)
    pair = join_part(y, message, message_y, table, tokens, poles, taps)
    weights = weights_part(after(table, pair), tokens, poles, taps, channels // LANES)
    w_y = permute("weights", after(out_weight, weights), over_y)
    pair_z = permute("state_z1", pair, lambda z, y, x, c: (z + 1, y, x, c), lambda z, y, x, c: z + 1 < 4)
    four = join_part(jnp.ones((), jnp.int32), pair, pair_z, table, 2 * tokens, poles, taps)
    four_z = permute("state_z2", four, lambda z, y, x, c: (z + 2, y, x, c), lambda z, y, x, c: z + 2 < 4)
    enter = functools.partial(enter_joined, (2, 4))
    messages = [message, message_y, pair_z, four_z]
    gated = far_part(enter, y, near, gate, table, messages, poles, taps, [weights])
    two = permute("gated_two", gated, over_z1)
    one = permute("gated_one", gated, over_z0)
    three = permute("gated_three", two, over_z0)
    odd = (z ^ tp) & 1
    place = jnp.stack([y, odd]).astype(jnp.int32)

    def odd_of(z, y, x, c):
        return (z ^ c) % 2

    def home(summed, far):
        def move(z, y, x, c):
            return z ^ far ^ odd_of(z, y, x, c), y, z // 2, z % 2

        return [
            permute(f"across_{far}", summed, move, lambda z, y, x, c: x != z // 2),
            permute(f"straight_{far}", summed, move, lambda z, y, x, c: x == z // 2),
        ]

    def add_cores(name, kept, sent):
        from_core = permute(name, sent, over_core)
        return (kept.astype(F32) + from_core.astype(F32)).astype(BF16)

    part_two = project_part(place, [two], out_weight, w_y)
    near = project_part(place, [after(gated, part_two), one], out_weight, w_y)
    far = project_part(place, [part_two, after(three, near)], out_weight, w_y, given=True)
    far_sum = add_cores("core_far", far[0], far[1])
    near = after(near, far_sum)
    near_sum = add_cores("core_near", near[0], near[1])
    parts = home(far_sum, 2) + home(near_sum, 0)
    kind = 1 - ((z ^ tp) >> 1)
    return pl.pallas_call(
        finish_kernel,
        out_shape=jax.ShapeDtypeStruct((tokens, 2 * out_weight.shape[0]), BF16),
        in_specs=[SMEM] + [VMEM] * len(parts),
        out_specs=VMEM,
        compiler_params=params(),
        cost_estimate=cost(4 * tokens * out_weight.shape[0], 2 << 20),
        name="finish",
    )(kind.reshape(1).astype(jnp.int32), *parts)


def per_device(features, short_taps, rates, residues, skip, out_weight):
    q, k, v = (features[:, group] for group in range(3))
    poles, taps = rates.shape[1], short_taps.shape[1]
    near, gate, message, table = local_part(q, k, v, short_taps, rates, residues, skip)
    messages = lax.all_gather(message, "seq")
    place = lax.axis_index("seq")
    gated = far_part(enter_any, place, near, gate, table, [messages], poles, taps)
    partial = lax.dot_general(
        gated,
        lax.all_gather(out_weight, "seq", axis=0, tiled=True),
        (((1,), (1,)), ((), ())),
        preferred_element_type=F32,
    )
    return lax.psum_scatter(partial.astype(BF16), "tp", scatter_dimension=1, tiled=True)


def solution(mesh):
    in_specs = (
        P("seq", None, "tp"),
        P(None, None, "tp"),
        P("tp", None),
        P("tp", None),
        P("tp"),
        P("seq", "tp"),
    )
    out_specs = P("seq", "tp")
    body = per_device_32 if (mesh.shape["seq"], mesh.shape["tp"]) == (8, 4) else per_device
    return jax.shard_map(body, mesh=mesh, in_specs=in_specs, out_specs=out_specs, check_vma=False)
```

```python
import functools

import jax
import jax.numpy as jnp
from jax import lax
from jax.experimental import pallas as pl
from jax.experimental.pallas import tpu as pltpu
from jax.sharding import PartitionSpec as P

LANES = 128
F32 = jnp.float32
BF16 = jnp.bfloat16
VMEM = pl.BlockSpec(memory_space=pltpu.VMEM)
SMEM = pl.BlockSpec(memory_space=pltpu.SMEM)
AXES = ("seq", "tp")


def cost(flops, bytes_accessed):
    return pl.CostEstimate(flops=flops, bytes_accessed=bytes_accessed, transcendentals=0)


def params(**kw):
    return pltpu.CompilerParams(vmem_limit_bytes=16 * 1024 * 1024, **kw)


def local_kernel(
    skip_ref, q_ref, k_ref, v_ref, taps_ref, rates_ref, residues_ref,
    out_ref, gate_ref, message_ref, table_ref,
    signal_s, conv_s, message_s,
):
    tokens, channels = q_ref.shape
    poles, taps = rates_ref.shape[0], taps_ref.shape[1]
    fold = channels // LANES
    edge = taps - 1
    tap_row = 2 * poles
    skip_row = tap_row + 3 * taps
    table_ref[skip_row * fold : (skip_row + 1) * fold, :] = skip_ref[...]
    later = lax.broadcasted_iota(jnp.int32, (tokens, LANES), 0) >= edge
    for j in range(fold):
        lanes = slice(j * LANES, (j + 1) * LANES)
        table_ref[pl.ds(j, poles, stride=fold), :] = rates_ref[:, lanes]
        table_ref[pl.ds(poles * fold + j, poles, stride=fold), :] = residues_ref[:, lanes]
        mixed = []
        for group, ref in enumerate((q_ref, k_ref, v_ref)):
            value = ref[:, lanes].astype(F32)
            total = None
            for shift in range(taps):
                row = (tap_row + group * taps + shift) * fold + j
                tap = taps_ref[group, shift : shift + 1, lanes].astype(F32)
                table_ref[row : row + 1, :] = tap
                moved = value if shift == 0 else pltpu.roll(value, shift, axis=0)
                total = tap * moved if total is None else total + tap * moved
            mixed.append(total)
            for place in range(2 * edge):
                source = place if place < edge else tokens - 2 * edge + place
                row = (poles + group * 2 * edge + place) * fold + j
                message_s[row : row + 1, :] = value[source : source + 1, :]
        gate_ref[:, lanes] = mixed[0]
        signal = jnp.where(later, mixed[1] * mixed[2], 0.0)
        signal_s[pl.ds(j, tokens, stride=fold), :] = signal
    decay = [jnp.exp(-table_ref[r * fold : (r + 1) * fold, :]) for r in range(poles)]
    residue = [table_ref[(poles + r) * fold : (poles + r + 1) * fold, :] for r in range(poles)]
    skip = table_ref[skip_row * fold : (skip_row + 1) * fold, :]

    def step(t, modes):
        rows = pl.ds(pl.multiple_of(t * fold, fold), fold)
        value = signal_s[rows, :]
        modes = tuple(d * m + c * value for d, c, m in zip(decay, residue, modes))
        conv_s[rows, :] = tree_sum(modes + (skip * value,))
        return modes

    modes = lax.fori_loop(0, tokens, step, (jnp.zeros((fold, LANES), F32),) * poles, unroll=4)
    for r in range(poles):
        message_s[r * fold : (r + 1) * fold, :] = modes[r]
    message_ref[...] = message_s[...].astype(BF16)
    for j in range(fold):
        lanes = slice(j * LANES, (j + 1) * LANES)
        conv = conv_s[pl.ds(j, tokens, stride=fold), :]
        out_ref[:, lanes] = (gate_ref[:, lanes] * conv).astype(BF16)


def tree_sum(values):
    values = list(values)
    while len(values) > 1:
        values = [a + b for a, b in zip(values[::2], values[1::2])] + (
            [values[-1]] if len(values) % 2 else []
        )
    return values[0]


def local_part(q, k, v, short_taps, rates, residues, skip):
    tokens, channels = q.shape
    poles, taps = rates.shape[1], short_taps.shape[1]
    fold = channels // LANES
    message_rows = (poles + 6 * (taps - 1)) * fold
    table_rows = (2 * poles + 3 * taps + 1) * fold
    return pl.pallas_call(
        local_kernel,
        out_shape=(
            jax.ShapeDtypeStruct((tokens, channels), BF16),
            jax.ShapeDtypeStruct((tokens, channels), F32),
            jax.ShapeDtypeStruct((message_rows, LANES), BF16),
            jax.ShapeDtypeStruct((table_rows, LANES), F32),
        ),
        in_specs=[VMEM] * 7,
        out_specs=(VMEM,) * 4,
        scratch_shapes=[
            pltpu.VMEM((tokens * fold, LANES), F32),
            pltpu.VMEM((tokens * fold, LANES), F32),
            pltpu.VMEM((message_rows, LANES), F32),
        ],
        compiler_params=params(),
        cost_estimate=cost(4 * tokens * channels * poles, 3 << 20),
        name="local_filter",
    )(skip.reshape(fold, LANES), q, k, v, short_taps, rates.T, residues.T)


class Table:
    def __init__(self, ref, poles, taps, fold, tokens, weights=None):
        self.ref, self.poles, self.taps, self.fold, self.edge = ref, poles, taps, fold, taps - 1
        self.rates = ref[0 : poles * fold, :].reshape(poles, fold, LANES)
        self.residues = ref[poles * fold : 2 * poles * fold, :].reshape(poles, fold, LANES)
        self.tap_base = 2 * poles * fold
        skip_base = self.tap_base + 3 * taps * fold
        self.skip = ref[skip_base : skip_base + fold, :]
        self.tokens = tokens
        self.weights = weights

    def span(self, shards):
        if self.weights is not None:
            return self.weights[shards // 4, 0]
        return jnp.exp(-self.rates * float(shards * self.tokens))

    def tap(self, group, shift):
        row = self.tap_base + (group * self.taps + shift) * self.fold
        return self.ref[row : row + self.fold, :]

    def message(self, value):
        return value.astype(F32).reshape(-1, self.fold, LANES)

    def first(self, message, group):
        base = self.poles + group * 2 * self.edge
        return [message[base + i] for i in range(self.edge)]

    def last(self, message, group):
        base = self.poles + group * 2 * self.edge + self.edge
        return [message[base + i] for i in range(self.edge)]

    def mixed(self, before, current, group):
        rows = self.last(before, group) + self.first(current, group)
        return [
            sum(self.tap(group, shift) * rows[self.edge + i - shift] for shift in range(self.taps))
            for i in range(self.edge)
        ]

    def signals(self, before, current):
        pairs = zip(self.mixed(before, current, 1), self.mixed(before, current, 2))
        return [k * v for k, v in pairs]

    def lead(self, shards):
        if self.weights is not None:
            return [self.weights[shards // 4, 1 + i] for i in range(self.edge)]
        last = shards * self.tokens - 1
        return [jnp.exp(-self.rates * float(last - i)) * self.residues for i in range(self.edge)]

    def enter(self, state, span, lead, before, current):
        state = span * state + current[: self.poles]
        for weight, value in zip(lead, self.signals(before, current)):
            state = state + weight * value[None]
        return state


def enter_any(table, place_ref, messages_ref):
    span, lead = table.span(1), table.lead(1)

    def pick(index):
        current = table.message(messages_ref[index])
        before = table.message(messages_ref[jnp.maximum(index - 1, 0)])
        return jnp.where(index > 0, before, 0.0), current

    def one(index, state):
        return table.enter(state, span, lead, *pick(index))

    zero = jnp.zeros((table.poles, table.fold, LANES), F32)
    state = lax.fori_loop(0, place_ref[0], one, zero)
    return (state,) + pick(place_ref[0])


def in_order(place, values):
    out = []
    for p in range(4):
        value = values[p]
        for g in range(1, 4):
            value = jnp.where(place == g, values[p ^ g], value)
        out.append(value)
    return out


def enter_group(table, place_ref, *refs):
    messages = [table.message(ref[...]) for ref in refs]
    place, group = place_ref[0], in_order(place_ref[0], messages[:4])
    before = jnp.zeros_like(messages[4])
    state = table.enter(before[: table.poles], table.span(4), table.lead(4), before, messages[4])
    before = messages[4]
    for p in range(3):
        behind = table.enter(state, table.span(1), table.lead(1), before, group[p])
        state = jnp.where(p < place, behind, state)
        before = jnp.where(p < place, group[p], before)
    return state, before, messages[0]


def join_kernel(poles, taps, tokens, place_ref, *refs):
    *message_refs, table_ref, out_ref = refs
    fold = out_ref.shape[0] // (poles + 6 * (taps - 1))
    table = Table(table_ref, poles, taps, fold, tokens)
    group = in_order(place_ref[0], [table.message(ref[...]) for ref in message_refs])
    span, lead = table.span(1), table.lead(1)
    state = group[0][:poles]
    for before, current in zip(group[:-1], group[1:]):
        state = table.enter(state, span, lead, before, current)
    out = [state[r] for r in range(poles)]
    for kind in range(3):
        out += table.first(group[0], kind) + table.last(group[3], kind)
    out_ref[...] = jnp.concatenate(out, axis=0).astype(BF16)


def join_part(place, messages, table, tokens, poles, taps):
    return pl.pallas_call(
        functools.partial(join_kernel, poles, taps, tokens),
        out_shape=jax.ShapeDtypeStruct(messages[0].shape, BF16),
        in_specs=[SMEM] + [VMEM] * 5,
        out_specs=VMEM,
        compiler_params=params(),
        cost_estimate=cost(1 << 20, 1 << 18),
        name="join_state",
    )(place.reshape(1).astype(jnp.int32), *messages, table)


def weights_kernel(poles, taps, tokens, table_ref, out_ref):
    fold = out_ref.shape[3]
    table = Table(table_ref, poles, taps, fold, tokens)
    for i, shards in enumerate((1, 4)):
        for j, weight in enumerate([table.span(shards)] + table.lead(shards)):
            out_ref[i, j] = weight


def weights_part(table, tokens, poles, taps, fold):
    return pl.pallas_call(
        functools.partial(weights_kernel, poles, taps, tokens),
        out_shape=jax.ShapeDtypeStruct((2, taps, poles, fold, LANES), F32),
        in_specs=[VMEM],
        out_specs=VMEM,
        compiler_params=params(),
        cost_estimate=cost(1 << 20, 1 << 20),
        name="state_weights",
    )(table)


def far_kernel(poles, taps, count, enter, place_ref, near_ref, gate_ref, table_ref, *refs):
    message_refs, weights_refs, (out_ref, conv_s) = refs[:count], refs[count:-2], refs[-2:]
    tokens, channels = near_ref.shape
    fold = channels // LANES
    table = Table(table_ref, poles, taps, fold, tokens, *weights_refs)
    edge = table.edge
    state, before, current = enter(table, place_ref, *message_refs)
    decay = [jnp.exp(-table.rates[r]) for r in range(poles)]
    modes = tuple(state[r] for r in range(poles))
    for t, value in enumerate(table.signals(before, current)):
        modes = tuple(decay[r] * modes[r] + table.residues[r] * value for r in range(poles))
        conv_s[t * fold : (t + 1) * fold, :] = tree_sum(modes + (table.skip * value,))

    def step(t, modes):
        modes = tuple(d * m for d, m in zip(decay, modes))
        conv_s[pl.ds(pl.multiple_of(t * fold, fold), fold), :] = tree_sum(modes)
        return modes

    lax.fori_loop(edge, tokens, step, modes, unroll=6)
    row_id = lax.broadcasted_iota(jnp.int32, (tokens, LANES), 0)
    first = table.mixed(before, current, 0)
    for j in range(fold):
        lanes = slice(j * LANES, (j + 1) * LANES)
        gate = gate_ref[:, lanes]
        for t in range(edge):
            gate = jnp.where(row_id == t, first[t][j : j + 1, :], gate)
        conv = conv_s[pl.ds(j, tokens, stride=fold), :]
        out_ref[:, lanes] = (near_ref[:, lanes].astype(F32) + gate * conv).astype(BF16)


def far_part(enter, place, near, gate, table, messages, poles, taps, weights=()):
    tokens, channels = near.shape
    fold = channels // LANES
    count = len(messages)
    return pl.pallas_call(
        functools.partial(far_kernel, poles, taps, count, enter),
        out_shape=jax.ShapeDtypeStruct((tokens, channels), BF16),
        in_specs=[SMEM] + [VMEM] * (3 + count + len(weights)),
        out_specs=VMEM,
        scratch_shapes=[pltpu.VMEM((tokens * fold, LANES), F32)],
        compiler_params=params(),
        cost_estimate=cost(4 * tokens * channels * poles, 3 << 20),
        name="far_filter",
    )(place.reshape(1).astype(jnp.int32), near, gate, table, *messages, *weights)


def project_kernel(given, place_ref, *refs):
    *rows_refs, own_ref, other_ref, out_ref = refs
    y, first = place_ref[0], place_ref[1]
    for i, rows_ref in enumerate(rows_refs):
        place = (first ^ i) if len(rows_refs) > 1 else 0
        if given and i == 0:
            out_ref[place] = rows_ref[0]
            continue
        for half, ref in ((y, own_ref), (1 - y, other_ref)):
            part = lax.dot_general(
                rows_ref[...], ref[...], (((1,), (1,)), ((), ())), preferred_element_type=F32
            )
            out_ref[place, half] = part.astype(BF16)


def project_part(place, rows, own, other, given=False):
    tokens, channels = rows[-1].shape
    width = own.shape[0]
    count = len(rows)
    return pl.pallas_call(
        functools.partial(project_kernel, given),
        out_shape=jax.ShapeDtypeStruct((count, 2, tokens, width), BF16),
        in_specs=[SMEM] + [VMEM] * (2 + count),
        out_specs=VMEM,
        compiler_params=params(),
        cost_estimate=cost(4 * count * tokens * channels * width, 3 << 20),
        name="project",
    )(place, *rows, own, other)


def finish_kernel(place_ref, *refs):
    out_ref = refs[-1]
    width = refs[0].shape[2]
    for pair in range((len(refs) - 1) // 2):

        @pl.when(place_ref[0] == pair)
        def _(pair=pair):
            for h in range(2):
                total = refs[2 * pair][h].astype(F32) + refs[2 * pair + 1][h].astype(F32)
                out_ref[:, h * width : (h + 1) * width] = total.astype(BF16)


def permute(name, x, move, keep=None):
    pairs = []
    for index in range(32):
        place = (index // 8, index // 4 % 2, index // 2 % 2, index % 2)
        if keep is None or keep(*place):
            z, y, x_, c = move(*place)
            pairs.append((index, ((z * 2 + y) * 2 + x_) * 2 + c))
    with jax.named_scope(name):
        return lax.ppermute(x, AXES, pairs)


def over_y(z, y, x, c):
    return z, 1 - y, x, c


def over_z0(z, y, x, c):
    return z ^ 1, y, x, c


def over_z1(z, y, x, c):
    return z ^ 2, y, x, c


def over_core(z, y, x, c):
    return z, y, x, 1 - c


def after(x, *others):
    return lax.optimization_barrier((x,) + others)[0]


def per_device_32(features, short_taps, rates, residues, skip, out_weight):
    tokens, _, channels = features.shape
    q, k, v = (features[:, group] for group in range(3))
    poles, taps = rates.shape[1], short_taps.shape[1]
    seq, tp = lax.axis_index("seq"), lax.axis_index("tp")
    z, y = seq >> 1, seq & 1
    near, gate, message, table = local_part(q, k, v, short_taps, rates, residues, skip)
    messages = [
        message,
        permute("state_y", message, over_y),
        permute("state_z", message, over_z0),
        permute("state_zy", message, lambda z, y, x, c: (z ^ 1, 1 - y, x, c)),
    ]
    place = seq & 3
    joined = join_part(place, messages, table, tokens, poles, taps)
    weights = weights_part(after(table, joined), tokens, poles, taps, channels // LANES)
    w_y = permute("weights", after(out_weight, weights), over_y)
    joined = permute("state_half", joined, over_z1, lambda z, y, x, c: z < 2)
    gated = far_part(
        enter_group, place, near, gate, table, messages + [joined], poles, taps, [weights]
    )
    two = permute("gated_two", gated, over_z1)
    one = permute("gated_one", gated, over_z0)
    three = permute("gated_three", two, over_z0)
    odd = (z ^ tp) & 1
    place = jnp.stack([y, odd]).astype(jnp.int32)

    def odd_of(z, y, x, c):
        return (z ^ c) % 2

    def home(summed, far):
        def move(z, y, x, c):
            return z ^ far ^ odd_of(z, y, x, c), y, z // 2, z % 2

        return [
            permute(f"across_{far}", summed, move, lambda z, y, x, c: x != z // 2),
            permute(f"straight_{far}", summed, move, lambda z, y, x, c: x == z // 2),
        ]

    def add_cores(name, kept, sent):
        from_core = permute(name, sent, over_core)
        return (kept.astype(F32) + from_core.astype(F32)).astype(BF16)

    part_two = project_part(place, [two], out_weight, w_y)
    near = project_part(place, [after(gated, part_two), one], out_weight, w_y)
    far = project_part(place, [part_two, after(three, near)], out_weight, w_y, given=True)
    far_sum = add_cores("core_far", far[0], far[1])
    near = after(near, far_sum)
    near_sum = add_cores("core_near", near[0], near[1])
    parts = home(far_sum, 2) + home(near_sum, 0)
    kind = 1 - ((z ^ tp) >> 1)
    return pl.pallas_call(
        finish_kernel,
        out_shape=jax.ShapeDtypeStruct((tokens, 2 * out_weight.shape[0]), BF16),
        in_specs=[SMEM] + [VMEM] * len(parts),
        out_specs=VMEM,
        compiler_params=params(),
        cost_estimate=cost(4 * tokens * out_weight.shape[0], 2 << 20),
        name="finish",
    )(kind.reshape(1).astype(jnp.int32), *parts)


def per_device(features, short_taps, rates, residues, skip, out_weight):
    q, k, v = (features[:, group] for group in range(3))
    poles, taps = rates.shape[1], short_taps.shape[1]
    near, gate, message, table = local_part(q, k, v, short_taps, rates, residues, skip)
    messages = lax.all_gather(message, "seq")
    place = lax.axis_index("seq")
    gated = far_part(enter_any, place, near, gate, table, [messages], poles, taps)
    partial = lax.dot_general(
        gated,
        lax.all_gather(out_weight, "seq", axis=0, tiled=True),
        (((1,), (1,)), ((), ())),
        preferred_element_type=F32,
    )
    return lax.psum_scatter(partial.astype(BF16), "tp", scatter_dimension=1, tiled=True)


def solution(mesh):
    in_specs = (
        P("seq", None, "tp"),
        P(None, None, "tp"),
        P("tp", None),
        P("tp", None),
        P("tp"),
        P("seq", "tp"),
    )
    out_specs = P("seq", "tp")
    body = per_device_32 if (mesh.shape["seq"], mesh.shape["tp"]) == (8, 4) else per_device
    return jax.shard_map(body, mesh=mesh, in_specs=in_specs, out_specs=out_specs, check_vma=False)
```

```python
import functools

import jax
import jax.numpy as jnp
from jax import lax
from jax.experimental import pallas as pl
from jax.experimental.pallas import tpu as pltpu
from jax.sharding import PartitionSpec as P

LANES = 128
SUBLANES = 16
F32 = jnp.float32
BF16 = jnp.bfloat16
VMEM = pl.BlockSpec(memory_space=pltpu.VMEM)
SMEM = pl.BlockSpec(memory_space=pltpu.SMEM)
AXES = ("seq", "tp")


def cost(flops, bytes_accessed):
    return pl.CostEstimate(flops=flops, bytes_accessed=bytes_accessed, transcendentals=0)


def params(**kw):
    return pltpu.CompilerParams(vmem_limit_bytes=16 * 1024 * 1024, **kw)


def signal_kernel(
    skip_ref, q_ref, k_ref, v_ref, taps_ref, rates_ref, residues_ref,
    signal_ref, message_ref, table_ref,
    message_s,
):
    tokens, channels = q_ref.shape
    poles, taps = rates_ref.shape[0], taps_ref.shape[1]
    fold = channels // LANES
    edge = taps - 1
    tap_row = 2 * poles
    skip_row = tap_row + 3 * taps
    table_ref[skip_row * fold : (skip_row + 1) * fold, :] = skip_ref[...]
    later = lax.broadcasted_iota(jnp.int32, (tokens, LANES), 0) >= edge
    for j in range(fold):
        lanes = slice(j * LANES, (j + 1) * LANES)
        table_ref[pl.ds(j, poles, stride=fold), :] = rates_ref[:, lanes]
        table_ref[pl.ds(poles * fold + j, poles, stride=fold), :] = residues_ref[:, lanes]
        mixed = []
        for group, ref in enumerate((q_ref, k_ref, v_ref)):
            total = None
            value = ref[:, lanes].astype(F32) if group else None
            for shift in range(taps):
                row = (tap_row + group * taps + shift) * fold + j
                tap = taps_ref[group, shift : shift + 1, lanes].astype(F32)
                table_ref[row : row + 1, :] = tap
                if group:
                    moved = value if shift == 0 else pltpu.roll(value, shift, axis=0)
                    total = tap * moved if total is None else total + tap * moved
            mixed.append(total)
            first, last = ref[:SUBLANES, lanes].astype(F32), ref[-SUBLANES:, lanes].astype(F32)
            for place in range(2 * edge):
                row = (poles + group * 2 * edge + place) * fold + j
                source = place if place < edge else SUBLANES - 2 * edge + place
                source_rows = first if place < edge else last
                message_s[row : row + 1, :] = source_rows[source : source + 1, :]
        signal = jnp.where(later, mixed[1] * mixed[2], 0.0)
        signal_ref[pl.ds(j, tokens, stride=fold), :] = signal
    decay = [jnp.exp(-table_ref[r * fold : (r + 1) * fold, :]) for r in range(poles)]

    def step(t, modes):
        value = signal_ref[pl.ds(pl.multiple_of(t * fold, fold), fold), :]
        return tuple(d * m + value for d, m in zip(decay, modes))

    modes = lax.fori_loop(0, tokens, step, (jnp.zeros((fold, LANES), F32),) * poles, unroll=8)
    for r in range(poles):
        residue = table_ref[(poles + r) * fold : (poles + r + 1) * fold, :]
        message_s[r * fold : (r + 1) * fold, :] = residue * modes[r]
    message_ref[...] = message_s[...].astype(BF16)


def near_kernel(poles, taps, q_ref, signal_ref, table_ref, out_ref, gate_ref, conv_s):
    tokens, channels = q_ref.shape
    fold = channels // LANES
    tap_row = 2 * poles
    skip_row = tap_row + 3 * taps
    decay = [jnp.exp(-table_ref[r * fold : (r + 1) * fold, :]) for r in range(poles)]
    residue = [table_ref[(poles + r) * fold : (poles + r + 1) * fold, :] for r in range(poles)]
    skip = table_ref[skip_row * fold : (skip_row + 1) * fold, :]

    def step(t, modes):
        rows = pl.ds(pl.multiple_of(t * fold, fold), fold)
        value = signal_ref[rows, :]
        modes = tuple(d * m + c * value for d, c, m in zip(decay, residue, modes))
        conv_s[rows, :] = tree_sum(modes + (skip * value,))
        return modes

    lax.fori_loop(0, tokens, step, (jnp.zeros((fold, LANES), F32),) * poles, unroll=4)
    for j in range(fold):
        lanes = slice(j * LANES, (j + 1) * LANES)
        value = q_ref[:, lanes].astype(F32)
        gate = None
        for shift in range(taps):
            row = (tap_row + shift) * fold + j
            moved = value if shift == 0 else pltpu.roll(value, shift, axis=0)
            term = table_ref[row : row + 1, :] * moved
            gate = term if gate is None else gate + term
        gate_ref[:, lanes] = gate
        conv = conv_s[pl.ds(j, tokens, stride=fold), :]
        out_ref[:, lanes] = (gate * conv).astype(BF16)


def tree_sum(values):
    values = list(values)
    while len(values) > 1:
        values = [a + b for a, b in zip(values[::2], values[1::2])] + (
            [values[-1]] if len(values) % 2 else []
        )
    return values[0]


def signal_part(q, k, v, short_taps, rates, residues, skip):
    tokens, channels = q.shape
    poles, taps = rates.shape[1], short_taps.shape[1]
    fold = channels // LANES
    message_rows = (poles + 6 * (taps - 1)) * fold
    table_rows = (2 * poles + 3 * taps + 1) * fold
    return pl.pallas_call(
        signal_kernel,
        out_shape=(
            jax.ShapeDtypeStruct((tokens * fold, LANES), F32),
            jax.ShapeDtypeStruct((message_rows, LANES), BF16),
            jax.ShapeDtypeStruct((table_rows, LANES), F32),
        ),
        in_specs=[VMEM] * 7,
        out_specs=(VMEM,) * 3,
        scratch_shapes=[pltpu.VMEM((message_rows, LANES), F32)],
        compiler_params=params(),
        cost_estimate=cost(2 * tokens * channels * poles, 2 << 20),
        name="signal",
    )(skip.reshape(fold, LANES), q, k, v, short_taps, rates.T, residues.T)


def near_part(q, signal, table, poles, taps):
    tokens, channels = q.shape
    return pl.pallas_call(
        functools.partial(near_kernel, poles, taps),
        out_shape=(
            jax.ShapeDtypeStruct((tokens, channels), BF16),
            jax.ShapeDtypeStruct((tokens, channels), F32),
        ),
        in_specs=[VMEM] * 3,
        out_specs=(VMEM,) * 2,
        scratch_shapes=[pltpu.VMEM(signal.shape, F32)],
        compiler_params=params(),
        cost_estimate=cost(4 * tokens * channels * poles, 2 << 20),
        name="near_filter",
    )(q, signal, table)


class Table:
    def __init__(self, ref, poles, taps, fold, tokens, weights=None):
        self.ref, self.poles, self.taps, self.fold, self.edge = ref, poles, taps, fold, taps - 1
        self.rates = ref[0 : poles * fold, :].reshape(poles, fold, LANES)
        self.residues = ref[poles * fold : 2 * poles * fold, :].reshape(poles, fold, LANES)
        self.tap_base = 2 * poles * fold
        skip_base = self.tap_base + 3 * taps * fold
        self.skip = ref[skip_base : skip_base + fold, :]
        self.tokens = tokens
        self.weights = weights

    def span(self, shards):
        if self.weights is not None:
            return self.weights[shards // 4, 0]
        return jnp.exp(-self.rates * float(shards * self.tokens))

    def tap(self, group, shift):
        row = self.tap_base + (group * self.taps + shift) * self.fold
        return self.ref[row : row + self.fold, :]

    def message(self, value):
        return value.astype(F32).reshape(-1, self.fold, LANES)

    def first(self, message, group):
        base = self.poles + group * 2 * self.edge
        return [message[base + i] for i in range(self.edge)]

    def last(self, message, group):
        base = self.poles + group * 2 * self.edge + self.edge
        return [message[base + i] for i in range(self.edge)]

    def mixed(self, before, current, group):
        rows = self.last(before, group) + self.first(current, group)
        return [
            sum(self.tap(group, shift) * rows[self.edge + i - shift] for shift in range(self.taps))
            for i in range(self.edge)
        ]

    def signals(self, before, current):
        pairs = zip(self.mixed(before, current, 1), self.mixed(before, current, 2))
        return [k * v for k, v in pairs]

    def lead(self, shards):
        if self.weights is not None:
            return [self.weights[shards // 4, 1 + i] for i in range(self.edge)]
        last = shards * self.tokens - 1
        return [jnp.exp(-self.rates * float(last - i)) * self.residues for i in range(self.edge)]

    def enter(self, state, span, lead, before, current):
        state = span * state + current[: self.poles]
        for weight, value in zip(lead, self.signals(before, current)):
            state = state + weight * value[None]
        return state


def enter_any(table, place_ref, messages_ref):
    span, lead = table.span(1), table.lead(1)

    def pick(index):
        current = table.message(messages_ref[index])
        before = table.message(messages_ref[jnp.maximum(index - 1, 0)])
        return jnp.where(index > 0, before, 0.0), current

    def one(index, state):
        return table.enter(state, span, lead, *pick(index))

    zero = jnp.zeros((table.poles, table.fold, LANES), F32)
    state = lax.fori_loop(0, place_ref[0], one, zero)
    return (state,) + pick(place_ref[0])


def in_order(place, values):
    out = []
    for p in range(4):
        value = values[p]
        for g in range(1, 4):
            value = jnp.where(place == g, values[p ^ g], value)
        out.append(value)
    return out


def enter_group(table, place_ref, *refs):
    messages = [table.message(ref[...]) for ref in refs]
    place, group = place_ref[0], in_order(place_ref[0], messages[:4])
    before = jnp.zeros_like(messages[4])
    state = table.enter(before[: table.poles], table.span(4), table.lead(4), before, messages[4])
    before = messages[4]
    for p in range(3):
        behind = table.enter(state, table.span(1), table.lead(1), before, group[p])
        state = jnp.where(p < place, behind, state)
        before = jnp.where(p < place, group[p], before)
    return state, before, messages[0]


def join_kernel(poles, taps, tokens, place_ref, *refs):
    *message_refs, table_ref, out_ref = refs
    fold = out_ref.shape[0] // (poles + 6 * (taps - 1))
    table = Table(table_ref, poles, taps, fold, tokens)
    group = in_order(place_ref[0], [table.message(ref[...]) for ref in message_refs])
    span, lead = table.span(1), table.lead(1)
    state = group[0][:poles]
    for before, current in zip(group[:-1], group[1:]):
        state = table.enter(state, span, lead, before, current)
    out = [state[r] for r in range(poles)]
    for kind in range(3):
        out += table.first(group[0], kind) + table.last(group[3], kind)
    out_ref[...] = jnp.concatenate(out, axis=0).astype(BF16)


def join_part(place, messages, table, tokens, poles, taps):
    return pl.pallas_call(
        functools.partial(join_kernel, poles, taps, tokens),
        out_shape=jax.ShapeDtypeStruct(messages[0].shape, BF16),
        in_specs=[SMEM] + [VMEM] * 5,
        out_specs=VMEM,
        compiler_params=params(),
        cost_estimate=cost(1 << 20, 1 << 18),
        name="join_state",
    )(place.reshape(1).astype(jnp.int32), *messages, table)


def weights_kernel(poles, taps, tokens, table_ref, out_ref):
    fold = out_ref.shape[3]
    table = Table(table_ref, poles, taps, fold, tokens)
    for i, shards in enumerate((1, 4)):
        for j, weight in enumerate([table.span(shards)] + table.lead(shards)):
            out_ref[i, j] = weight


def weights_part(table, tokens, poles, taps, fold):
    return pl.pallas_call(
        functools.partial(weights_kernel, poles, taps, tokens),
        out_shape=jax.ShapeDtypeStruct((2, taps, poles, fold, LANES), F32),
        in_specs=[VMEM],
        out_specs=VMEM,
        compiler_params=params(),
        cost_estimate=cost(1 << 20, 1 << 20),
        name="state_weights",
    )(table)


def far_kernel(poles, taps, count, enter, place_ref, near_ref, gate_ref, table_ref, *refs):
    message_refs, weights_refs, (out_ref, conv_s) = refs[:count], refs[count:-2], refs[-2:]
    tokens, channels = near_ref.shape
    fold = channels // LANES
    table = Table(table_ref, poles, taps, fold, tokens, *weights_refs)
    edge = table.edge
    state, before, current = enter(table, place_ref, *message_refs)
    decay = [jnp.exp(-table.rates[r]) for r in range(poles)]
    modes = tuple(state[r] for r in range(poles))
    for t, value in enumerate(table.signals(before, current)):
        modes = tuple(decay[r] * modes[r] + table.residues[r] * value for r in range(poles))
        conv_s[t * fold : (t + 1) * fold, :] = tree_sum(modes + (table.skip * value,))

    def step(t, modes):
        modes = tuple(d * m for d, m in zip(decay, modes))
        conv_s[pl.ds(pl.multiple_of(t * fold, fold), fold), :] = tree_sum(modes)
        return modes

    lax.fori_loop(edge, tokens, step, modes, unroll=6)
    row_id = lax.broadcasted_iota(jnp.int32, (tokens, LANES), 0)
    first = table.mixed(before, current, 0)
    for j in range(fold):
        lanes = slice(j * LANES, (j + 1) * LANES)
        gate = gate_ref[:, lanes]
        for t in range(edge):
            gate = jnp.where(row_id == t, first[t][j : j + 1, :], gate)
        conv = conv_s[pl.ds(j, tokens, stride=fold), :]
        out_ref[:, lanes] = (near_ref[:, lanes].astype(F32) + gate * conv).astype(BF16)


def far_part(enter, place, near, gate, table, messages, poles, taps, weights=()):
    tokens, channels = near.shape
    fold = channels // LANES
    count = len(messages)
    return pl.pallas_call(
        functools.partial(far_kernel, poles, taps, count, enter),
        out_shape=jax.ShapeDtypeStruct((tokens, channels), BF16),
        in_specs=[SMEM] + [VMEM] * (3 + count + len(weights)),
        out_specs=VMEM,
        scratch_shapes=[pltpu.VMEM((tokens * fold, LANES), F32)],
        compiler_params=params(),
        cost_estimate=cost(4 * tokens * channels * poles, 3 << 20),
        name="far_filter",
    )(place.reshape(1).astype(jnp.int32), near, gate, table, *messages, *weights)


def project_kernel(given, place_ref, *refs):
    *rows_refs, own_ref, other_ref, out_ref = refs
    y, first = place_ref[0], place_ref[1]
    for i, rows_ref in enumerate(rows_refs):
        place = (first ^ i) if len(rows_refs) > 1 else 0
        if given and i == 0:
            out_ref[place] = rows_ref[0]
            continue
        for half, ref in ((y, own_ref), (1 - y, other_ref)):
            part = lax.dot_general(
                rows_ref[...], ref[...], (((1,), (1,)), ((), ())), preferred_element_type=F32
            )
            out_ref[place, half] = part.astype(BF16)


def project_part(place, rows, own, other, given=False):
    tokens, channels = rows[-1].shape
    width = own.shape[0]
    count = len(rows)
    return pl.pallas_call(
        functools.partial(project_kernel, given),
        out_shape=jax.ShapeDtypeStruct((count, 2, tokens, width), BF16),
        in_specs=[SMEM] + [VMEM] * (2 + count),
        out_specs=VMEM,
        compiler_params=params(),
        cost_estimate=cost(4 * count * tokens * channels * width, 3 << 20),
        name="project",
    )(place, *rows, own, other)


def finish_kernel(place_ref, *refs):
    out_ref = refs[-1]
    width = refs[0].shape[2]
    for pair in range((len(refs) - 1) // 2):

        @pl.when(place_ref[0] == pair)
        def _(pair=pair):
            for h in range(2):
                total = refs[2 * pair][h].astype(F32) + refs[2 * pair + 1][h].astype(F32)
                out_ref[:, h * width : (h + 1) * width] = total.astype(BF16)


def permute(name, x, move, keep=None):
    pairs = []
    for index in range(32):
        place = (index // 8, index // 4 % 2, index // 2 % 2, index % 2)
        if keep is None or keep(*place):
            z, y, x_, c = move(*place)
            pairs.append((index, ((z * 2 + y) * 2 + x_) * 2 + c))
    with jax.named_scope(name):
        return lax.ppermute(x, AXES, pairs)


def over_y(z, y, x, c):
    return z, 1 - y, x, c


def over_z0(z, y, x, c):
    return z ^ 1, y, x, c


def over_z1(z, y, x, c):
    return z ^ 2, y, x, c


def over_core(z, y, x, c):
    return z, y, x, 1 - c


def after(x, *others):
    return lax.optimization_barrier((x,) + others)[0]


def per_device_32(features, short_taps, rates, residues, skip, out_weight):
    tokens, _, channels = features.shape
    q, k, v = (features[:, group] for group in range(3))
    poles, taps = rates.shape[1], short_taps.shape[1]
    seq, tp = lax.axis_index("seq"), lax.axis_index("tp")
    z, y = seq >> 1, seq & 1
    signal, message, table = signal_part(q, k, v, short_taps, rates, residues, skip)
    near, gate = near_part(q, signal, table, poles, taps)
    messages = [
        message,
        permute("state_y", message, over_y),
        permute("state_z", message, over_z0),
        permute("state_zy", message, lambda z, y, x, c: (z ^ 1, 1 - y, x, c)),
    ]
    place = seq & 3
    joined = join_part(place, messages, table, tokens, poles, taps)
    weights = weights_part(after(table, joined), tokens, poles, taps, channels // LANES)
    w_y = permute("weights", after(out_weight, weights), over_y)
    joined = permute("state_half", joined, over_z1, lambda z, y, x, c: z < 2)
    gated = far_part(
        enter_group, place, near, gate, table, messages + [joined], poles, taps, [weights]
    )
    two = permute("gated_two", gated, over_z1)
    one = permute("gated_one", gated, over_z0)
    three = permute("gated_three", two, over_z0)
    odd = (z ^ tp) & 1
    place = jnp.stack([y, odd]).astype(jnp.int32)

    def odd_of(z, y, x, c):
        return (z ^ c) % 2

    def home(summed, far):
        def move(z, y, x, c):
            return z ^ far ^ odd_of(z, y, x, c), y, z // 2, z % 2

        return [
            permute(f"across_{far}", summed, move, lambda z, y, x, c: x != z // 2),
            permute(f"straight_{far}", summed, move, lambda z, y, x, c: x == z // 2),
        ]

    def add_cores(name, kept, sent):
        from_core = permute(name, sent, over_core)
        return (kept.astype(F32) + from_core.astype(F32)).astype(BF16)

    part_two = project_part(place, [two], out_weight, w_y)
    near = project_part(place, [after(gated, part_two), one], out_weight, w_y)
    far = project_part(place, [part_two, after(three, near)], out_weight, w_y, given=True)
    far_sum = add_cores("core_far", far[0], far[1])
    near = after(near, far_sum)
    near_sum = add_cores("core_near", near[0], near[1])
    parts = home(far_sum, 2) + home(near_sum, 0)
    kind = 1 - ((z ^ tp) >> 1)
    return pl.pallas_call(
        finish_kernel,
        out_shape=jax.ShapeDtypeStruct((tokens, 2 * out_weight.shape[0]), BF16),
        in_specs=[SMEM] + [VMEM] * len(parts),
        out_specs=VMEM,
        compiler_params=params(),
        cost_estimate=cost(4 * tokens * out_weight.shape[0], 2 << 20),
        name="finish",
    )(kind.reshape(1).astype(jnp.int32), *parts)


def per_device(features, short_taps, rates, residues, skip, out_weight):
    q, k, v = (features[:, group] for group in range(3))
    poles, taps = rates.shape[1], short_taps.shape[1]
    signal, message, table = signal_part(q, k, v, short_taps, rates, residues, skip)
    near, gate = near_part(q, signal, table, poles, taps)
    messages = lax.all_gather(message, "seq")
    place = lax.axis_index("seq")
    gated = far_part(enter_any, place, near, gate, table, [messages], poles, taps)
    partial = lax.dot_general(
        gated,
        lax.all_gather(out_weight, "seq", axis=0, tiled=True),
        (((1,), (1,)), ((), ())),
        preferred_element_type=F32,
    )
    return lax.psum_scatter(partial.astype(BF16), "tp", scatter_dimension=1, tiled=True)


def solution(mesh):
    in_specs = (
        P("seq", None, "tp"),
        P(None, None, "tp"),
        P("tp", None),
        P("tp", None),
        P("tp"),
        P("seq", "tp"),
    )
    out_specs = P("seq", "tp")
    body = per_device_32 if (mesh.shape["seq"], mesh.shape["tp"]) == (8, 4) else per_device
    return jax.shard_map(body, mesh=mesh, in_specs=in_specs, out_specs=out_specs, check_vma=False)
```

```python
import functools

import jax
import jax.numpy as jnp
from jax import lax
from jax.experimental import pallas as pl
from jax.experimental.pallas import tpu as pltpu
from jax.sharding import PartitionSpec as P

LANES = 128
SUBLANES = 16
F32 = jnp.float32
BF16 = jnp.bfloat16
VMEM = pl.BlockSpec(memory_space=pltpu.VMEM)
SMEM = pl.BlockSpec(memory_space=pltpu.SMEM)
AXES = ("seq", "tp")


def cost(flops, bytes_accessed):
    return pl.CostEstimate(flops=flops, bytes_accessed=bytes_accessed, transcendentals=0)


def params(**kw):
    return pltpu.CompilerParams(vmem_limit_bytes=16 * 1024 * 1024, **kw)


def signal_kernel(
    skip_ref, q_ref, k_ref, v_ref, taps_ref, rates_ref, residues_ref,
    signal_ref, message_ref, table_ref,
    message_s,
):
    tokens, channels = q_ref.shape
    poles, taps = rates_ref.shape[0], taps_ref.shape[1]
    fold = channels // LANES
    edge = taps - 1
    tap_row = 2 * poles
    skip_row = tap_row + 3 * taps
    table_ref[skip_row * fold : (skip_row + 1) * fold, :] = skip_ref[...]
    later = lax.broadcasted_iota(jnp.int32, (tokens, LANES), 0) >= edge
    for j in range(fold):
        lanes = slice(j * LANES, (j + 1) * LANES)
        table_ref[pl.ds(j, poles, stride=fold), :] = rates_ref[:, lanes]
        table_ref[pl.ds(poles * fold + j, poles, stride=fold), :] = residues_ref[:, lanes]
        mixed = []
        for group, ref in enumerate((q_ref, k_ref, v_ref)):
            total = None
            value = ref[:, lanes].astype(F32) if group else None
            for shift in range(taps):
                row = (tap_row + group * taps + shift) * fold + j
                tap = taps_ref[group, shift : shift + 1, lanes].astype(F32)
                table_ref[row : row + 1, :] = tap
                if group:
                    moved = value if shift == 0 else pltpu.roll(value, shift, axis=0)
                    total = tap * moved if total is None else total + tap * moved
            mixed.append(total)
            first, last = ref[:SUBLANES, lanes].astype(F32), ref[-SUBLANES:, lanes].astype(F32)
            for place in range(2 * edge):
                row = (poles + group * 2 * edge + place) * fold + j
                source = place if place < edge else SUBLANES - 2 * edge + place
                source_rows = first if place < edge else last
                message_s[row : row + 1, :] = source_rows[source : source + 1, :]
        signal = jnp.where(later, mixed[1] * mixed[2], 0.0)
        signal_ref[pl.ds(j, tokens, stride=fold), :] = signal
    decay = [jnp.exp(-table_ref[r * fold : (r + 1) * fold, :]) for r in range(poles)]

    def step(t, modes):
        value = signal_ref[pl.ds(pl.multiple_of(t * fold, fold), fold), :]
        return tuple(d * m + value for d, m in zip(decay, modes))

    modes = lax.fori_loop(0, tokens, step, (jnp.zeros((fold, LANES), F32),) * poles, unroll=8)
    for r in range(poles):
        residue = table_ref[(poles + r) * fold : (poles + r + 1) * fold, :]
        message_s[r * fold : (r + 1) * fold, :] = residue * modes[r]
    message_ref[...] = message_s[...].astype(BF16)


def near_kernel(poles, taps, q_ref, signal_ref, table_ref, out_ref, gate_ref, conv_s):
    tokens, channels = q_ref.shape
    fold = channels // LANES
    tap_row = 2 * poles
    skip_row = tap_row + 3 * taps
    decay = [jnp.exp(-table_ref[r * fold : (r + 1) * fold, :]) for r in range(poles)]
    residue = [table_ref[(poles + r) * fold : (poles + r + 1) * fold, :] for r in range(poles)]
    skip = table_ref[skip_row * fold : (skip_row + 1) * fold, :]

    def step(t, modes):
        rows = pl.ds(pl.multiple_of(t * fold, fold), fold)
        value = signal_ref[rows, :]
        modes = tuple(d * m + c * value for d, c, m in zip(decay, residue, modes))
        conv_s[rows, :] = tree_sum(modes + (skip * value,))
        return modes

    lax.fori_loop(0, tokens, step, (jnp.zeros((fold, LANES), F32),) * poles, unroll=4)
    for j in range(fold):
        lanes = slice(j * LANES, (j + 1) * LANES)
        value = q_ref[:, lanes].astype(F32)
        gate = None
        for shift in range(taps):
            row = (tap_row + shift) * fold + j
            moved = value if shift == 0 else pltpu.roll(value, shift, axis=0)
            term = table_ref[row : row + 1, :] * moved
            gate = term if gate is None else gate + term
        gate_ref[:, lanes] = gate
        conv = conv_s[pl.ds(j, tokens, stride=fold), :]
        out_ref[:, lanes] = (gate * conv).astype(BF16)


def tree_sum(values):
    values = list(values)
    while len(values) > 1:
        values = [a + b for a, b in zip(values[::2], values[1::2])] + (
            [values[-1]] if len(values) % 2 else []
        )
    return values[0]


def signal_part(q, k, v, short_taps, rates, residues, skip):
    tokens, channels = q.shape
    poles, taps = rates.shape[1], short_taps.shape[1]
    fold = channels // LANES
    message_rows = (poles + 6 * (taps - 1)) * fold
    table_rows = (2 * poles + 3 * taps + 1) * fold
    return pl.pallas_call(
        signal_kernel,
        out_shape=(
            jax.ShapeDtypeStruct((tokens * fold, LANES), F32),
            jax.ShapeDtypeStruct((message_rows, LANES), BF16),
            jax.ShapeDtypeStruct((table_rows, LANES), F32),
        ),
        in_specs=[VMEM] * 7,
        out_specs=(VMEM,) * 3,
        scratch_shapes=[pltpu.VMEM((message_rows, LANES), F32)],
        compiler_params=params(),
        cost_estimate=cost(2 * tokens * channels * poles, 2 << 20),
        name="signal",
    )(skip.reshape(fold, LANES), q, k, v, short_taps, rates.T, residues.T)


def near_part(q, signal, table, poles, taps):
    tokens, channels = q.shape
    return pl.pallas_call(
        functools.partial(near_kernel, poles, taps),
        out_shape=(
            jax.ShapeDtypeStruct((tokens, channels), BF16),
            jax.ShapeDtypeStruct((tokens, channels), F32),
        ),
        in_specs=[VMEM] * 3,
        out_specs=(VMEM,) * 2,
        scratch_shapes=[pltpu.VMEM(signal.shape, F32)],
        compiler_params=params(),
        cost_estimate=cost(4 * tokens * channels * poles, 2 << 20),
        name="near_filter",
    )(q, signal, table)


class Table:
    def __init__(self, ref, poles, taps, fold, tokens, weights=None):
        self.ref, self.poles, self.taps, self.fold, self.edge = ref, poles, taps, fold, taps - 1
        self.rates = ref[0 : poles * fold, :].reshape(poles, fold, LANES)
        self.residues = ref[poles * fold : 2 * poles * fold, :].reshape(poles, fold, LANES)
        self.tap_base = 2 * poles * fold
        skip_base = self.tap_base + 3 * taps * fold
        self.skip = ref[skip_base : skip_base + fold, :]
        self.tokens = tokens
        self.weights = weights

    def span(self, shards):
        if self.weights is not None:
            return self.weights[shards // 4, 0]
        return jnp.exp(-self.rates * float(shards * self.tokens))

    def tap(self, group, shift):
        row = self.tap_base + (group * self.taps + shift) * self.fold
        return self.ref[row : row + self.fold, :]

    def message(self, value):
        return value.astype(F32).reshape(-1, self.fold, LANES)

    def first(self, message, group):
        base = self.poles + group * 2 * self.edge
        return [message[base + i] for i in range(self.edge)]

    def last(self, message, group):
        base = self.poles + group * 2 * self.edge + self.edge
        return [message[base + i] for i in range(self.edge)]

    def mixed(self, before, current, group):
        rows = self.last(before, group) + self.first(current, group)
        return [
            sum(self.tap(group, shift) * rows[self.edge + i - shift] for shift in range(self.taps))
            for i in range(self.edge)
        ]

    def signals(self, before, current):
        pairs = zip(self.mixed(before, current, 1), self.mixed(before, current, 2))
        return [k * v for k, v in pairs]

    def lead(self, shards):
        if self.weights is not None:
            return [self.weights[shards // 4, 1 + i] for i in range(self.edge)]
        last = shards * self.tokens - 1
        return [jnp.exp(-self.rates * float(last - i)) * self.residues for i in range(self.edge)]

    def enter(self, state, span, lead, before, current):
        state = span * state + current[: self.poles]
        for weight, value in zip(lead, self.signals(before, current)):
            state = state + weight * value[None]
        return state


def enter_any(table, place_ref, messages_ref):
    span, lead = table.span(1), table.lead(1)

    def pick(index):
        current = table.message(messages_ref[index])
        before = table.message(messages_ref[jnp.maximum(index - 1, 0)])
        return jnp.where(index > 0, before, 0.0), current

    def one(index, state):
        return table.enter(state, span, lead, *pick(index))

    zero = jnp.zeros((table.poles, table.fold, LANES), F32)
    state = lax.fori_loop(0, place_ref[0], one, zero)
    return (state,) + pick(place_ref[0])


def in_order(place, values):
    out = []
    for p in range(4):
        value = values[p]
        for g in range(1, 4):
            value = jnp.where(place == g, values[p ^ g], value)
        out.append(value)
    return out


def enter_group(table, place_ref, *refs):
    messages = [table.message(ref[...]) for ref in refs[3::-1] + refs[4:]]
    place, group = place_ref[0], in_order(place_ref[0], messages[:4])
    before = jnp.zeros_like(messages[4])
    state = table.enter(before[: table.poles], table.span(4), table.lead(4), before, messages[4])
    before = messages[4]
    for p in range(3):
        behind = table.enter(state, table.span(1), table.lead(1), before, group[p])
        state = jnp.where(p < place, behind, state)
        before = jnp.where(p < place, group[p], before)
    return state, before, messages[0]


def join_kernel(poles, taps, tokens, place_ref, *refs):
    message_refs, (table_ref, out_ref) = refs[3::-1], refs[4:]
    fold = out_ref.shape[0] // (poles + 6 * (taps - 1))
    table = Table(table_ref, poles, taps, fold, tokens)
    group = in_order(place_ref[0], [table.message(ref[...]) for ref in message_refs])
    span, lead = table.span(1), table.lead(1)
    state = group[0][:poles]
    for before, current in zip(group[:-1], group[1:]):
        state = table.enter(state, span, lead, before, current)
    out = [state[r] for r in range(poles)]
    for kind in range(3):
        out += table.first(group[0], kind) + table.last(group[3], kind)
    out_ref[...] = jnp.concatenate(out, axis=0).astype(BF16)


def join_part(place, messages, table, tokens, poles, taps):
    return pl.pallas_call(
        functools.partial(join_kernel, poles, taps, tokens),
        out_shape=jax.ShapeDtypeStruct(messages[0].shape, BF16),
        in_specs=[SMEM] + [VMEM] * 5,
        out_specs=VMEM,
        compiler_params=params(),
        cost_estimate=cost(1 << 20, 1 << 18),
        name="join_state",
    )(place.reshape(1).astype(jnp.int32), *messages[::-1], table)


def weights_kernel(poles, taps, tokens, table_ref, out_ref):
    fold = out_ref.shape[3]
    table = Table(table_ref, poles, taps, fold, tokens)
    for i, shards in enumerate((1, 4)):
        for j, weight in enumerate([table.span(shards)] + table.lead(shards)):
            out_ref[i, j] = weight


def weights_part(table, tokens, poles, taps, fold):
    return pl.pallas_call(
        functools.partial(weights_kernel, poles, taps, tokens),
        out_shape=jax.ShapeDtypeStruct((2, taps, poles, fold, LANES), F32),
        in_specs=[VMEM],
        out_specs=VMEM,
        compiler_params=params(),
        cost_estimate=cost(1 << 20, 1 << 20),
        name="state_weights",
    )(table)


def far_kernel(poles, taps, count, enter, place_ref, near_ref, gate_ref, table_ref, *refs):
    message_refs, weights_refs, (out_ref, conv_s) = refs[:count], refs[count:-2], refs[-2:]
    tokens, channels = near_ref.shape
    fold = channels // LANES
    table = Table(table_ref, poles, taps, fold, tokens, *weights_refs)
    edge = table.edge
    state, before, current = enter(table, place_ref, *message_refs)
    decay = [jnp.exp(-table.rates[r]) for r in range(poles)]
    modes = tuple(state[r] for r in range(poles))
    for t, value in enumerate(table.signals(before, current)):
        modes = tuple(decay[r] * modes[r] + table.residues[r] * value for r in range(poles))
        conv_s[t * fold : (t + 1) * fold, :] = tree_sum(modes + (table.skip * value,))

    def step(t, modes):
        modes = tuple(d * m for d, m in zip(decay, modes))
        conv_s[pl.ds(pl.multiple_of(t * fold, fold), fold), :] = tree_sum(modes)
        return modes

    lax.fori_loop(edge, tokens, step, modes, unroll=6)
    row_id = lax.broadcasted_iota(jnp.int32, (tokens, LANES), 0)
    first = table.mixed(before, current, 0)
    for j in range(fold):
        lanes = slice(j * LANES, (j + 1) * LANES)
        gate = gate_ref[:, lanes]
        for t in range(edge):
            gate = jnp.where(row_id == t, first[t][j : j + 1, :], gate)
        conv = conv_s[pl.ds(j, tokens, stride=fold), :]
        out_ref[:, lanes] = (near_ref[:, lanes].astype(F32) + gate * conv).astype(BF16)


def far_part(enter, place, near, gate, table, messages, poles, taps, weights=()):
    tokens, channels = near.shape
    fold = channels // LANES
    count = len(messages)
    return pl.pallas_call(
        functools.partial(far_kernel, poles, taps, count, enter),
        out_shape=jax.ShapeDtypeStruct((tokens, channels), BF16),
        in_specs=[SMEM] + [VMEM] * (3 + count + len(weights)),
        out_specs=VMEM,
        scratch_shapes=[pltpu.VMEM((tokens * fold, LANES), F32)],
        compiler_params=params(),
        cost_estimate=cost(4 * tokens * channels * poles, 3 << 20),
        name="far_filter",
    )(place.reshape(1).astype(jnp.int32), near, gate, table, *messages, *weights)


def project(rows, weight_ref):
    stacked = jnp.concatenate([r[...] for r in rows], axis=0) if len(rows) > 1 else rows[0][...]
    product = lax.dot_general(
        stacked, weight_ref[...], (((1,), (1,)), ((), ())), preferred_element_type=F32
    ).astype(BF16)
    tokens = rows[0].shape[0]
    return [product[i * tokens : (i + 1) * tokens] for i in range(len(rows))]


def own_kernel(*refs):
    *rows_refs, weight_ref, out_ref = refs
    for i, product in enumerate(project(rows_refs, weight_ref)):
        out_ref[i] = product


def other_kernel(
    place_ref, zero_ref, one_ref, two_ref, near_own_ref, two_own_ref, weight_ref, near_ref, out_ref
):
    y, odd = place_ref[0], place_ref[1]
    zero, one, two = project([zero_ref, one_ref, two_ref], weight_ref)
    for i, product in enumerate((zero, one)):
        near_ref[odd ^ i, y] = near_own_ref[i]
        near_ref[odd ^ i, 1 - y] = product
    out_ref[y] = two_own_ref[0]
    out_ref[1 - y] = two


def far_project_kernel(place_ref, two_ref, three_ref, own_ref, other_ref, out_ref):
    y, odd = place_ref[0], place_ref[1]
    out_ref[odd] = two_ref[...]
    for half, ref in ((y, own_ref), (1 - y, other_ref)):
        out_ref[1 - odd, half] = project([three_ref], ref)[0]


def project_part(kernel, name, operands, shapes, flops):
    out_shape = tuple(jax.ShapeDtypeStruct(shape, BF16) for shape in shapes)
    return pl.pallas_call(
        kernel,
        out_shape=out_shape,
        in_specs=[SMEM if x.dtype == jnp.int32 else VMEM for x in operands],
        out_specs=(VMEM,) * len(shapes),
        compiler_params=params(),
        cost_estimate=cost(flops, 3 << 20),
        name=name,
    )(*operands)


def finish_kernel(place_ref, *refs):
    out_ref = refs[-1]
    width = refs[0].shape[2]
    for pair in range((len(refs) - 1) // 2):

        @pl.when(place_ref[0] == pair)
        def _(pair=pair):
            for h in range(2):
                total = refs[2 * pair][h].astype(F32) + refs[2 * pair + 1][h].astype(F32)
                out_ref[:, h * width : (h + 1) * width] = total.astype(BF16)


def permute(name, x, move, keep=None):
    pairs = []
    for index in range(32):
        place = (index // 8, index // 4 % 2, index // 2 % 2, index % 2)
        if keep is None or keep(*place):
            z, y, x_, c = move(*place)
            pairs.append((index, ((z * 2 + y) * 2 + x_) * 2 + c))
    with jax.named_scope(name):
        return lax.ppermute(x, AXES, pairs)


def over_y(z, y, x, c):
    return z, 1 - y, x, c


def over_z0(z, y, x, c):
    return z ^ 1, y, x, c


def over_z1(z, y, x, c):
    return z ^ 2, y, x, c


def over_core(z, y, x, c):
    return z, y, x, 1 - c


def after(x, *others):
    return lax.optimization_barrier((x,) + others)[0]


def per_device_32(features, short_taps, rates, residues, skip, out_weight):
    tokens, _, channels = features.shape
    q, k, v = (features[:, group] for group in range(3))
    poles, taps = rates.shape[1], short_taps.shape[1]
    seq, tp = lax.axis_index("seq"), lax.axis_index("tp")
    z, y = seq >> 1, seq & 1
    signal, message, table = signal_part(q, k, v, short_taps, rates, residues, skip)
    near, gate = near_part(q, signal, table, poles, taps)
    messages = [
        message,
        permute("state_y", message, over_y),
        permute("state_z", message, over_z0),
        permute("state_zy", message, lambda z, y, x, c: (z ^ 1, 1 - y, x, c)),
    ]
    place = seq & 3
    joined = join_part(place, messages, table, tokens, poles, taps)
    weights = weights_part(after(table, joined), tokens, poles, taps, channels // LANES)
    w_y = permute("weights", after(out_weight, weights), over_y)
    joined = permute("state_half", joined, over_z1, lambda z, y, x, c: z < 2)
    gated = far_part(
        enter_group, place, near, gate, table, messages[::-1] + [joined], poles, taps, [weights]
    )
    two = permute("gated_two", gated, over_z1)
    one = permute("gated_one", gated, over_z0)
    three = permute("gated_three", two, over_z0)
    odd = (z ^ tp) & 1
    place = jnp.stack([y, odd]).astype(jnp.int32)

    def odd_of(z, y, x, c):
        return (z ^ c) % 2

    def home(summed, far):
        def move(z, y, x, c):
            return z ^ far ^ odd_of(z, y, x, c), y, z // 2, z % 2

        return [
            permute(f"straight_{far}", summed, move, lambda z, y, x, c: x == z // 2),
            permute(f"across_{far}", summed, move, lambda z, y, x, c: x != z // 2),
        ]

    def add_cores(name, kept, sent):
        from_core = permute(name, sent, over_core)
        return (kept.astype(F32) + from_core.astype(F32)).astype(BF16)

    width = out_weight.shape[0]
    whole, flops = (2, tokens, width), 2 * tokens * channels * width
    (two_own,) = project_part(own_kernel, "project_two", [two, out_weight], [(1, tokens, width)], flops)
    (near_own,) = project_part(
        own_kernel, "project_near", [gated, one, out_weight], [whole], 2 * flops
    )
    near, part_two = project_part(
        other_kernel,
        "project_other",
        [place, gated, one, two, near_own, two_own, w_y],
        [(2,) + whole, whole],
        3 * flops,
    )
    (far,) = project_part(
        far_project_kernel,
        "project_far",
        [place, part_two, three, out_weight, w_y],
        [(2,) + whole],
        2 * flops,
    )
    far_sum = add_cores("core_far", far[0], far[1])
    near = after(near, far_sum)
    near_sum = add_cores("core_near", near[0], near[1])
    parts = home(near_sum, 0) + home(far_sum, 2)
    kind = (z ^ tp) >> 1
    return pl.pallas_call(
        finish_kernel,
        out_shape=jax.ShapeDtypeStruct((tokens, 2 * out_weight.shape[0]), BF16),
        in_specs=[SMEM] + [VMEM] * len(parts),
        out_specs=VMEM,
        compiler_params=params(),
        cost_estimate=cost(4 * tokens * out_weight.shape[0], 2 << 20),
        name="finish",
    )(kind.reshape(1).astype(jnp.int32), *parts)


def per_device(features, short_taps, rates, residues, skip, out_weight):
    q, k, v = (features[:, group] for group in range(3))
    poles, taps = rates.shape[1], short_taps.shape[1]
    signal, message, table = signal_part(q, k, v, short_taps, rates, residues, skip)
    near, gate = near_part(q, signal, table, poles, taps)
    messages = lax.all_gather(message, "seq")
    place = lax.axis_index("seq")
    gated = far_part(enter_any, place, near, gate, table, [messages], poles, taps)
    partial = lax.dot_general(
        gated,
        lax.all_gather(out_weight, "seq", axis=0, tiled=True),
        (((1,), (1,)), ((), ())),
        preferred_element_type=F32,
    )
    return lax.psum_scatter(partial.astype(BF16), "tp", scatter_dimension=1, tiled=True)


def solution(mesh):
    in_specs = (
        P("seq", None, "tp"),
        P(None, None, "tp"),
        P("tp", None),
        P("tp", None),
        P("tp"),
        P("seq", "tp"),
    )
    out_specs = P("seq", "tp")
    body = per_device_32 if (mesh.shape["seq"], mesh.shape["tp"]) == (8, 4) else per_device
    return jax.shard_map(body, mesh=mesh, in_specs=in_specs, out_specs=out_specs, check_vma=False)
```

```python
import functools

import jax
import jax.numpy as jnp
from jax import lax
from jax.experimental import pallas as pl
from jax.experimental.pallas import tpu as pltpu
from jax.sharding import PartitionSpec as P

LANES = 128
SUBLANES = 16
F32 = jnp.float32
BF16 = jnp.bfloat16
VMEM = pl.BlockSpec(memory_space=pltpu.VMEM)
SMEM = pl.BlockSpec(memory_space=pltpu.SMEM)
AXES = ("seq", "tp")


def cost(flops, bytes_accessed):
    return pl.CostEstimate(flops=flops, bytes_accessed=bytes_accessed, transcendentals=0)


def params(**kw):
    return pltpu.CompilerParams(vmem_limit_bytes=16 * 1024 * 1024, **kw)


def signal_kernel(
    skip_ref, q_ref, k_ref, v_ref, taps_ref, rates_ref, residues_ref,
    signal_ref, message_ref, table_ref,
    message_s,
):
    tokens, channels = q_ref.shape
    poles, taps = rates_ref.shape[0], taps_ref.shape[1]
    fold = channels // LANES
    edge = taps - 1
    tap_row = 2 * poles
    skip_row = tap_row + 3 * taps
    table_ref[skip_row * fold : (skip_row + 1) * fold, :] = skip_ref[...]
    later = lax.broadcasted_iota(jnp.int32, (tokens, LANES), 0) >= edge
    for j in range(fold):
        lanes = slice(j * LANES, (j + 1) * LANES)
        table_ref[pl.ds(j, poles, stride=fold), :] = rates_ref[:, lanes]
        table_ref[pl.ds(poles * fold + j, poles, stride=fold), :] = residues_ref[:, lanes]
        mixed = []
        for group, ref in enumerate((q_ref, k_ref, v_ref)):
            total = None
            value = ref[:, lanes].astype(F32) if group else None
            for shift in range(taps):
                row = (tap_row + group * taps + shift) * fold + j
                tap = taps_ref[group, shift : shift + 1, lanes].astype(F32)
                table_ref[row : row + 1, :] = tap
                if group:
                    moved = value if shift == 0 else pltpu.roll(value, shift, axis=0)
                    total = tap * moved if total is None else total + tap * moved
            mixed.append(total)
            first, last = ref[:SUBLANES, lanes].astype(F32), ref[-SUBLANES:, lanes].astype(F32)
            for place in range(2 * edge):
                row = (poles + group * 2 * edge + place) * fold + j
                source = place if place < edge else SUBLANES - 2 * edge + place
                source_rows = first if place < edge else last
                message_s[row : row + 1, :] = source_rows[source : source + 1, :]
        signal = jnp.where(later, mixed[1] * mixed[2], 0.0)
        signal_ref[pl.ds(j, tokens, stride=fold), :] = signal
    decay = [jnp.exp(-table_ref[r * fold : (r + 1) * fold, :]) for r in range(poles)]

    def step(t, modes):
        value = signal_ref[pl.ds(pl.multiple_of(t * fold, fold), fold), :]
        return tuple(d * m + value for d, m in zip(decay, modes))

    modes = lax.fori_loop(0, tokens, step, (jnp.zeros((fold, LANES), F32),) * poles, unroll=8)
    for r in range(poles):
        residue = table_ref[(poles + r) * fold : (poles + r + 1) * fold, :]
        message_s[r * fold : (r + 1) * fold, :] = residue * modes[r]
    message_ref[...] = message_s[...].astype(BF16)


def near_kernel(poles, taps, q_ref, signal_ref, table_ref, out_ref, gate_ref, conv_s):
    tokens, channels = q_ref.shape
    fold = channels // LANES
    tap_row = 2 * poles
    skip_row = tap_row + 3 * taps
    decay = [jnp.exp(-table_ref[r * fold : (r + 1) * fold, :]) for r in range(poles)]
    residue = [table_ref[(poles + r) * fold : (poles + r + 1) * fold, :] for r in range(poles)]
    skip = table_ref[skip_row * fold : (skip_row + 1) * fold, :]

    def step(t, modes):
        rows = pl.ds(pl.multiple_of(t * fold, fold), fold)
        value = signal_ref[rows, :]
        modes = tuple(d * m + c * value for d, c, m in zip(decay, residue, modes))
        conv_s[rows, :] = tree_sum(modes + (skip * value,))
        return modes

    lax.fori_loop(0, tokens, step, (jnp.zeros((fold, LANES), F32),) * poles, unroll=4)
    for j in range(fold):
        lanes = slice(j * LANES, (j + 1) * LANES)
        value = q_ref[:, lanes].astype(F32)
        gate = None
        for shift in range(taps):
            row = (tap_row + shift) * fold + j
            moved = value if shift == 0 else pltpu.roll(value, shift, axis=0)
            term = table_ref[row : row + 1, :] * moved
            gate = term if gate is None else gate + term
        gate_ref[:, lanes] = gate
        conv = conv_s[pl.ds(j, tokens, stride=fold), :]
        out_ref[:, lanes] = (gate * conv).astype(BF16)


def folded_shape(tokens, fold):
    return ((tokens + 1) * fold, LANES)


def tree_sum(values):
    values = list(values)
    while len(values) > 1:
        values = [a + b for a, b in zip(values[::2], values[1::2])] + (
            [values[-1]] if len(values) % 2 else []
        )
    return values[0]


def signal_part(q, k, v, short_taps, rates, residues, skip):
    tokens, channels = q.shape
    poles, taps = rates.shape[1], short_taps.shape[1]
    fold = channels // LANES
    message_rows = (poles + 6 * (taps - 1)) * fold
    table_rows = (2 * poles + 3 * taps + 1) * fold
    return pl.pallas_call(
        signal_kernel,
        out_shape=(
            jax.ShapeDtypeStruct(folded_shape(tokens, fold), F32),
            jax.ShapeDtypeStruct((message_rows, LANES), BF16),
            jax.ShapeDtypeStruct((table_rows, LANES), F32),
        ),
        in_specs=[VMEM] * 7,
        out_specs=(VMEM,) * 3,
        scratch_shapes=[pltpu.VMEM((message_rows, LANES), F32)],
        compiler_params=params(),
        cost_estimate=cost(2 * tokens * channels * poles, 2 << 20),
        name="signal",
    )(skip.reshape(fold, LANES), q, k, v, short_taps, rates.T, residues.T)


def near_part(q, signal, table, poles, taps):
    tokens, channels = q.shape
    return pl.pallas_call(
        functools.partial(near_kernel, poles, taps),
        out_shape=(
            jax.ShapeDtypeStruct((tokens, channels), BF16),
            jax.ShapeDtypeStruct((tokens, channels), F32),
        ),
        in_specs=[VMEM] * 3,
        out_specs=(VMEM,) * 2,
        scratch_shapes=[pltpu.VMEM(signal.shape, F32)],
        compiler_params=params(),
        cost_estimate=cost(4 * tokens * channels * poles, 2 << 20),
        name="near_filter",
    )(q, signal, table)


class Table:
    def __init__(self, ref, poles, taps, fold, tokens, weights=None):
        self.ref, self.poles, self.taps, self.fold, self.edge = ref, poles, taps, fold, taps - 1
        self.rates = ref[0 : poles * fold, :].reshape(poles, fold, LANES)
        self.residues = ref[poles * fold : 2 * poles * fold, :].reshape(poles, fold, LANES)
        self.tap_base = 2 * poles * fold
        skip_base = self.tap_base + 3 * taps * fold
        self.skip = ref[skip_base : skip_base + fold, :]
        self.tokens = tokens
        self.weights = weights

    def span(self, shards):
        if self.weights is not None:
            return self.weights[shards // 4, 0]
        return jnp.exp(-self.rates * float(shards * self.tokens))

    def tap(self, group, shift):
        row = self.tap_base + (group * self.taps + shift) * self.fold
        return self.ref[row : row + self.fold, :]

    def message(self, value):
        return value.astype(F32).reshape(-1, self.fold, LANES)

    def first(self, message, group):
        base = self.poles + group * 2 * self.edge
        return [message[base + i] for i in range(self.edge)]

    def last(self, message, group):
        base = self.poles + group * 2 * self.edge + self.edge
        return [message[base + i] for i in range(self.edge)]

    def mixed(self, before, current, group):
        rows = self.last(before, group) + self.first(current, group)
        return [
            sum(self.tap(group, shift) * rows[self.edge + i - shift] for shift in range(self.taps))
            for i in range(self.edge)
        ]

    def signals(self, before, current):
        pairs = zip(self.mixed(before, current, 1), self.mixed(before, current, 2))
        return [k * v for k, v in pairs]

    def lead(self, shards):
        if self.weights is not None:
            return [self.weights[shards // 4, 1 + i] for i in range(self.edge)]
        last = shards * self.tokens - 1
        return [jnp.exp(-self.rates * float(last - i)) * self.residues for i in range(self.edge)]

    def enter(self, state, span, lead, before, current):
        state = span * state + current[: self.poles]
        for weight, value in zip(lead, self.signals(before, current)):
            state = state + weight * value[None]
        return state


def enter_any(table, place_ref, messages_ref):
    span, lead = table.span(1), table.lead(1)

    def pick(index):
        current = table.message(messages_ref[index])
        before = table.message(messages_ref[jnp.maximum(index - 1, 0)])
        return jnp.where(index > 0, before, 0.0), current

    def one(index, state):
        return table.enter(state, span, lead, *pick(index))

    zero = jnp.zeros((table.poles, table.fold, LANES), F32)
    state = lax.fori_loop(0, place_ref[0], one, zero)
    return (state,) + pick(place_ref[0])


def in_order(place, values):
    out = []
    for p in range(4):
        value = values[p]
        for g in range(1, 4):
            value = jnp.where(place == g, values[p ^ g], value)
        out.append(value)
    return out


def enter_group(table, place_ref, *refs):
    messages = [table.message(ref[...]) for ref in refs[3::-1] + refs[4:]]
    place, group = place_ref[0], in_order(place_ref[0], messages[:4])
    before = jnp.zeros_like(messages[4])
    state = table.enter(before[: table.poles], table.span(4), table.lead(4), before, messages[4])
    before = messages[4]
    for p in range(3):
        behind = table.enter(state, table.span(1), table.lead(1), before, group[p])
        state = jnp.where(p < place, behind, state)
        before = jnp.where(p < place, group[p], before)
    return state, before, messages[0]


def join_kernel(poles, taps, tokens, place_ref, *refs):
    message_refs, (table_ref, out_ref) = refs[3::-1], refs[4:]
    fold = out_ref.shape[0] // (poles + 6 * (taps - 1))
    table = Table(table_ref, poles, taps, fold, tokens)
    group = in_order(place_ref[0], [table.message(ref[...]) for ref in message_refs])
    span, lead = table.span(1), table.lead(1)
    state = group[0][:poles]
    for before, current in zip(group[:-1], group[1:]):
        state = table.enter(state, span, lead, before, current)
    out = [state[r] for r in range(poles)]
    for kind in range(3):
        out += table.first(group[0], kind) + table.last(group[3], kind)
    out_ref[...] = jnp.concatenate(out, axis=0).astype(BF16)


def join_part(place, messages, table, tokens, poles, taps):
    return pl.pallas_call(
        functools.partial(join_kernel, poles, taps, tokens),
        out_shape=jax.ShapeDtypeStruct(messages[0].shape, BF16),
        in_specs=[SMEM] + [VMEM] * 5,
        out_specs=VMEM,
        compiler_params=params(),
        cost_estimate=cost(1 << 20, 1 << 18),
        name="join_state",
    )(place.reshape(1).astype(jnp.int32), *messages[::-1], table)


def weights_kernel(poles, taps, tokens, table_ref, out_ref):
    fold = out_ref.shape[3]
    table = Table(table_ref, poles, taps, fold, tokens)
    for i, shards in enumerate((1, 4)):
        for j, weight in enumerate([table.span(shards)] + table.lead(shards)):
            out_ref[i, j] = weight


def weights_part(table, tokens, poles, taps, fold):
    return pl.pallas_call(
        functools.partial(weights_kernel, poles, taps, tokens),
        out_shape=jax.ShapeDtypeStruct((2, taps, poles, fold, LANES), F32),
        in_specs=[VMEM],
        out_specs=VMEM,
        compiler_params=params(),
        cost_estimate=cost(1 << 20, 1 << 20),
        name="state_weights",
    )(table)


def far_kernel(poles, taps, count, enter, place_ref, near_ref, gate_ref, table_ref, *refs):
    message_refs, weights_refs, (out_ref, conv_s) = refs[:count], refs[count:-2], refs[-2:]
    tokens, channels = near_ref.shape
    fold = channels // LANES
    table = Table(table_ref, poles, taps, fold, tokens, *weights_refs)
    edge = table.edge
    state, before, current = enter(table, place_ref, *message_refs)
    decay = [jnp.exp(-table.rates[r]) for r in range(poles)]
    modes = tuple(state[r] for r in range(poles))
    for t, value in enumerate(table.signals(before, current)):
        modes = tuple(decay[r] * modes[r] + table.residues[r] * value for r in range(poles))
        conv_s[t * fold : (t + 1) * fold, :] = tree_sum(modes + (table.skip * value,))

    def step(t, modes):
        modes = tuple(d * m for d, m in zip(decay, modes))
        conv_s[pl.ds(pl.multiple_of(t * fold, fold), fold), :] = tree_sum(modes)
        return modes

    lax.fori_loop(edge, tokens, step, modes, unroll=6)
    row_id = lax.broadcasted_iota(jnp.int32, (tokens, LANES), 0)
    first = table.mixed(before, current, 0)
    for j in range(fold):
        lanes = slice(j * LANES, (j + 1) * LANES)
        gate = gate_ref[:, lanes]
        for t in range(edge):
            gate = jnp.where(row_id == t, first[t][j : j + 1, :], gate)
        conv = conv_s[pl.ds(j, tokens, stride=fold), :]
        out_ref[:, lanes] = (near_ref[:, lanes].astype(F32) + gate * conv).astype(BF16)


def far_part(enter, place, near, gate, table, messages, poles, taps, weights=()):
    tokens, channels = near.shape
    fold = channels // LANES
    count = len(messages)
    return pl.pallas_call(
        functools.partial(far_kernel, poles, taps, count, enter),
        out_shape=jax.ShapeDtypeStruct((tokens, channels), BF16),
        in_specs=[SMEM] + [VMEM] * (3 + count + len(weights)),
        out_specs=VMEM,
        scratch_shapes=[pltpu.VMEM(folded_shape(tokens, fold), F32)],
        compiler_params=params(),
        cost_estimate=cost(4 * tokens * channels * poles, 3 << 20),
        name="far_filter",
    )(place.reshape(1).astype(jnp.int32), near, gate, table, *messages, *weights)


def project(rows, weight_ref):
    stacked = jnp.concatenate([r[...] for r in rows], axis=0) if len(rows) > 1 else rows[0][...]
    product = lax.dot_general(
        stacked, weight_ref[...], (((1,), (1,)), ((), ())), preferred_element_type=F32
    ).astype(BF16)
    tokens = rows[0].shape[0]
    return [product[i * tokens : (i + 1) * tokens] for i in range(len(rows))]


def own_kernel(*refs):
    *rows_refs, weight_ref, out_ref = refs
    for i, product in enumerate(project(rows_refs, weight_ref)):
        out_ref[i] = product


def other_kernel(
    place_ref, zero_ref, one_ref, two_ref, near_own_ref, two_own_ref, weight_ref, near_ref, out_ref
):
    y, odd = place_ref[0], place_ref[1]
    zero, one, two = project([zero_ref, one_ref, two_ref], weight_ref)
    for i, product in enumerate((zero, one)):
        near_ref[odd ^ i, y] = near_own_ref[i]
        near_ref[odd ^ i, 1 - y] = product
    out_ref[y] = two_own_ref[0]
    out_ref[1 - y] = two


def far_project_kernel(place_ref, two_ref, three_ref, own_ref, other_ref, out_ref):
    y, odd = place_ref[0], place_ref[1]
    out_ref[odd] = two_ref[...]
    for half, ref in ((y, own_ref), (1 - y, other_ref)):
        out_ref[1 - odd, half] = project([three_ref], ref)[0]


def project_part(kernel, name, operands, shapes, flops):
    out_shape = tuple(jax.ShapeDtypeStruct(shape, BF16) for shape in shapes)
    return pl.pallas_call(
        kernel,
        out_shape=out_shape,
        in_specs=[SMEM if x.dtype == jnp.int32 else VMEM for x in operands],
        out_specs=(VMEM,) * len(shapes),
        compiler_params=params(),
        cost_estimate=cost(flops, 3 << 20),
        name=name,
    )(*operands)


def finish_kernel(place_ref, *refs):
    out_ref = refs[-1]
    width = refs[0].shape[2]
    for pair in range((len(refs) - 1) // 2):

        @pl.when(place_ref[0] == pair)
        def _(pair=pair):
            for h in range(2):
                total = refs[2 * pair][h].astype(F32) + refs[2 * pair + 1][h].astype(F32)
                out_ref[:, h * width : (h + 1) * width] = total.astype(BF16)


def permute(name, x, move, keep=None):
    pairs = []
    for index in range(32):
        place = (index // 8, index // 4 % 2, index // 2 % 2, index % 2)
        if keep is None or keep(*place):
            z, y, x_, c = move(*place)
            pairs.append((index, ((z * 2 + y) * 2 + x_) * 2 + c))
    with jax.named_scope(name):
        return lax.ppermute(x, AXES, pairs)


def over_y(z, y, x, c):
    return z, 1 - y, x, c


def over_z0(z, y, x, c):
    return z ^ 1, y, x, c


def over_z1(z, y, x, c):
    return z ^ 2, y, x, c


def over_core(z, y, x, c):
    return z, y, x, 1 - c


def after(x, *others):
    return lax.optimization_barrier((x,) + others)[0]


def per_device_32(features, short_taps, rates, residues, skip, out_weight):
    tokens, _, channels = features.shape
    q, k, v = (features[:, group] for group in range(3))
    poles, taps = rates.shape[1], short_taps.shape[1]
    seq, tp = lax.axis_index("seq"), lax.axis_index("tp")
    z, y = seq >> 1, seq & 1
    signal, message, table = signal_part(q, k, v, short_taps, rates, residues, skip)
    near, gate = near_part(q, signal, table, poles, taps)
    messages = [
        message,
        permute("state_y", message, over_y),
        permute("state_z", message, over_z0),
        permute("state_zy", message, lambda z, y, x, c: (z ^ 1, 1 - y, x, c)),
    ]
    place = seq & 3
    joined = join_part(place, messages, table, tokens, poles, taps)
    weights = weights_part(after(table, joined), tokens, poles, taps, channels // LANES)
    w_y = permute("weights", after(out_weight, weights), over_y)
    joined = permute("state_half", joined, over_z1, lambda z, y, x, c: z < 2)
    gated = far_part(
        enter_group, place, near, gate, table, messages[::-1] + [joined], poles, taps, [weights]
    )
    two = permute("gated_two", gated, over_z1)
    one = permute("gated_one", gated, over_z0)
    three = permute("gated_three", two, over_z0)
    odd = (z ^ tp) & 1
    place = jnp.stack([y, odd]).astype(jnp.int32)

    def odd_of(z, y, x, c):
        return (z ^ c) % 2

    def home(summed, far):
        def move(z, y, x, c):
            return z ^ far ^ odd_of(z, y, x, c), y, z // 2, z % 2

        return [
            permute(f"straight_{far}", summed, move, lambda z, y, x, c: x == z // 2),
            permute(f"across_{far}", summed, move, lambda z, y, x, c: x != z // 2),
        ]

    def add_cores(name, kept, sent):
        from_core = permute(name, sent, over_core)
        return (kept.astype(F32) + from_core.astype(F32)).astype(BF16)

    width = out_weight.shape[0]
    whole, flops = (2, tokens, width), 2 * tokens * channels * width
    (two_own,) = project_part(own_kernel, "project_two", [two, out_weight], [(1, tokens, width)], flops)
    (near_own,) = project_part(
        own_kernel, "project_near", [gated, one, out_weight], [whole], 2 * flops
    )
    near, part_two = project_part(
        other_kernel,
        "project_other",
        [place, gated, one, two, near_own, two_own, w_y],
        [(2,) + whole, whole],
        3 * flops,
    )
    (far,) = project_part(
        far_project_kernel,
        "project_far",
        [place, part_two, three, out_weight, w_y],
        [(2,) + whole],
        2 * flops,
    )
    far_sum = add_cores("core_far", far[0], far[1])
    near = after(near, far_sum)
    near_sum = add_cores("core_near", near[0], near[1])
    parts = home(near_sum, 0) + home(far_sum, 2)
    kind = (z ^ tp) >> 1
    return pl.pallas_call(
        finish_kernel,
        out_shape=jax.ShapeDtypeStruct((tokens, 2 * out_weight.shape[0]), BF16),
        in_specs=[SMEM] + [VMEM] * len(parts),
        out_specs=VMEM,
        compiler_params=params(),
        cost_estimate=cost(4 * tokens * out_weight.shape[0], 2 << 20),
        name="finish",
    )(kind.reshape(1).astype(jnp.int32), *parts)


def per_device(features, short_taps, rates, residues, skip, out_weight):
    q, k, v = (features[:, group] for group in range(3))
    poles, taps = rates.shape[1], short_taps.shape[1]
    signal, message, table = signal_part(q, k, v, short_taps, rates, residues, skip)
    near, gate = near_part(q, signal, table, poles, taps)
    messages = lax.all_gather(message, "seq")
    place = lax.axis_index("seq")
    gated = far_part(enter_any, place, near, gate, table, [messages], poles, taps)
    partial = lax.dot_general(
        gated,
        lax.all_gather(out_weight, "seq", axis=0, tiled=True),
        (((1,), (1,)), ((), ())),
        preferred_element_type=F32,
    )
    return lax.psum_scatter(partial.astype(BF16), "tp", scatter_dimension=1, tiled=True)


def solution(mesh):
    in_specs = (
        P("seq", None, "tp"),
        P(None, None, "tp"),
        P("tp", None),
        P("tp", None),
        P("tp"),
        P("seq", "tp"),
    )
    out_specs = P("seq", "tp")
    body = per_device_32 if (mesh.shape["seq"], mesh.shape["tp"]) == (8, 4) else per_device
    return jax.shard_map(body, mesh=mesh, in_specs=in_specs, out_specs=out_specs, check_vma=False)
```

```python
import functools

import jax
import jax.numpy as jnp
from jax import lax
from jax.experimental import pallas as pl
from jax.experimental.pallas import tpu as pltpu
from jax.sharding import PartitionSpec as P

LANES = 128
SUBLANES = 16
F32 = jnp.float32
BF16 = jnp.bfloat16
VMEM = pl.BlockSpec(memory_space=pltpu.VMEM)
SMEM = pl.BlockSpec(memory_space=pltpu.SMEM)
AXES = ("seq", "tp")


def cost(flops, bytes_accessed):
    return pl.CostEstimate(flops=flops, bytes_accessed=bytes_accessed, transcendentals=0)


def params(**kw):
    return pltpu.CompilerParams(vmem_limit_bytes=16 * 1024 * 1024, **kw)


def signal_kernel(
    skip_ref, q_ref, k_ref, v_ref, taps_ref, rates_ref, residues_ref,
    signal_ref, message_ref, table_ref,
    message_s,
):
    tokens, channels = q_ref.shape
    poles, taps = rates_ref.shape[0], taps_ref.shape[1]
    fold = channels // LANES
    edge = taps - 1
    tap_row = 2 * poles
    skip_row = tap_row + 3 * taps
    table_ref[skip_row * fold : (skip_row + 1) * fold, :] = skip_ref[...]
    later = lax.broadcasted_iota(jnp.int32, (tokens, LANES), 0) >= edge
    for j in range(fold):
        lanes = slice(j * LANES, (j + 1) * LANES)
        table_ref[pl.ds(j, poles, stride=fold), :] = rates_ref[:, lanes]
        table_ref[pl.ds(poles * fold + j, poles, stride=fold), :] = residues_ref[:, lanes]
        mixed = []
        for group, ref in enumerate((q_ref, k_ref, v_ref)):
            total = None
            value = ref[:, lanes].astype(F32) if group else None
            for shift in range(taps):
                row = (tap_row + group * taps + shift) * fold + j
                tap = taps_ref[group, shift : shift + 1, lanes].astype(F32)
                table_ref[row : row + 1, :] = tap
                if group:
                    moved = value if shift == 0 else pltpu.roll(value, shift, axis=0)
                    total = tap * moved if total is None else total + tap * moved
            mixed.append(total)
            first, last = ref[:SUBLANES, lanes].astype(F32), ref[-SUBLANES:, lanes].astype(F32)
            for place in range(2 * edge):
                row = (poles + group * 2 * edge + place) * fold + j
                source = place if place < edge else SUBLANES - 2 * edge + place
                source_rows = first if place < edge else last
                message_s[row : row + 1, :] = source_rows[source : source + 1, :]
        signal = jnp.where(later, mixed[1] * mixed[2], 0.0)
        signal_ref[pl.ds(j, tokens, stride=fold), :] = signal
    decay = [jnp.exp(-table_ref[r * fold : (r + 1) * fold, :]) for r in range(poles)]

    def step(t, modes):
        value = signal_ref[pl.ds(pl.multiple_of(t * fold, fold), fold), :]
        return tuple(d * m + value for d, m in zip(decay, modes))

    modes = lax.fori_loop(0, tokens, step, (jnp.zeros((fold, LANES), F32),) * poles, unroll=8)
    for r in range(poles):
        residue = table_ref[(poles + r) * fold : (poles + r + 1) * fold, :]
        message_s[r * fold : (r + 1) * fold, :] = residue * modes[r]
    message_ref[...] = message_s[...].astype(BF16)


def near_kernel(poles, taps, q_ref, signal_ref, table_ref, out_ref, gate_ref, conv_s):
    tokens, channels = q_ref.shape
    fold = channels // LANES
    tap_row = 2 * poles
    skip_row = tap_row + 3 * taps
    decay = [jnp.exp(-table_ref[r * fold : (r + 1) * fold, :]) for r in range(poles)]
    residue = [table_ref[(poles + r) * fold : (poles + r + 1) * fold, :] for r in range(poles)]
    skip = table_ref[skip_row * fold : (skip_row + 1) * fold, :]

    def step(t, modes):
        rows = pl.ds(pl.multiple_of(t * fold, fold), fold)
        value = signal_ref[rows, :]
        modes = tuple(d * m + c * value for d, c, m in zip(decay, residue, modes))
        conv_s[rows, :] = tree_sum(modes + (skip * value,))
        return modes

    lax.fori_loop(0, tokens, step, (jnp.zeros((fold, LANES), F32),) * poles, unroll=4)
    for j in range(fold):
        lanes = slice(j * LANES, (j + 1) * LANES)
        value = q_ref[:, lanes].astype(F32)
        gate = None
        for shift in range(taps):
            row = (tap_row + shift) * fold + j
            moved = value if shift == 0 else pltpu.roll(value, shift, axis=0)
            term = table_ref[row : row + 1, :] * moved
            gate = term if gate is None else gate + term
        gate_ref[:, lanes] = gate
        conv = conv_s[pl.ds(j, tokens, stride=fold), :]
        out_ref[:, lanes] = (gate * conv).astype(BF16)


def folded_shape(tokens, fold):
    return ((tokens + 1) * fold, LANES)


def tree_sum(values):
    values = list(values)
    while len(values) > 1:
        values = [a + b for a, b in zip(values[::2], values[1::2])] + (
            [values[-1]] if len(values) % 2 else []
        )
    return values[0]


def signal_part(q, k, v, short_taps, rates, residues, skip):
    tokens, channels = q.shape
    poles, taps = rates.shape[1], short_taps.shape[1]
    fold = channels // LANES
    message_rows = (poles + 6 * (taps - 1)) * fold
    table_rows = (2 * poles + 3 * taps + 1) * fold
    return pl.pallas_call(
        signal_kernel,
        out_shape=(
            jax.ShapeDtypeStruct(folded_shape(tokens, fold), F32),
            jax.ShapeDtypeStruct((message_rows, LANES), BF16),
            jax.ShapeDtypeStruct((table_rows, LANES), F32),
        ),
        in_specs=[VMEM] * 7,
        out_specs=(VMEM,) * 3,
        scratch_shapes=[pltpu.VMEM((message_rows, LANES), F32)],
        compiler_params=params(),
        cost_estimate=cost(2 * tokens * channels * poles, 2 << 20),
        name="signal",
    )(skip.reshape(fold, LANES), q, k, v, short_taps, rates.T, residues.T)


def near_part(q, signal, table, poles, taps):
    tokens, channels = q.shape
    return pl.pallas_call(
        functools.partial(near_kernel, poles, taps),
        out_shape=(
            jax.ShapeDtypeStruct((tokens, channels), BF16),
            jax.ShapeDtypeStruct((tokens, channels), F32),
        ),
        in_specs=[VMEM] * 3,
        out_specs=(VMEM,) * 2,
        scratch_shapes=[pltpu.VMEM(signal.shape, F32)],
        compiler_params=params(),
        cost_estimate=cost(4 * tokens * channels * poles, 2 << 20),
        name="near_filter",
    )(q, signal, table)


class Table:
    def __init__(self, ref, poles, taps, fold, tokens, weights=None):
        self.ref, self.poles, self.taps, self.fold, self.edge = ref, poles, taps, fold, taps - 1
        self.rates = ref[0 : poles * fold, :].reshape(poles, fold, LANES)
        self.residues = ref[poles * fold : 2 * poles * fold, :].reshape(poles, fold, LANES)
        self.tap_base = 2 * poles * fold
        skip_base = self.tap_base + 3 * taps * fold
        self.skip = ref[skip_base : skip_base + fold, :]
        self.tokens = tokens
        self.weights = weights

    def span(self, shards):
        if self.weights is not None:
            return self.weights[shards // 4, 0]
        return jnp.exp(-self.rates * float(shards * self.tokens))

    def tap(self, group, shift):
        row = self.tap_base + (group * self.taps + shift) * self.fold
        return self.ref[row : row + self.fold, :]

    def message(self, value):
        return value.astype(F32).reshape(-1, self.fold, LANES)

    def first(self, message, group):
        base = self.poles + group * 2 * self.edge
        return [message[base + i] for i in range(self.edge)]

    def last(self, message, group):
        base = self.poles + group * 2 * self.edge + self.edge
        return [message[base + i] for i in range(self.edge)]

    def mixed(self, before, current, group):
        rows = self.last(before, group) + self.first(current, group)
        return [
            sum(self.tap(group, shift) * rows[self.edge + i - shift] for shift in range(self.taps))
            for i in range(self.edge)
        ]

    def signals(self, before, current):
        pairs = zip(self.mixed(before, current, 1), self.mixed(before, current, 2))
        return [k * v for k, v in pairs]

    def lead(self, shards):
        if self.weights is not None:
            return [self.weights[shards // 4, 1 + i] for i in range(self.edge)]
        last = shards * self.tokens - 1
        return [jnp.exp(-self.rates * float(last - i)) * self.residues for i in range(self.edge)]

    def enter(self, state, span, lead, before, current):
        state = span * state + current[: self.poles]
        for weight, value in zip(lead, self.signals(before, current)):
            state = state + weight * value[None]
        return state


def enter_any(table, place_ref, messages_ref):
    span, lead = table.span(1), table.lead(1)

    def pick(index):
        current = table.message(messages_ref[index])
        before = table.message(messages_ref[jnp.maximum(index - 1, 0)])
        return jnp.where(index > 0, before, 0.0), current

    def one(index, state):
        return table.enter(state, span, lead, *pick(index))

    zero = jnp.zeros((table.poles, table.fold, LANES), F32)
    state = lax.fori_loop(0, place_ref[0], one, zero)
    return (state,) + pick(place_ref[0])


def in_order(place, values):
    out = []
    for p in range(4):
        value = values[p]
        for g in range(1, 4):
            value = jnp.where(place == g, values[p ^ g], value)
        out.append(value)
    return out


def enter_group(table, place_ref, *refs):
    messages = [table.message(ref[...]) for ref in refs[3::-1] + refs[4:]]
    place, group = place_ref[0], in_order(place_ref[0], messages[:4])
    before = jnp.zeros_like(messages[4])
    state = table.enter(before[: table.poles], table.span(4), table.lead(4), before, messages[4])
    before = messages[4]
    for p in range(3):
        behind = table.enter(state, table.span(1), table.lead(1), before, group[p])
        state = jnp.where(p < place, behind, state)
        before = jnp.where(p < place, group[p], before)
    return state, before, messages[0]


def join_kernel(poles, taps, tokens, place_ref, *refs):
    message_refs, (table_ref, out_ref) = refs[3::-1], refs[4:]
    fold = out_ref.shape[0] // (poles + 6 * (taps - 1))
    table = Table(table_ref, poles, taps, fold, tokens)
    group = in_order(place_ref[0], [table.message(ref[...]) for ref in message_refs])
    span, lead = table.span(1), table.lead(1)
    state = group[0][:poles]
    for before, current in zip(group[:-1], group[1:]):
        state = table.enter(state, span, lead, before, current)
    out = [state[r] for r in range(poles)]
    for kind in range(3):
        out += table.first(group[0], kind) + table.last(group[3], kind)
    out_ref[...] = jnp.concatenate(out, axis=0).astype(BF16)


def join_part(place, messages, table, tokens, poles, taps):
    return pl.pallas_call(
        functools.partial(join_kernel, poles, taps, tokens),
        out_shape=jax.ShapeDtypeStruct(messages[0].shape, BF16),
        in_specs=[SMEM] + [VMEM] * 5,
        out_specs=VMEM,
        compiler_params=params(),
        cost_estimate=cost(1 << 20, 1 << 18),
        name="join_state",
    )(place.reshape(1).astype(jnp.int32), *messages[::-1], table)


def weights_kernel(poles, taps, tokens, table_ref, out_ref):
    fold = out_ref.shape[3]
    table = Table(table_ref, poles, taps, fold, tokens)
    for i, shards in enumerate((1, 4)):
        for j, weight in enumerate([table.span(shards)] + table.lead(shards)):
            out_ref[i, j] = weight


def weights_part(table, tokens, poles, taps, fold):
    return pl.pallas_call(
        functools.partial(weights_kernel, poles, taps, tokens),
        out_shape=jax.ShapeDtypeStruct((2, taps, poles, fold, LANES), F32),
        in_specs=[VMEM],
        out_specs=VMEM,
        compiler_params=params(),
        cost_estimate=cost(1 << 20, 1 << 20),
        name="state_weights",
    )(table)


def far_kernel(poles, taps, count, enter, place_ref, near_ref, gate_ref, table_ref, *refs):
    message_refs, weights_refs, (out_ref, conv_s) = refs[:count], refs[count:-2], refs[-2:]
    tokens, channels = near_ref.shape
    fold = channels // LANES
    table = Table(table_ref, poles, taps, fold, tokens, *weights_refs)
    edge = table.edge
    state, before, current = enter(table, place_ref, *message_refs)
    decay = [jnp.exp(-table.rates[r]) for r in range(poles)]
    modes = tuple(state[r] for r in range(poles))
    for t, value in enumerate(table.signals(before, current)):
        modes = tuple(decay[r] * modes[r] + table.residues[r] * value for r in range(poles))
        conv_s[t * fold : (t + 1) * fold, :] = tree_sum(modes + (table.skip * value,))

    def step(t, modes):
        modes = tuple(d * m for d, m in zip(decay, modes))
        conv_s[pl.ds(pl.multiple_of(t * fold, fold), fold), :] = tree_sum(modes)
        return modes

    lax.fori_loop(edge, tokens, step, modes, unroll=6)
    row_id = lax.broadcasted_iota(jnp.int32, (tokens, LANES), 0)
    first = table.mixed(before, current, 0)
    for j in range(fold):
        lanes = slice(j * LANES, (j + 1) * LANES)
        gate = gate_ref[:, lanes]
        for t in range(edge):
            gate = jnp.where(row_id == t, first[t][j : j + 1, :], gate)
        conv = conv_s[pl.ds(j, tokens, stride=fold), :]
        out_ref[:, lanes] = (near_ref[:, lanes].astype(F32) + gate * conv).astype(BF16)


def far_part(enter, place, near, gate, table, messages, poles, taps, weights=()):
    tokens, channels = near.shape
    fold = channels // LANES
    count = len(messages)
    return pl.pallas_call(
        functools.partial(far_kernel, poles, taps, count, enter),
        out_shape=jax.ShapeDtypeStruct((tokens, channels), BF16),
        in_specs=[SMEM] + [VMEM] * (3 + count + len(weights)),
        out_specs=VMEM,
        scratch_shapes=[pltpu.VMEM(folded_shape(tokens, fold), F32)],
        compiler_params=params(),
        cost_estimate=cost(4 * tokens * channels * poles, 3 << 20),
        name="far_filter",
    )(place.reshape(1).astype(jnp.int32), near, gate, table, *messages, *weights)


def project(rows, weight_ref):
    stacked = jnp.concatenate([r[...] for r in rows], axis=0) if len(rows) > 1 else rows[0][...]
    product = lax.dot_general(
        stacked, weight_ref[...], (((1,), (1,)), ((), ())), preferred_element_type=F32
    ).astype(BF16)
    tokens = rows[0].shape[0]
    return [product[i * tokens : (i + 1) * tokens] for i in range(len(rows))]


def own_kernel(*refs):
    *rows_refs, weight_ref, out_ref = refs
    for i, product in enumerate(project(rows_refs, weight_ref)):
        out_ref[i] = product


def other_kernel(
    place_ref, zero_ref, one_ref, two_ref, near_own_ref, two_own_ref, weight_ref, near_ref, out_ref
):
    odd = place_ref[0]
    zero, one, two = project([zero_ref, one_ref, two_ref], weight_ref)
    for i, product in enumerate((zero, one)):
        near_ref[odd ^ i, 0] = near_own_ref[i]
        near_ref[odd ^ i, 1] = product
    out_ref[0] = two_own_ref[0]
    out_ref[1] = two


def far_project_kernel(place_ref, two_ref, three_ref, own_ref, other_ref, out_ref):
    odd = place_ref[0]
    out_ref[odd] = two_ref[...]
    for half, ref in enumerate((own_ref, other_ref)):
        out_ref[1 - odd, half] = project([three_ref], ref)[0]


def project_part(kernel, name, operands, shapes, flops):
    out_shape = tuple(jax.ShapeDtypeStruct(shape, BF16) for shape in shapes)
    return pl.pallas_call(
        kernel,
        out_shape=out_shape,
        in_specs=[SMEM if x.dtype == jnp.int32 else VMEM for x in operands],
        out_specs=(VMEM,) * len(shapes),
        compiler_params=params(),
        cost_estimate=cost(flops, 3 << 20),
        name=name,
    )(*operands)


def finish_kernel(kind_ref, y_ref, *refs):
    out_ref = refs[-1]
    width = refs[0].shape[2]
    for pair in range((len(refs) - 1) // 2):
        for y in range(2):

            @pl.when((kind_ref[0] == pair) & (y_ref[0] == y))
            def _(pair=pair, y=y):
                for h in range(2):
                    total = refs[2 * pair][h ^ y].astype(F32) + refs[2 * pair + 1][h ^ y].astype(F32)
                    out_ref[:, h * width : (h + 1) * width] = total.astype(BF16)


def permute(name, x, move, keep=None):
    pairs = []
    for index in range(32):
        place = (index // 8, index // 4 % 2, index // 2 % 2, index % 2)
        if keep is None or keep(*place):
            z, y, x_, c = move(*place)
            pairs.append((index, ((z * 2 + y) * 2 + x_) * 2 + c))
    with jax.named_scope(name):
        return lax.ppermute(x, AXES, pairs)


def over_y(z, y, x, c):
    return z, 1 - y, x, c


def over_z0(z, y, x, c):
    return z ^ 1, y, x, c


def over_z1(z, y, x, c):
    return z ^ 2, y, x, c


def over_core(z, y, x, c):
    return z, y, x, 1 - c


def after(x, *others):
    return lax.optimization_barrier((x,) + others)[0]


def per_device_32(features, short_taps, rates, residues, skip, out_weight):
    tokens, _, channels = features.shape
    q, k, v = (features[:, group] for group in range(3))
    poles, taps = rates.shape[1], short_taps.shape[1]
    seq, tp = lax.axis_index("seq"), lax.axis_index("tp")
    z, y = seq >> 1, seq & 1
    signal, message, table = signal_part(q, k, v, short_taps, rates, residues, skip)
    near, gate = near_part(q, signal, table, poles, taps)
    messages = [
        message,
        permute("state_y", message, over_y),
        permute("state_z", message, over_z0),
        permute("state_zy", message, lambda z, y, x, c: (z ^ 1, 1 - y, x, c)),
    ]
    place = seq & 3
    joined = join_part(place, messages, table, tokens, poles, taps)
    weights = weights_part(after(table, joined), tokens, poles, taps, channels // LANES)
    w_y = permute("weights", after(out_weight, weights), over_y)
    joined = permute("state_half", joined, over_z1, lambda z, y, x, c: z < 2)
    gated = far_part(
        enter_group, place, near, gate, table, messages[::-1] + [joined], poles, taps, [weights]
    )
    two = permute("gated_two", gated, over_z1)
    one = permute("gated_one", gated, over_z0)
    three = permute("gated_three", two, over_z0)
    odd = (z ^ tp) & 1
    place = odd.reshape(1).astype(jnp.int32)

    def odd_of(z, y, x, c):
        return (z ^ c) % 2

    def home(summed, far):
        def move(z, y, x, c):
            return z ^ far ^ odd_of(z, y, x, c), y, z // 2, z % 2

        return [
            permute(f"straight_{far}", summed, move, lambda z, y, x, c: x == z // 2),
            permute(f"across_{far}", summed, move, lambda z, y, x, c: x != z // 2),
        ]

    def add_cores(name, kept, sent):
        from_core = permute(name, sent, over_core)
        return (kept.astype(F32) + from_core.astype(F32)).astype(BF16)

    width = out_weight.shape[0]
    whole, flops = (2, tokens, width), 2 * tokens * channels * width
    (two_own,) = project_part(own_kernel, "project_two", [two, out_weight], [(1, tokens, width)], flops)
    (near_own,) = project_part(
        own_kernel, "project_near", [gated, one, out_weight], [whole], 2 * flops
    )
    near, part_two = project_part(
        other_kernel,
        "project_other",
        [place, gated, one, two, near_own, two_own, w_y],
        [(2,) + whole, whole],
        3 * flops,
    )
    (far,) = project_part(
        far_project_kernel,
        "project_far",
        [place, part_two, three, out_weight, w_y],
        [(2,) + whole],
        2 * flops,
    )
    far_sum = add_cores("core_far", far[0], far[1])
    near = after(near, far_sum)
    near_sum = add_cores("core_near", near[0], near[1])
    parts = home(near_sum, 0) + home(far_sum, 2)
    kind = (z ^ tp) >> 1
    return pl.pallas_call(
        finish_kernel,
        out_shape=jax.ShapeDtypeStruct((tokens, 2 * out_weight.shape[0]), BF16),
        in_specs=[SMEM] * 2 + [VMEM] * len(parts),
        out_specs=VMEM,
        compiler_params=params(),
        cost_estimate=cost(4 * tokens * out_weight.shape[0], 2 << 20),
        name="finish",
    )(kind.reshape(1).astype(jnp.int32), y.reshape(1).astype(jnp.int32), *parts)


def per_device(features, short_taps, rates, residues, skip, out_weight):
    q, k, v = (features[:, group] for group in range(3))
    poles, taps = rates.shape[1], short_taps.shape[1]
    signal, message, table = signal_part(q, k, v, short_taps, rates, residues, skip)
    near, gate = near_part(q, signal, table, poles, taps)
    messages = lax.all_gather(message, "seq")
    place = lax.axis_index("seq")
    gated = far_part(enter_any, place, near, gate, table, [messages], poles, taps)
    partial = lax.dot_general(
        gated,
        lax.all_gather(out_weight, "seq", axis=0, tiled=True),
        (((1,), (1,)), ((), ())),
        preferred_element_type=F32,
    )
    return lax.psum_scatter(partial.astype(BF16), "tp", scatter_dimension=1, tiled=True)


def solution(mesh):
    in_specs = (
        P("seq", None, "tp"),
        P(None, None, "tp"),
        P("tp", None),
        P("tp", None),
        P("tp"),
        P("seq", "tp"),
    )
    out_specs = P("seq", "tp")
    body = per_device_32 if (mesh.shape["seq"], mesh.shape["tp"]) == (8, 4) else per_device
    return jax.shard_map(body, mesh=mesh, in_specs=in_specs, out_specs=out_specs, check_vma=False)
```

```python
import functools

import jax
import jax.numpy as jnp
from jax import lax
from jax.experimental import pallas as pl
from jax.experimental.pallas import tpu as pltpu
from jax.sharding import PartitionSpec as P

LANES = 128
SUBLANES = 16
F32 = jnp.float32
BF16 = jnp.bfloat16
VMEM = pl.BlockSpec(memory_space=pltpu.VMEM)
SMEM = pl.BlockSpec(memory_space=pltpu.SMEM)
AXES = ("seq", "tp")


def cost(flops, bytes_accessed):
    return pl.CostEstimate(flops=flops, bytes_accessed=bytes_accessed, transcendentals=0)


def params(**kw):
    return pltpu.CompilerParams(vmem_limit_bytes=16 * 1024 * 1024, **kw)


def signal_kernel(
    skip_ref, q_ref, k_ref, v_ref, taps_ref, rates_ref, residues_ref,
    signal_ref, message_ref, table_ref,
    message_s,
):
    tokens, channels = q_ref.shape
    poles, taps = rates_ref.shape[0], taps_ref.shape[1]
    fold = channels // LANES
    edge = taps - 1
    tap_row = 2 * poles
    skip_row = tap_row + 3 * taps
    table_ref[skip_row * fold : (skip_row + 1) * fold, :] = skip_ref[...]
    later = lax.broadcasted_iota(jnp.int32, (tokens, LANES), 0) >= edge
    for j in range(fold):
        lanes = slice(j * LANES, (j + 1) * LANES)
        table_ref[pl.ds(j, poles, stride=fold), :] = rates_ref[:, lanes]
        table_ref[pl.ds(poles * fold + j, poles, stride=fold), :] = residues_ref[:, lanes]
        mixed = []
        for group, ref in enumerate((q_ref, k_ref, v_ref)):
            total = None
            value = ref[:, lanes].astype(F32) if group else None
            for shift in range(taps):
                row = (tap_row + group * taps + shift) * fold + j
                tap = taps_ref[group, shift : shift + 1, lanes].astype(F32)
                table_ref[row : row + 1, :] = tap
                if group:
                    moved = value if shift == 0 else pltpu.roll(value, shift, axis=0)
                    total = tap * moved if total is None else total + tap * moved
            mixed.append(total)
            first, last = ref[:SUBLANES, lanes].astype(F32), ref[-SUBLANES:, lanes].astype(F32)
            for place in range(2 * edge):
                row = (poles + group * 2 * edge + place) * fold + j
                source = place if place < edge else SUBLANES - 2 * edge + place
                source_rows = first if place < edge else last
                message_s[row : row + 1, :] = source_rows[source : source + 1, :]
        signal = jnp.where(later, mixed[1] * mixed[2], 0.0)
        signal_ref[pl.ds(j, tokens, stride=fold), :] = signal
    decay = [jnp.exp(-table_ref[r * fold : (r + 1) * fold, :]) for r in range(poles)]

    def step(t, modes):
        value = signal_ref[pl.ds(pl.multiple_of(t * fold, fold), fold), :]
        return tuple(d * m + value for d, m in zip(decay, modes))

    modes = lax.fori_loop(0, tokens, step, (jnp.zeros((fold, LANES), F32),) * poles, unroll=32)
    for r in range(poles):
        residue = table_ref[(poles + r) * fold : (poles + r + 1) * fold, :]
        message_s[r * fold : (r + 1) * fold, :] = residue * modes[r]
    message_ref[...] = message_s[...].astype(BF16)


def near_kernel(poles, taps, q_ref, signal_ref, table_ref, out_ref, gate_ref, conv_s):
    tokens, channels = q_ref.shape
    fold = channels // LANES
    tap_row = 2 * poles
    skip_row = tap_row + 3 * taps
    decay = [jnp.exp(-table_ref[r * fold : (r + 1) * fold, :]) for r in range(poles)]
    residue = [table_ref[(poles + r) * fold : (poles + r + 1) * fold, :] for r in range(poles)]
    skip = table_ref[skip_row * fold : (skip_row + 1) * fold, :]

    def step(t, modes):
        rows = pl.ds(pl.multiple_of(t * fold, fold), fold)
        value = signal_ref[rows, :]
        modes = tuple(d * m + c * value for d, c, m in zip(decay, residue, modes))
        conv_s[rows, :] = tree_sum(modes + (skip * value,))
        return modes

    lax.fori_loop(0, tokens, step, (jnp.zeros((fold, LANES), F32),) * poles, unroll=4)
    for j in range(fold):
        lanes = slice(j * LANES, (j + 1) * LANES)
        value = q_ref[:, lanes].astype(F32)
        gate = None
        for shift in range(taps):
            row = (tap_row + shift) * fold + j
            moved = value if shift == 0 else pltpu.roll(value, shift, axis=0)
            term = table_ref[row : row + 1, :] * moved
            gate = term if gate is None else gate + term
        gate_ref[:, lanes] = gate
        conv = conv_s[pl.ds(j, tokens, stride=fold), :]
        out_ref[:, lanes] = (gate * conv).astype(BF16)


def folded_shape(tokens, fold):
    return ((tokens + 1) * fold, LANES)


def tree_sum(values):
    values = list(values)
    while len(values) > 1:
        values = [a + b for a, b in zip(values[::2], values[1::2])] + (
            [values[-1]] if len(values) % 2 else []
        )
    return values[0]


def signal_part(q, k, v, short_taps, rates, residues, skip):
    tokens, channels = q.shape
    poles, taps = rates.shape[1], short_taps.shape[1]
    fold = channels // LANES
    message_rows = (poles + 6 * (taps - 1)) * fold
    table_rows = (2 * poles + 3 * taps + 1) * fold
    return pl.pallas_call(
        signal_kernel,
        out_shape=(
            jax.ShapeDtypeStruct(folded_shape(tokens, fold), F32),
            jax.ShapeDtypeStruct((message_rows, LANES), BF16),
            jax.ShapeDtypeStruct((table_rows, LANES), F32),
        ),
        in_specs=[VMEM] * 7,
        out_specs=(VMEM,) * 3,
        scratch_shapes=[pltpu.VMEM((message_rows, LANES), F32)],
        compiler_params=params(),
        cost_estimate=cost(2 * tokens * channels * poles, 2 << 20),
        name="signal",
    )(skip.reshape(fold, LANES), q, k, v, short_taps, rates.T, residues.T)


def near_part(q, signal, table, poles, taps):
    tokens, channels = q.shape
    return pl.pallas_call(
        functools.partial(near_kernel, poles, taps),
        out_shape=(
            jax.ShapeDtypeStruct((tokens, channels), BF16),
            jax.ShapeDtypeStruct((tokens, channels), F32),
        ),
        in_specs=[VMEM] * 3,
        out_specs=(VMEM,) * 2,
        scratch_shapes=[pltpu.VMEM(signal.shape, F32)],
        compiler_params=params(),
        cost_estimate=cost(4 * tokens * channels * poles, 2 << 20),
        name="near_filter",
    )(q, signal, table)


class Table:
    def __init__(self, ref, poles, taps, fold, tokens, weights=None):
        self.ref, self.poles, self.taps, self.fold, self.edge = ref, poles, taps, fold, taps - 1
        self.rates = ref[0 : poles * fold, :].reshape(poles, fold, LANES)
        self.residues = ref[poles * fold : 2 * poles * fold, :].reshape(poles, fold, LANES)
        self.tap_base = 2 * poles * fold
        skip_base = self.tap_base + 3 * taps * fold
        self.skip = ref[skip_base : skip_base + fold, :]
        self.tokens = tokens
        self.weights = weights

    def span(self, shards):
        if self.weights is not None:
            return self.weights[shards // 4, 0]
        return jnp.exp(-self.rates * float(shards * self.tokens))

    def tap(self, group, shift):
        row = self.tap_base + (group * self.taps + shift) * self.fold
        return self.ref[row : row + self.fold, :]

    def message(self, value):
        return value.astype(F32).reshape(-1, self.fold, LANES)

    def first(self, message, group):
        base = self.poles + group * 2 * self.edge
        return [message[base + i] for i in range(self.edge)]

    def last(self, message, group):
        base = self.poles + group * 2 * self.edge + self.edge
        return [message[base + i] for i in range(self.edge)]

    def mixed(self, before, current, group):
        rows = self.last(before, group) + self.first(current, group)
        return [
            sum(self.tap(group, shift) * rows[self.edge + i - shift] for shift in range(self.taps))
            for i in range(self.edge)
        ]

    def signals(self, before, current):
        pairs = zip(self.mixed(before, current, 1), self.mixed(before, current, 2))
        return [k * v for k, v in pairs]

    def lead(self, shards):
        if self.weights is not None:
            return [self.weights[shards // 4, 1 + i] for i in range(self.edge)]
        last = shards * self.tokens - 1
        return [jnp.exp(-self.rates * float(last - i)) * self.residues for i in range(self.edge)]

    def enter(self, state, span, lead, before, current):
        state = span * state + current[: self.poles]
        for weight, value in zip(lead, self.signals(before, current)):
            state = state + weight * value[None]
        return state


def enter_any(table, place_ref, messages_ref):
    span, lead = table.span(1), table.lead(1)

    def pick(index):
        current = table.message(messages_ref[index])
        before = table.message(messages_ref[jnp.maximum(index - 1, 0)])
        return jnp.where(index > 0, before, 0.0), current

    def one(index, state):
        return table.enter(state, span, lead, *pick(index))

    zero = jnp.zeros((table.poles, table.fold, LANES), F32)
    state = lax.fori_loop(0, place_ref[0], one, zero)
    return (state,) + pick(place_ref[0])


def in_order(place, values):
    out = []
    for p in range(4):
        value = values[p]
        for g in range(1, 4):
            value = jnp.where(place == g, values[p ^ g], value)
        out.append(value)
    return out


def enter_group(table, place_ref, *refs):
    messages = [table.message(ref[...]) for ref in refs[3::-1] + refs[4:]]
    place, group = place_ref[0], in_order(place_ref[0], messages[:4])
    before = jnp.zeros_like(messages[4])
    state = table.enter(before[: table.poles], table.span(4), table.lead(4), before, messages[4])
    before = messages[4]
    for p in range(3):
        behind = table.enter(state, table.span(1), table.lead(1), before, group[p])
        state = jnp.where(p < place, behind, state)
        before = jnp.where(p < place, group[p], before)
    return state, before, messages[0]


def join_kernel(poles, taps, tokens, place_ref, *refs):
    message_refs, (table_ref, out_ref) = refs[3::-1], refs[4:]
    fold = out_ref.shape[0] // (poles + 6 * (taps - 1))
    table = Table(table_ref, poles, taps, fold, tokens)
    group = in_order(place_ref[0], [table.message(ref[...]) for ref in message_refs])
    span, lead = table.span(1), table.lead(1)
    state = group[0][:poles]
    for before, current in zip(group[:-1], group[1:]):
        state = table.enter(state, span, lead, before, current)
    out = [state[r] for r in range(poles)]
    for kind in range(3):
        out += table.first(group[0], kind) + table.last(group[3], kind)
    out_ref[...] = jnp.concatenate(out, axis=0).astype(BF16)


def join_part(place, messages, table, tokens, poles, taps):
    return pl.pallas_call(
        functools.partial(join_kernel, poles, taps, tokens),
        out_shape=jax.ShapeDtypeStruct(messages[0].shape, BF16),
        in_specs=[SMEM] + [VMEM] * 5,
        out_specs=VMEM,
        compiler_params=params(),
        cost_estimate=cost(1 << 20, 1 << 18),
        name="join_state",
    )(place.reshape(1).astype(jnp.int32), *messages[::-1], table)


def weights_kernel(poles, taps, tokens, table_ref, out_ref):
    fold = out_ref.shape[3]
    table = Table(table_ref, poles, taps, fold, tokens)
    for i, shards in enumerate((1, 4)):
        for j, weight in enumerate([table.span(shards)] + table.lead(shards)):
            out_ref[i, j] = weight


def weights_part(table, tokens, poles, taps, fold):
    return pl.pallas_call(
        functools.partial(weights_kernel, poles, taps, tokens),
        out_shape=jax.ShapeDtypeStruct((2, taps, poles, fold, LANES), F32),
        in_specs=[VMEM],
        out_specs=VMEM,
        compiler_params=params(),
        cost_estimate=cost(1 << 20, 1 << 20),
        name="state_weights",
    )(table)


def far_kernel(poles, taps, count, enter, place_ref, near_ref, gate_ref, table_ref, *refs):
    message_refs, weights_refs, (out_ref, conv_s) = refs[:count], refs[count:-2], refs[-2:]
    tokens, channels = near_ref.shape
    fold = channels // LANES
    table = Table(table_ref, poles, taps, fold, tokens, *weights_refs)
    edge = table.edge
    state, before, current = enter(table, place_ref, *message_refs)
    decay = [jnp.exp(-table.rates[r]) for r in range(poles)]
    modes = tuple(state[r] for r in range(poles))
    for t, value in enumerate(table.signals(before, current)):
        modes = tuple(decay[r] * modes[r] + table.residues[r] * value for r in range(poles))
        conv_s[t * fold : (t + 1) * fold, :] = tree_sum(modes + (table.skip * value,))

    def step(t, modes):
        modes = tuple(d * m for d, m in zip(decay, modes))
        conv_s[pl.ds(pl.multiple_of(t * fold, fold), fold), :] = tree_sum(modes)
        return modes

    lax.fori_loop(edge, tokens, step, modes, unroll=18)
    row_id = lax.broadcasted_iota(jnp.int32, (tokens, LANES), 0)
    first = table.mixed(before, current, 0)
    for j in range(fold):
        lanes = slice(j * LANES, (j + 1) * LANES)
        gate = gate_ref[:, lanes]
        for t in range(edge):
            gate = jnp.where(row_id == t, first[t][j : j + 1, :], gate)
        conv = conv_s[pl.ds(j, tokens, stride=fold), :]
        out_ref[:, lanes] = (near_ref[:, lanes].astype(F32) + gate * conv).astype(BF16)


def far_part(enter, place, near, gate, table, messages, poles, taps, weights=()):
    tokens, channels = near.shape
    fold = channels // LANES
    count = len(messages)
    return pl.pallas_call(
        functools.partial(far_kernel, poles, taps, count, enter),
        out_shape=jax.ShapeDtypeStruct((tokens, channels), BF16),
        in_specs=[SMEM] + [VMEM] * (3 + count + len(weights)),
        out_specs=VMEM,
        scratch_shapes=[pltpu.VMEM(folded_shape(tokens, fold), F32)],
        compiler_params=params(),
        cost_estimate=cost(4 * tokens * channels * poles, 3 << 20),
        name="far_filter",
    )(place.reshape(1).astype(jnp.int32), near, gate, table, *messages, *weights)


def project(rows, weight_ref):
    stacked = jnp.concatenate([r[...] for r in rows], axis=0) if len(rows) > 1 else rows[0][...]
    product = lax.dot_general(
        stacked, weight_ref[...], (((1,), (1,)), ((), ())), preferred_element_type=F32
    ).astype(BF16)
    tokens = rows[0].shape[0]
    return [product[i * tokens : (i + 1) * tokens] for i in range(len(rows))]


def own_kernel(*refs):
    *rows_refs, weight_ref, out_ref = refs
    for i, product in enumerate(project(rows_refs, weight_ref)):
        out_ref[i] = product


def other_kernel(
    place_ref, zero_ref, one_ref, two_ref, near_own_ref, two_own_ref, weight_ref, near_ref, out_ref
):
    odd = place_ref[0]
    zero, one, two = project([zero_ref, one_ref, two_ref], weight_ref)
    for i, product in enumerate((zero, one)):
        near_ref[odd ^ i, 0] = near_own_ref[i]
        near_ref[odd ^ i, 1] = product
    out_ref[0] = two_own_ref[0]
    out_ref[1] = two


def far_project_kernel(place_ref, two_ref, three_ref, own_ref, other_ref, out_ref):
    odd = place_ref[0]
    out_ref[odd] = two_ref[...]
    for half, ref in enumerate((own_ref, other_ref)):
        out_ref[1 - odd, half] = project([three_ref], ref)[0]


def project_part(kernel, name, operands, shapes, flops):
    out_shape = tuple(jax.ShapeDtypeStruct(shape, BF16) for shape in shapes)
    return pl.pallas_call(
        kernel,
        out_shape=out_shape,
        in_specs=[SMEM if x.dtype == jnp.int32 else VMEM for x in operands],
        out_specs=(VMEM,) * len(shapes),
        compiler_params=params(),
        cost_estimate=cost(flops, 3 << 20),
        name=name,
    )(*operands)


def finish_kernel(kind_ref, y_ref, *refs):
    out_ref = refs[-1]
    width = refs[0].shape[2]
    for pair in range((len(refs) - 1) // 2):
        for y in range(2):

            @pl.when((kind_ref[0] == pair) & (y_ref[0] == y))
            def _(pair=pair, y=y):
                for h in range(2):
                    total = refs[2 * pair][h ^ y].astype(F32) + refs[2 * pair + 1][h ^ y].astype(F32)
                    out_ref[:, h * width : (h + 1) * width] = total.astype(BF16)


def permute(name, x, move, keep=None):
    pairs = []
    for index in range(32):
        place = (index // 8, index // 4 % 2, index // 2 % 2, index % 2)
        if keep is None or keep(*place):
            z, y, x_, c = move(*place)
            pairs.append((index, ((z * 2 + y) * 2 + x_) * 2 + c))
    with jax.named_scope(name):
        return lax.ppermute(x, AXES, pairs)


def over_y(z, y, x, c):
    return z, 1 - y, x, c


def over_z0(z, y, x, c):
    return z ^ 1, y, x, c


def over_z1(z, y, x, c):
    return z ^ 2, y, x, c


def over_core(z, y, x, c):
    return z, y, x, 1 - c


def after(x, *others):
    return lax.optimization_barrier((x,) + others)[0]


def per_device_32(features, short_taps, rates, residues, skip, out_weight):
    tokens, _, channels = features.shape
    q, k, v = (features[:, group] for group in range(3))
    poles, taps = rates.shape[1], short_taps.shape[1]
    seq, tp = lax.axis_index("seq"), lax.axis_index("tp")
    z, y = seq >> 1, seq & 1
    signal, message, table = signal_part(q, k, v, short_taps, rates, residues, skip)
    near, gate = near_part(q, signal, table, poles, taps)
    messages = [
        message,
        permute("state_y", message, over_y),
        permute("state_z", message, over_z0),
        permute("state_zy", message, lambda z, y, x, c: (z ^ 1, 1 - y, x, c)),
    ]
    place = seq & 3
    joined = join_part(place, messages, table, tokens, poles, taps)
    weights = weights_part(after(table, joined), tokens, poles, taps, channels // LANES)
    w_y = permute("weights", after(out_weight, weights), over_y)
    joined = permute("state_half", joined, over_z1, lambda z, y, x, c: z < 2)
    gated = far_part(
        enter_group, place, near, gate, table, messages[::-1] + [joined], poles, taps, [weights]
    )
    two = permute("gated_two", gated, over_z1)
    one = permute("gated_one", gated, over_z0)
    three = permute("gated_three", two, over_z0)
    odd = (z ^ tp) & 1
    place = odd.reshape(1).astype(jnp.int32)

    def odd_of(z, y, x, c):
        return (z ^ c) % 2

    def home(summed, far):
        def move(z, y, x, c):
            return z ^ far ^ odd_of(z, y, x, c), y, z // 2, z % 2

        return [
            permute(f"straight_{far}", summed, move, lambda z, y, x, c: x == z // 2),
            permute(f"across_{far}", summed, move, lambda z, y, x, c: x != z // 2),
        ]

    def add_cores(name, kept, sent):
        from_core = permute(name, sent, over_core)
        return (kept.astype(F32) + from_core.astype(F32)).astype(BF16)

    width = out_weight.shape[0]
    whole, flops = (2, tokens, width), 2 * tokens * channels * width
    (two_own,) = project_part(own_kernel, "project_two", [two, out_weight], [(1, tokens, width)], flops)
    (near_own,) = project_part(
        own_kernel, "project_near", [gated, one, out_weight], [whole], 2 * flops
    )
    near, part_two = project_part(
        other_kernel,
        "project_other",
        [place, gated, one, two, near_own, two_own, w_y],
        [(2,) + whole, whole],
        3 * flops,
    )
    (far,) = project_part(
        far_project_kernel,
        "project_far",
        [place, part_two, three, out_weight, w_y],
        [(2,) + whole],
        2 * flops,
    )
    far_sum = add_cores("core_far", far[0], far[1])
    near = after(near, far_sum)
    near_sum = add_cores("core_near", near[0], near[1])
    parts = home(near_sum, 0) + home(far_sum, 2)
    kind = (z ^ tp) >> 1
    return pl.pallas_call(
        finish_kernel,
        out_shape=jax.ShapeDtypeStruct((tokens, 2 * out_weight.shape[0]), BF16),
        in_specs=[SMEM] * 2 + [VMEM] * len(parts),
        out_specs=VMEM,
        compiler_params=params(),
        cost_estimate=cost(4 * tokens * out_weight.shape[0], 2 << 20),
        name="finish",
    )(kind.reshape(1).astype(jnp.int32), y.reshape(1).astype(jnp.int32), *parts)


def per_device(features, short_taps, rates, residues, skip, out_weight):
    q, k, v = (features[:, group] for group in range(3))
    poles, taps = rates.shape[1], short_taps.shape[1]
    signal, message, table = signal_part(q, k, v, short_taps, rates, residues, skip)
    near, gate = near_part(q, signal, table, poles, taps)
    messages = lax.all_gather(message, "seq")
    place = lax.axis_index("seq")
    gated = far_part(enter_any, place, near, gate, table, [messages], poles, taps)
    partial = lax.dot_general(
        gated,
        lax.all_gather(out_weight, "seq", axis=0, tiled=True),
        (((1,), (1,)), ((), ())),
        preferred_element_type=F32,
    )
    return lax.psum_scatter(partial.astype(BF16), "tp", scatter_dimension=1, tiled=True)


def solution(mesh):
    in_specs = (
        P("seq", None, "tp"),
        P(None, None, "tp"),
        P("tp", None),
        P("tp", None),
        P("tp"),
        P("seq", "tp"),
    )
    out_specs = P("seq", "tp")
    body = per_device_32 if (mesh.shape["seq"], mesh.shape["tp"]) == (8, 4) else per_device
    return jax.shard_map(body, mesh=mesh, in_specs=in_specs, out_specs=out_specs, check_vma=False)
```

```python
import functools

import jax
import jax.numpy as jnp
from jax import lax
from jax.experimental import pallas as pl
from jax.experimental.pallas import tpu as pltpu
from jax.sharding import PartitionSpec as P

LANES = 128
SUBLANES = 16
F32 = jnp.float32
BF16 = jnp.bfloat16
VMEM = pl.BlockSpec(memory_space=pltpu.VMEM)
SMEM = pl.BlockSpec(memory_space=pltpu.SMEM)
AXES = ("seq", "tp")


def cost(flops, bytes_accessed):
    return pl.CostEstimate(flops=flops, bytes_accessed=bytes_accessed, transcendentals=0)


def params(**kw):
    return pltpu.CompilerParams(vmem_limit_bytes=16 * 1024 * 1024, **kw)


def signal_kernel(
    skip_ref, q_ref, k_ref, v_ref, taps_ref, rates_ref, residues_ref,
    signal_ref, message_ref, table_ref,
    message_s,
):
    tokens, channels = q_ref.shape
    poles, taps = rates_ref.shape[0], taps_ref.shape[1]
    fold = channels // LANES
    edge = taps - 1
    tap_row = 2 * poles
    skip_row = tap_row + 3 * taps
    table_ref[skip_row * fold : (skip_row + 1) * fold, :] = skip_ref[...]
    later = lax.broadcasted_iota(jnp.int32, (tokens, LANES), 0) >= edge
    for j in range(fold):
        lanes = slice(j * LANES, (j + 1) * LANES)
        table_ref[pl.ds(j, poles, stride=fold), :] = rates_ref[:, lanes]
        table_ref[pl.ds(poles * fold + j, poles, stride=fold), :] = residues_ref[:, lanes]
        mixed = []
        for group, ref in enumerate((q_ref, k_ref, v_ref)):
            total = None
            value = ref[:, lanes].astype(F32) if group else None
            for shift in range(taps):
                row = (tap_row + group * taps + shift) * fold + j
                tap = taps_ref[group, shift : shift + 1, lanes].astype(F32)
                table_ref[row : row + 1, :] = tap
                if group:
                    moved = value if shift == 0 else pltpu.roll(value, shift, axis=0)
                    total = tap * moved if total is None else total + tap * moved
            mixed.append(total)
            first, last = ref[:SUBLANES, lanes].astype(F32), ref[-SUBLANES:, lanes].astype(F32)
            for place in range(2 * edge):
                row = (poles + group * 2 * edge + place) * fold + j
                source = place if place < edge else SUBLANES - 2 * edge + place
                source_rows = first if place < edge else last
                message_s[row : row + 1, :] = source_rows[source : source + 1, :]
        signal = jnp.where(later, mixed[1] * mixed[2], 0.0)
        signal_ref[pl.ds(j, tokens, stride=fold), :] = signal
    decay = [jnp.exp(-table_ref[r * fold : (r + 1) * fold, :]) for r in range(poles)]

    def step(t, modes):
        value = signal_ref[pl.ds(pl.multiple_of(t * fold, fold), fold), :]
        return tuple(d * m + value for d, m in zip(decay, modes))

    modes = lax.fori_loop(0, tokens, step, (jnp.zeros((fold, LANES), F32),) * poles, unroll=32)
    for r in range(poles):
        residue = table_ref[(poles + r) * fold : (poles + r + 1) * fold, :]
        message_s[r * fold : (r + 1) * fold, :] = residue * modes[r]
    message_ref[...] = message_s[...].astype(BF16)


def near_kernel(poles, taps, q_ref, signal_ref, table_ref, out_ref, gate_ref, conv_s):
    tokens, channels = q_ref.shape
    fold = channels // LANES
    tap_row = 2 * poles
    skip_row = tap_row + 3 * taps
    decay = [jnp.exp(-table_ref[r * fold : (r + 1) * fold, :]) for r in range(poles)]
    residue = [table_ref[(poles + r) * fold : (poles + r + 1) * fold, :] for r in range(poles)]
    skip = table_ref[skip_row * fold : (skip_row + 1) * fold, :]

    def step(t, modes):
        rows = pl.ds(pl.multiple_of(t * fold, fold), fold)
        value = signal_ref[rows, :]
        modes = tuple(d * m + c * value for d, c, m in zip(decay, residue, modes))
        conv_s[rows, :] = tree_sum(modes + (skip * value,))
        return modes

    lax.fori_loop(0, tokens, step, (jnp.zeros((fold, LANES), F32),) * poles, unroll=8)
    for j in range(fold):
        lanes = slice(j * LANES, (j + 1) * LANES)
        value = q_ref[:, lanes].astype(F32)
        gate = None
        for shift in range(taps):
            row = (tap_row + shift) * fold + j
            moved = value if shift == 0 else pltpu.roll(value, shift, axis=0)
            term = table_ref[row : row + 1, :] * moved
            gate = term if gate is None else gate + term
        gate_ref[:, lanes] = gate
        conv = conv_s[pl.ds(j, tokens, stride=fold), :]
        out_ref[:, lanes] = (gate * conv).astype(BF16)


def folded_shape(tokens, fold):
    return ((tokens + 1) * fold, LANES)


def tree_sum(values):
    values = list(values)
    while len(values) > 1:
        values = [a + b for a, b in zip(values[::2], values[1::2])] + (
            [values[-1]] if len(values) % 2 else []
        )
    return values[0]


def signal_part(q, k, v, short_taps, rates, residues, skip):
    tokens, channels = q.shape
    poles, taps = rates.shape[1], short_taps.shape[1]
    fold = channels // LANES
    message_rows = (poles + 6 * (taps - 1)) * fold
    table_rows = (2 * poles + 3 * taps + 1) * fold
    return pl.pallas_call(
        signal_kernel,
        out_shape=(
            jax.ShapeDtypeStruct(folded_shape(tokens, fold), F32),
            jax.ShapeDtypeStruct((message_rows, LANES), BF16),
            jax.ShapeDtypeStruct((table_rows, LANES), F32),
        ),
        in_specs=[VMEM] * 7,
        out_specs=(VMEM,) * 3,
        scratch_shapes=[pltpu.VMEM((message_rows, LANES), F32)],
        compiler_params=params(),
        cost_estimate=cost(2 * tokens * channels * poles, 2 << 20),
        name="signal",
    )(skip.reshape(fold, LANES), q, k, v, short_taps, rates.T, residues.T)


def near_part(q, signal, table, poles, taps):
    tokens, channels = q.shape
    return pl.pallas_call(
        functools.partial(near_kernel, poles, taps),
        out_shape=(
            jax.ShapeDtypeStruct((tokens, channels), BF16),
            jax.ShapeDtypeStruct((tokens, channels), F32),
        ),
        in_specs=[VMEM] * 3,
        out_specs=(VMEM,) * 2,
        scratch_shapes=[pltpu.VMEM(signal.shape, F32)],
        compiler_params=params(),
        cost_estimate=cost(4 * tokens * channels * poles, 2 << 20),
        name="near_filter",
    )(q, signal, table)


class Table:
    def __init__(self, ref, poles, taps, fold, tokens, weights=None):
        self.ref, self.poles, self.taps, self.fold, self.edge = ref, poles, taps, fold, taps - 1
        self.rates = ref[0 : poles * fold, :].reshape(poles, fold, LANES)
        self.residues = ref[poles * fold : 2 * poles * fold, :].reshape(poles, fold, LANES)
        self.tap_base = 2 * poles * fold
        skip_base = self.tap_base + 3 * taps * fold
        self.skip = ref[skip_base : skip_base + fold, :]
        self.tokens = tokens
        self.weights = weights

    def span(self, shards):
        if self.weights is not None:
            return self.weights[shards // 4, 0]
        return jnp.exp(-self.rates * float(shards * self.tokens))

    def tap(self, group, shift):
        row = self.tap_base + (group * self.taps + shift) * self.fold
        return self.ref[row : row + self.fold, :]

    def message(self, value):
        return value.astype(F32).reshape(-1, self.fold, LANES)

    def first(self, message, group):
        base = self.poles + group * 2 * self.edge
        return [message[base + i] for i in range(self.edge)]

    def last(self, message, group):
        base = self.poles + group * 2 * self.edge + self.edge
        return [message[base + i] for i in range(self.edge)]

    def mixed(self, before, current, group):
        rows = self.last(before, group) + self.first(current, group)
        return [
            sum(self.tap(group, shift) * rows[self.edge + i - shift] for shift in range(self.taps))
            for i in range(self.edge)
        ]

    def signals(self, before, current):
        pairs = zip(self.mixed(before, current, 1), self.mixed(before, current, 2))
        return [k * v for k, v in pairs]

    def lead(self, shards):
        if self.weights is not None:
            return [self.weights[shards // 4, 1 + i] for i in range(self.edge)]
        last = shards * self.tokens - 1
        return [jnp.exp(-self.rates * float(last - i)) * self.residues for i in range(self.edge)]

    def enter(self, state, span, lead, before, current):
        state = span * state + current[: self.poles]
        for weight, value in zip(lead, self.signals(before, current)):
            state = state + weight * value[None]
        return state


def enter_any(table, place_ref, messages_ref):
    span, lead = table.span(1), table.lead(1)

    def pick(index):
        current = table.message(messages_ref[index])
        before = table.message(messages_ref[jnp.maximum(index - 1, 0)])
        return jnp.where(index > 0, before, 0.0), current

    def one(index, state):
        return table.enter(state, span, lead, *pick(index))

    zero = jnp.zeros((table.poles, table.fold, LANES), F32)
    state = lax.fori_loop(0, place_ref[0], one, zero)
    return (state,) + pick(place_ref[0])


def in_order(place, values):
    out = []
    for p in range(4):
        value = values[p]
        for g in range(1, 4):
            value = jnp.where(place == g, values[p ^ g], value)
        out.append(value)
    return out


def enter_group(table, place_ref, *refs):
    messages = [table.message(ref[...]) for ref in refs[3::-1] + refs[4:]]
    place, group = place_ref[0], in_order(place_ref[0], messages[:4])
    before = jnp.zeros_like(messages[4])
    state = table.enter(before[: table.poles], table.span(4), table.lead(4), before, messages[4])
    before = messages[4]
    for p in range(3):
        behind = table.enter(state, table.span(1), table.lead(1), before, group[p])
        state = jnp.where(p < place, behind, state)
        before = jnp.where(p < place, group[p], before)
    return state, before, messages[0]


def join_kernel(poles, taps, tokens, place_ref, *refs):
    message_refs, (table_ref, out_ref) = refs[3::-1], refs[4:]
    fold = out_ref.shape[0] // (poles + 6 * (taps - 1))
    table = Table(table_ref, poles, taps, fold, tokens)
    group = in_order(place_ref[0], [table.message(ref[...]) for ref in message_refs])
    span, lead = table.span(1), table.lead(1)
    state = group[0][:poles]
    for before, current in zip(group[:-1], group[1:]):
        state = table.enter(state, span, lead, before, current)
    out = [state[r] for r in range(poles)]
    for kind in range(3):
        out += table.first(group[0], kind) + table.last(group[3], kind)
    out_ref[...] = jnp.concatenate(out, axis=0).astype(BF16)


def join_part(place, messages, table, tokens, poles, taps):
    return pl.pallas_call(
        functools.partial(join_kernel, poles, taps, tokens),
        out_shape=jax.ShapeDtypeStruct(messages[0].shape, BF16),
        in_specs=[SMEM] + [VMEM] * 5,
        out_specs=VMEM,
        compiler_params=params(),
        cost_estimate=cost(1 << 20, 1 << 18),
        name="join_state",
    )(place.reshape(1).astype(jnp.int32), *messages[::-1], table)


def weights_kernel(poles, taps, tokens, table_ref, out_ref):
    fold = out_ref.shape[3]
    table = Table(table_ref, poles, taps, fold, tokens)
    for i, shards in enumerate((1, 4)):
        for j, weight in enumerate([table.span(shards)] + table.lead(shards)):
            out_ref[i, j] = weight


def weights_part(table, tokens, poles, taps, fold):
    return pl.pallas_call(
        functools.partial(weights_kernel, poles, taps, tokens),
        out_shape=jax.ShapeDtypeStruct((2, taps, poles, fold, LANES), F32),
        in_specs=[VMEM],
        out_specs=VMEM,
        compiler_params=params(),
        cost_estimate=cost(1 << 20, 1 << 20),
        name="state_weights",
    )(table)


def far_kernel(poles, taps, count, enter, place_ref, near_ref, gate_ref, table_ref, *refs):
    message_refs, weights_refs, (out_ref, conv_s) = refs[:count], refs[count:-2], refs[-2:]
    tokens, channels = near_ref.shape
    fold = channels // LANES
    table = Table(table_ref, poles, taps, fold, tokens, *weights_refs)
    edge = table.edge
    state, before, current = enter(table, place_ref, *message_refs)
    decay = [jnp.exp(-table.rates[r]) for r in range(poles)]
    modes = tuple(state[r] for r in range(poles))
    for t, value in enumerate(table.signals(before, current)):
        modes = tuple(decay[r] * modes[r] + table.residues[r] * value for r in range(poles))
        conv_s[t * fold : (t + 1) * fold, :] = tree_sum(modes + (table.skip * value,))

    def step(t, modes):
        modes = tuple(d * m for d, m in zip(decay, modes))
        conv_s[pl.ds(pl.multiple_of(t * fold, fold), fold), :] = tree_sum(modes)
        return modes

    lax.fori_loop(edge, tokens, step, modes, unroll=18)
    row_id = lax.broadcasted_iota(jnp.int32, (tokens, LANES), 0)
    first = table.mixed(before, current, 0)
    for j in range(fold):
        lanes = slice(j * LANES, (j + 1) * LANES)
        gate = gate_ref[:, lanes]
        for t in range(edge):
            gate = jnp.where(row_id == t, first[t][j : j + 1, :], gate)
        conv = conv_s[pl.ds(j, tokens, stride=fold), :]
        out_ref[:, lanes] = (near_ref[:, lanes].astype(F32) + gate * conv).astype(BF16)


def far_part(enter, place, near, gate, table, messages, poles, taps, weights=()):
    tokens, channels = near.shape
    fold = channels // LANES
    count = len(messages)
    return pl.pallas_call(
        functools.partial(far_kernel, poles, taps, count, enter),
        out_shape=jax.ShapeDtypeStruct((tokens, channels), BF16),
        in_specs=[SMEM] + [VMEM] * (3 + count + len(weights)),
        out_specs=VMEM,
        scratch_shapes=[pltpu.VMEM(folded_shape(tokens, fold), F32)],
        compiler_params=params(),
        cost_estimate=cost(4 * tokens * channels * poles, 3 << 20),
        name="far_filter",
    )(place.reshape(1).astype(jnp.int32), near, gate, table, *messages, *weights)


def project(rows, weight_ref):
    stacked = jnp.concatenate([r[...] for r in rows], axis=0) if len(rows) > 1 else rows[0][...]
    product = lax.dot_general(
        stacked, weight_ref[...], (((1,), (1,)), ((), ())), preferred_element_type=F32
    ).astype(BF16)
    tokens = rows[0].shape[0]
    return [product[i * tokens : (i + 1) * tokens] for i in range(len(rows))]


def own_kernel(*refs):
    *rows_refs, weight_ref, out_ref = refs
    for i, product in enumerate(project(rows_refs, weight_ref)):
        out_ref[i] = product


def other_kernel(
    place_ref, zero_ref, one_ref, two_ref, near_own_ref, two_own_ref, weight_ref, near_ref, out_ref
):
    odd = place_ref[0]
    zero, one, two = project([zero_ref, one_ref, two_ref], weight_ref)
    for i, product in enumerate((zero, one)):
        near_ref[odd ^ i, 0] = near_own_ref[i]
        near_ref[odd ^ i, 1] = product
    out_ref[0] = two_own_ref[0]
    out_ref[1] = two


def far_project_kernel(place_ref, two_ref, three_ref, own_ref, other_ref, out_ref):
    odd = place_ref[0]
    out_ref[odd] = two_ref[...]
    for half, ref in enumerate((own_ref, other_ref)):
        out_ref[1 - odd, half] = project([three_ref], ref)[0]


def project_part(kernel, name, operands, shapes, flops):
    out_shape = tuple(jax.ShapeDtypeStruct(shape, BF16) for shape in shapes)
    return pl.pallas_call(
        kernel,
        out_shape=out_shape,
        in_specs=[SMEM if x.dtype == jnp.int32 else VMEM for x in operands],
        out_specs=(VMEM,) * len(shapes),
        compiler_params=params(),
        cost_estimate=cost(flops, 3 << 20),
        name=name,
    )(*operands)


def finish_kernel(kind_ref, y_ref, *refs):
    out_ref = refs[-1]
    width = refs[0].shape[2]
    for pair in range((len(refs) - 1) // 2):
        for y in range(2):

            @pl.when((kind_ref[0] == pair) & (y_ref[0] == y))
            def _(pair=pair, y=y):
                for h in range(2):
                    total = refs[2 * pair][h ^ y].astype(F32) + refs[2 * pair + 1][h ^ y].astype(F32)
                    out_ref[:, h * width : (h + 1) * width] = total.astype(BF16)


def permute(name, x, move, keep=None):
    pairs = []
    for index in range(32):
        place = (index // 8, index // 4 % 2, index // 2 % 2, index % 2)
        if keep is None or keep(*place):
            z, y, x_, c = move(*place)
            pairs.append((index, ((z * 2 + y) * 2 + x_) * 2 + c))
    with jax.named_scope(name):
        return lax.ppermute(x, AXES, pairs)


def over_y(z, y, x, c):
    return z, 1 - y, x, c


def over_z0(z, y, x, c):
    return z ^ 1, y, x, c


def over_z1(z, y, x, c):
    return z ^ 2, y, x, c


def over_core(z, y, x, c):
    return z, y, x, 1 - c


def after(x, *others):
    return lax.optimization_barrier((x,) + others)[0]


def per_device_32(features, short_taps, rates, residues, skip, out_weight):
    tokens, _, channels = features.shape
    q, k, v = (features[:, group] for group in range(3))
    poles, taps = rates.shape[1], short_taps.shape[1]
    seq, tp = lax.axis_index("seq"), lax.axis_index("tp")
    z, y = seq >> 1, seq & 1
    signal, message, table = signal_part(q, k, v, short_taps, rates, residues, skip)
    near, gate = near_part(q, signal, table, poles, taps)
    messages = [
        message,
        permute("state_y", message, over_y),
        permute("state_z", message, over_z0),
        permute("state_zy", message, lambda z, y, x, c: (z ^ 1, 1 - y, x, c)),
    ]
    place = seq & 3
    joined = join_part(place, messages, table, tokens, poles, taps)
    weights = weights_part(after(table, joined), tokens, poles, taps, channels // LANES)
    w_y = permute("weights", after(out_weight, weights), over_y)
    joined = permute("state_half", joined, over_z1, lambda z, y, x, c: z < 2)
    gated = far_part(
        enter_group, place, near, gate, table, messages[::-1] + [joined], poles, taps, [weights]
    )
    two = permute("gated_two", gated, over_z1)
    one = permute("gated_one", gated, over_z0)
    three = permute("gated_three", two, over_z0)
    odd = (z ^ tp) & 1
    place = odd.reshape(1).astype(jnp.int32)

    def odd_of(z, y, x, c):
        return (z ^ c) % 2

    def home(summed, far):
        def move(z, y, x, c):
            return z ^ far ^ odd_of(z, y, x, c), y, z // 2, z % 2

        return [
            permute(f"straight_{far}", summed, move, lambda z, y, x, c: x == z // 2),
            permute(f"across_{far}", summed, move, lambda z, y, x, c: x != z // 2),
        ]

    def add_cores(name, kept, sent):
        from_core = permute(name, sent, over_core)
        return (kept.astype(F32) + from_core.astype(F32)).astype(BF16)

    width = out_weight.shape[0]
    whole, flops = (2, tokens, width), 2 * tokens * channels * width
    (two_own,) = project_part(own_kernel, "project_two", [two, out_weight], [(1, tokens, width)], flops)
    (near_own,) = project_part(
        own_kernel, "project_near", [gated, one, out_weight], [whole], 2 * flops
    )
    near, part_two = project_part(
        other_kernel,
        "project_other",
        [place, gated, one, two, near_own, two_own, w_y],
        [(2,) + whole, whole],
        3 * flops,
    )
    (far,) = project_part(
        far_project_kernel,
        "project_far",
        [place, part_two, three, out_weight, w_y],
        [(2,) + whole],
        2 * flops,
    )
    far_sum = add_cores("core_far", far[0], far[1])
    near = after(near, far_sum)
    near_sum = add_cores("core_near", near[0], near[1])
    parts = home(near_sum, 0) + home(far_sum, 2)
    kind = (z ^ tp) >> 1
    return pl.pallas_call(
        finish_kernel,
        out_shape=jax.ShapeDtypeStruct((tokens, 2 * out_weight.shape[0]), BF16),
        in_specs=[SMEM] * 2 + [VMEM] * len(parts),
        out_specs=VMEM,
        compiler_params=params(),
        cost_estimate=cost(4 * tokens * out_weight.shape[0], 2 << 20),
        name="finish",
    )(kind.reshape(1).astype(jnp.int32), y.reshape(1).astype(jnp.int32), *parts)


def per_device(features, short_taps, rates, residues, skip, out_weight):
    q, k, v = (features[:, group] for group in range(3))
    poles, taps = rates.shape[1], short_taps.shape[1]
    signal, message, table = signal_part(q, k, v, short_taps, rates, residues, skip)
    near, gate = near_part(q, signal, table, poles, taps)
    messages = lax.all_gather(message, "seq")
    place = lax.axis_index("seq")
    gated = far_part(enter_any, place, near, gate, table, [messages], poles, taps)
    partial = lax.dot_general(
        gated,
        lax.all_gather(out_weight, "seq", axis=0, tiled=True),
        (((1,), (1,)), ((), ())),
        preferred_element_type=F32,
    )
    return lax.psum_scatter(partial.astype(BF16), "tp", scatter_dimension=1, tiled=True)


def solution(mesh):
    in_specs = (
        P("seq", None, "tp"),
        P(None, None, "tp"),
        P("tp", None),
        P("tp", None),
        P("tp"),
        P("seq", "tp"),
    )
    out_specs = P("seq", "tp")
    body = per_device_32 if (mesh.shape["seq"], mesh.shape["tp"]) == (8, 4) else per_device
    return jax.shard_map(body, mesh=mesh, in_specs=in_specs, out_specs=out_specs, check_vma=False)
```
